32 devices in a mesh: narrow: 4 (over x, core), wide: 8 (over z, y).
Axes of the slice: x: 2, y: 2, z: 4, core: 2. Of those that a mesh axis runs over, the one named last changes fastest.
Arguments:
- block_input: bfloat16 [32, 14, 14, 2048], P('wide', None, None, 'narrow'), may hold values from -8 to 8, as said below
- out_grad: bfloat16 [32, 14, 14, 2048], P('wide', None, None, 'narrow'), may hold values from -6 to 6
- conv_reduce: float32 [2, 2048, 512], P(None, 'wide', 'narrow'), may hold values from -2 to 2, as said below
- conv_spatial: float32 [2, 4608, 512], P(None, 'wide', 'narrow'), may hold values from -2 to 2, as said below
- conv_expand: float32 [2, 512, 2048], P(None, 'wide', 'narrow'), may hold values from -2 to 2, as said below
- first_reduce: float32 [2, 2048, 512], P(None, 'wide', 'narrow'), may hold values from -56 to 56
- first_spatial: float32 [2, 4608, 512], P(None, 'wide', 'narrow'), may hold values from -56 to 56
- first_expand: float32 [2, 512, 2048], P(None, 'wide', 'narrow'), may hold values from -56 to 56
- second_reduce: float32 [2, 2048, 512], P(None, 'wide', 'narrow'), may hold values from 6.272 to 25.088
- second_spatial: float32 [2, 4608, 512], P(None, 'wide', 'narrow'), may hold values from 6.272 to 25.088
- second_expand: float32 [2, 512, 2048], P(None, 'wide', 'narrow'), may hold values from 6.272 to 25.088
- norm_params: float32 [2, 2, 4, 768], P(None, None, 'narrow'), may hold values from -1 to 2, as said below
- norm_first: float32 [2, 2, 4, 768], P(None, None, 'narrow'), may hold values from -56 to 56
- norm_second: float32 [2, 2, 4, 768], P(None, None, 'narrow'), may hold values from 6.272 to 25.088
Outputs:
- block_output: float32 [32, 14, 14, 2048], P('wide', None, None, 'narrow')
- input_grad: float32 [32, 14, 14, 2048], P('wide', None, None, 'narrow')
- grad_reduce: float32 [2, 2048, 512], P(None, 'wide', 'narrow')
- grad_spatial: float32 [2, 4608, 512], P(None, 'wide', 'narrow')
- grad_expand: float32 [2, 512, 2048], P(None, 'wide', 'narrow')
- square_reduce: float32 [2, 2048, 512], P(None, 'wide', 'narrow')
- square_spatial: float32 [2, 4608, 512], P(None, 'wide', 'narrow')
- square_expand: float32 [2, 512, 2048], P(None, 'wide', 'narrow')
- new_reduce: float32 [2, 2048, 512], P(None, 'wide', 'narrow')
- new_spatial: float32 [2, 4608, 512], P(None, 'wide', 'narrow')
- new_expand: float32 [2, 512, 2048], P(None, 'wide', 'narrow')
- norm_grads: float32 [2, 2, 4, 768], P(None, None, 'narrow')
- norm_square: float32 [2, 2, 4, 768], P(None, None, 'narrow')
- norm_new: float32 [2, 2, 4, 768], P(None, None, 'narrow')
- layer_norms: float32 [2, 3, 2], replicated
The draws below stay inside these ranges and needn't reach their ends.
Inputs may be any that keep to these rules, and one draw needn't show every extreme that they name: `block_input`: real-valued activations. `norm_params`: gains near one and shifts near zero. `conv_reduce`: real-valued weights. `conv_spatial`: real-valued weights. `conv_expand`: real-valued weights.
All inputs are finite; a program needn't handle non-finite values.
Results may differ from the reference program's by a relative error of at most 0.024.
Values may be sent and summed in bfloat16 or wider, within the bound.
No kernel may reach another device: no remote copies, remote signals or barrier semaphores. Data moves between devices by JAX's collectives and lax.ppermute only.
A program may use at most 192 MiB of HBM per device.

```python
import math
import jax
import jax.numpy as jnp
from jax import lax

C = 2048
M = 512
H = 14
BLOCKS = 2
STEP = 10
IMAGES = 32
GROUP = 768
N_NARROW = 4


def draw_block_input(key, part):
    key = jax.random.fold_in(key, 1)
    first_key = jax.random.fold_in(key, 0)
    ramp = jnp.arange(IMAGES, dtype=jnp.float32) / IMAGES
    scales = 0.6 + 1.2 * ramp
    values = jnp.clip(jax.random.normal(first_key, (IMAGES, H, H, C), jnp.float32), -4.0, 4.0) * scales[:, None, None, None]
    return values.astype(jnp.bfloat16)


def draw_norm_params(key, part):
    key = jax.random.fold_in(key, 2)
    first_key, second_key = jax.random.split(key)
    shape = (BLOCKS, 1, N_NARROW, GROUP)
    gains = jax.random.uniform(first_key, shape, jnp.float32, 0.7, 1.3)
    shifts = jax.random.uniform(second_key, shape, jnp.float32, -0.4, 0.4)
    return jnp.concatenate([gains, shifts], axis=1)


def ramped(base, fan_in, growth):
    rows = base.shape[1]
    cols = base.shape[2]
    row_ramp = 1.0 + (growth ** 0.25 - 1.0) * jnp.arange(rows, dtype=jnp.float32) / (rows - 1)
    col_ramp = 1.0 + (growth ** 0.5 - 1.0) * jnp.arange(cols, dtype=jnp.float32) / (cols - 1)
    return base * fan_in ** (-0.5) * row_ramp[None, :, None] * col_ramp[None, None, :]


def base_values(key, shape):
    return (jnp.clip(jax.random.normal(key, shape, jnp.float32), -4.0, 4.0), 3.0)


def draw_conv_reduce(key, part):
    key = jax.random.fold_in(key, 3)
    base, growth = base_values(key, (BLOCKS, C, M))
    return ramped(base, C, growth)


def draw_conv_spatial(key, part):
    key = jax.random.fold_in(key, 4)
    base, growth = base_values(key, (BLOCKS, 9 * M, M))
    return ramped(base, 9 * M, growth)


def draw_conv_expand(key, part):
    key = jax.random.fold_in(key, 5)
    base, growth = base_values(key, (BLOCKS, M, C))
    return ramped(base, M, growth)


def block_levels(rng, extent, cuts, low, high):
    def one(position, blocks):
        heights = jax.random.uniform(jax.random.fold_in(jax.random.fold_in(rng, 6), position), (blocks,), jnp.float32, low / len(cuts), high / len(cuts))
        return jnp.repeat(jnp.exp(heights), extent[position] // blocks).reshape((-1,) + (1,) * (len(extent) - position - 1))

    loudness = one(*cuts[0])
    for cut in cuts[1:]:
        loudness = loudness * one(*cut)
    return loudness


def gaussian(stream_key, dims, width, limit, cuts=(), kind=jnp.bfloat16):
    array = width * jax.random.normal(stream_key, dims, jnp.float32)
    if cuts:
        array = array * block_levels(stream_key, dims, cuts, -0.22, 0.18)
    return jnp.clip(array, -limit, limit).astype(kind)


def setup_inputs(seed: int = 0) -> dict:
    keys = jax.random.split(jax.random.key(seed), 15)
    block_input = draw_block_input(jax.random.fold_in(keys[14], 71), 0)
    out_grad = gaussian(keys[1], (IMAGES, H, H, C), 1.0, 6.0, ((0, 8), (3, 4)))
    conv_reduce = draw_conv_reduce(jax.random.fold_in(keys[14], 71), 0)
    conv_spatial = draw_conv_spatial(jax.random.fold_in(keys[14], 71), 0)
    conv_expand = draw_conv_expand(jax.random.fold_in(keys[14], 71), 0)
    first_reduce = gaussian(keys[5], (BLOCKS, C, M), (0.11 * (IMAGES * H * H) ** 0.5), 56.0, ((1, 8), (2, 4)), jnp.float32)
    first_spatial = gaussian(keys[6], (BLOCKS, 9 * M, M), (0.11 * (IMAGES * H * H) ** 0.5), 56.0, ((1, 8), (2, 4)), jnp.float32)
    first_expand = gaussian(keys[7], (BLOCKS, M, C), (0.11 * (IMAGES * H * H) ** 0.5), 56.0, ((1, 8), (2, 4)), jnp.float32)
    second_reduce = jnp.clip(jnp.exp(math.log(25.088) - 1.3862944 * jax.random.uniform(keys[8], (BLOCKS, C, M), jnp.float32) ** block_levels(keys[8], (BLOCKS, C, M), ((1, 8), (2, 4)), -0.2, 0.2)), 6.272, 25.088)
    second_spatial = jnp.clip(jnp.exp(math.log(25.088) - 1.3862944 * jax.random.uniform(keys[9], (BLOCKS, 9 * M, M), jnp.float32) ** block_levels(keys[9], (BLOCKS, 9 * M, M), ((1, 8), (2, 4)), -0.2, 0.2)), 6.272, 25.088)
    second_expand = jnp.clip(jnp.exp(math.log(25.088) - 1.3862944 * jax.random.uniform(keys[10], (BLOCKS, M, C), jnp.float32) ** block_levels(keys[10], (BLOCKS, M, C), ((1, 8), (2, 4)), -0.2, 0.2)), 6.272, 25.088)
    norm_params = draw_norm_params(jax.random.fold_in(keys[14], 71), 0)
    norm_first = gaussian(keys[12], (BLOCKS, 2, N_NARROW, GROUP), (0.11 * (IMAGES * H * H) ** 0.5), 56.0, ((2, 4),), jnp.float32)
    norm_second = jnp.clip(jnp.exp(math.log(25.088) - 1.3862944 * jax.random.uniform(keys[13], (BLOCKS, 2, N_NARROW, GROUP), jnp.float32) ** block_levels(keys[13], (BLOCKS, 2, N_NARROW, GROUP), ((2, 4),), -0.2, 0.2)), 6.272, 25.088)
    return {"block_input": block_input, "out_grad": out_grad, "conv_reduce": conv_reduce, "conv_spatial": conv_spatial, "conv_expand": conv_expand, "first_reduce": first_reduce, "first_spatial": first_spatial, "first_expand": first_expand, "second_reduce": second_reduce, "second_spatial": second_spatial, "second_expand": second_expand, "norm_params": norm_params, "norm_first": norm_first, "norm_second": norm_second}


BN_EPS = 1e-05
FIRST_DECAY = 0.9
SECOND_DECAY = 0.999
ADAM_EPSILON = 1e-06
WEIGHT_DECAY = 0.01
MATRIX_RATE = 0.5
NORM_RATE = 0.3

@jax.custom_vjp
def low(v):
    return lax.optimization_barrier(v.astype(jnp.bfloat16)).astype(jnp.float32)

@jax.custom_vjp
def low_back(v):
    return v

def low_keep(v):
    return (low(v), None)

def low_pass(kept, grad):
    return (grad,)

def back_keep(v):
    return (v, None)

def back_low(kept, grad):
    return (low(grad),)
low.defvjp(low_keep, low_pass)
low_back.defvjp(back_keep, back_low)

def unpack(norm_params, block_index, kind_index):
    param_row = norm_params[block_index, kind_index]
    narrow_width = M // N_NARROW
    return (param_row[:, :narrow_width].reshape(-1), param_row[:, narrow_width:2 * narrow_width].reshape(-1), param_row[:, 2 * narrow_width:].reshape(-1))

def project(left_side, matrix):
    return jnp.einsum('ihwc,cd->ihwd', left_side, matrix, precision=lax.Precision.HIGHEST)

def spatial(hidden, matrix):
    map_side = hidden.shape[1]
    channels = hidden.shape[3]
    padded = jnp.pad(hidden, ((0, 0), (1, 1), (1, 1), (0, 0)))
    total = jnp.zeros(hidden.shape[:3] + (matrix.shape[1],), jnp.float32)
    for tap_index in range(9):
        row_shift = tap_index // 3
        col_shift = tap_index % 3
        piece = padded[:, row_shift:row_shift + map_side, col_shift:col_shift + map_side, :]
        total = total + project(piece, matrix[tap_index * channels:(tap_index + 1) * channels])
    return total

def normalize(pre_norm, gain_row, shift_row):
    center = lax.optimization_barrier(jnp.mean(pre_norm, axis=(0, 1, 2)))
    spread_sq = lax.optimization_barrier(jnp.mean(pre_norm * pre_norm, axis=(0, 1, 2))) - center * center
    return gain_row * (pre_norm - center) * lax.rsqrt(spread_sq + BN_EPS) + shift_row

def forward(stream, conv_reduce, conv_spatial, conv_expand, norm_params):
    reduce_low = low(conv_reduce)
    spatial_low = low(conv_spatial)
    expand_low = low(conv_expand)
    for block_index in range(BLOCKS):
        gain_rows = unpack(norm_params, block_index, 0)
        shift_rows = unpack(norm_params, block_index, 1)
        first_pre = low_back(project(low(stream), reduce_low[block_index]))
        first_hidden = jax.nn.silu(normalize(first_pre, gain_rows[0], shift_rows[0]))
        middle_pre = low_back(spatial(low(first_hidden), spatial_low[block_index]))
        middle_hidden = jax.nn.silu(normalize(middle_pre, gain_rows[1], shift_rows[1]))
        last_pre = low_back(project(low(middle_hidden), expand_low[block_index]))
        stream = jax.nn.silu(normalize(last_pre, gain_rows[2], shift_rows[2]) + stream)
    return stream

def lamb(master, first, second, gradient):
    first_new = FIRST_DECAY * first + (1.0 - FIRST_DECAY) * gradient
    second_new = SECOND_DECAY * second + (1.0 - SECOND_DECAY) * gradient * gradient
    update = first_new / (1.0 - FIRST_DECAY ** STEP) / (jnp.sqrt(second_new / (1.0 - SECOND_DECAY ** STEP)) + ADAM_EPSILON) + WEIGHT_DECAY * master
    master_norm = jnp.sqrt(lax.optimization_barrier(jnp.sum(master * master, axis=(1, 2))))
    update_norm = jnp.sqrt(lax.optimization_barrier(jnp.sum(update * update, axis=(1, 2))))
    renewed = master - MATRIX_RATE * (master_norm / update_norm)[:, None, None] * update
    return (second_new, renewed, jnp.stack([master_norm, update_norm], -1))

def reference(block_input, out_grad, conv_reduce, conv_spatial, conv_expand, first_reduce, first_spatial, first_expand, second_reduce, second_spatial, second_expand, norm_params, norm_first, norm_second):
    stream = block_input.astype(jnp.float32)
    cotangent = out_grad.astype(jnp.float32)
    block_output, pullback = jax.vjp(forward, stream, conv_reduce, conv_spatial, conv_expand, norm_params)
    input_grad, grad_reduce, grad_spatial, grad_expand, norm_grads = pullback(cotangent)
    square_reduce, new_reduce, norms_reduce = lamb(conv_reduce, first_reduce, second_reduce, grad_reduce)
    square_spatial, new_spatial, norms_spatial = lamb(conv_spatial, first_spatial, second_spatial, grad_spatial)
    square_expand, new_expand, norms_expand = lamb(conv_expand, first_expand, second_expand, grad_expand)
    layer_norms = jnp.stack([norms_reduce, norms_spatial, norms_expand], 1)
    norm_moment = FIRST_DECAY * norm_first + (1.0 - FIRST_DECAY) * norm_grads
    norm_square = SECOND_DECAY * norm_second + (1.0 - SECOND_DECAY) * norm_grads * norm_grads
    norm_new = norm_params - NORM_RATE * (norm_moment / (1.0 - FIRST_DECAY ** STEP)) / (jnp.sqrt(norm_square / (1.0 - SECOND_DECAY ** STEP)) + ADAM_EPSILON)
    return (block_output, input_grad, grad_reduce, grad_spatial, grad_expand, square_reduce, square_spatial, square_expand, new_reduce, new_spatial, new_expand, norm_grads, norm_square, norm_new, layer_norms)
```

```python
import functools

import jax
import jax.numpy as jnp
import numpy as np
from jax import lax
from jax.experimental import pallas as pl
from jax.experimental.pallas import tpu as pltpu
from jax.sharding import Mesh
from jax.sharding import PartitionSpec as P

STEP = 10
BN_EPS = 1e-05
FIRST_DECAY = 0.9
SECOND_DECAY = 0.999
ADAM_EPSILON = 1e-06
WEIGHT_DECAY = 0.01
MATRIX_RATE = 0.5
NORM_RATE = 0.3

ALL = ("x", "core", "wide")
CROSS = ("x", "wide")
BF = jnp.bfloat16
F32 = jnp.float32

SIDE = 14
LINE = 16
IMG = SIDE * LINE
NIMG = 2
ROWS = NIMG * IMG
SPAN = ROWS + LINE * (NIMG - 1)
PIECES = 8


def dot(a, b):
    return lax.dot_general(a, b, (((1,), (0,)), ((), ())), preferred_element_type=F32)


def dot_nt(a, b):
    return lax.dot_general(a, b, (((1,), (1,)), ((), ())), preferred_element_type=F32)


def dot_tn(a, b):
    return lax.dot_general(a, b, (((0,), (0,)), ((), ())), preferred_element_type=F32)


def lanes(parts):
    return jnp.concatenate(parts, axis=1)


def rows(parts):
    return jnp.concatenate(parts, axis=0)


def sigmoid(v):
    return 0.5 * jnp.tanh(0.5 * v) + 0.5


def silu(v):
    return v * sigmoid(v)


def silu_slope(v):
    s = sigmoid(v)
    return s * (1.0 + v * (1.0 - s))


def inside(shape):
    return (lax.broadcasted_iota(jnp.int32, shape, 0) & (LINE - 1)) < SIDE


def keep_inside(v):
    return jnp.where(inside(v.shape), v, 0.0)


def pack_rows(total, other):
    n = total.shape[1] // 128
    return rows([v[:, i * 128 : (i + 1) * 128] for v in (total, other) for i in range(n)])


def unpack_rows(block):
    n = block.shape[0] // 2
    return tuple(lanes([block[k * n + i : k * n + i + 1] for i in range(n)]) for k in range(2))


def column_sums(a, b):
    return pack_rows(jnp.sum(a, 0, keepdims=True), jnp.sum(b, 0, keepdims=True))


def mean_inverse(block, population):
    total, square = unpack_rows(block)
    mean = total / population
    return mean, lax.rsqrt(square / population - mean * mean + BN_EPS)


def call(kernel, outs, *args, scratch=(), name=None, smem=(), limit=48):
    specs = [
        pl.BlockSpec(memory_space=pltpu.SMEM) if i in smem else pl.BlockSpec(memory_space=pltpu.VMEM)
        for i in range(len(args))
    ]
    return pl.pallas_call(
        kernel,
        out_shape=[jax.ShapeDtypeStruct(s, d) for s, d in outs],
        in_specs=specs,
        out_specs=[pl.BlockSpec(memory_space=pltpu.VMEM) for _ in outs],
        scratch_shapes=list(scratch),
        compiler_params=pltpu.CompilerParams(vmem_limit_bytes=limit * 1024 * 1024),
        name=name,
    )(*args)


def place(ids, half, piece):
    return ids[4 + PIECES * half + piece]


def enter_kernel(ids, image_ref, grad_ref, keep_x, send_x, keep_g, send_g):
    x = ids[0]
    for src, keep, send in ((image_ref, keep_x, send_x), (grad_ref, keep_g, send_g)):
        for dst, owner in ((keep, x), (send, 1 - x)):
            for i in range(NIMG):
                img = src[owner * NIMG + i]
                pad = jnp.zeros((SIDE, LINE - SIDE, img.shape[2]), img.dtype)
                full = jnp.concatenate([img, pad], axis=1)
                dst[i * IMG : (i + 1) * IMG] = full.reshape(IMG, img.shape[2])


def join_kernel(ids, keep_x, recv_x, keep_g, recv_g, out_x, out_g):
    first = ids[0] == 0
    for keep, recv, out in ((keep_x, recv_x, out_x), (keep_g, recv_g, out_g)):
        a = keep[...]
        b = recv[...]
        n = a.shape[1]
        out[:, :n] = jnp.where(first, a, b)
        out[:, n:] = jnp.where(first, b, a)


def params_kernel(ids, all_ref, own_ref, oth_ref):
    core = ids[1]
    for c, dst in ((core, own_ref), (1 - core, oth_ref)):
        for k in range(2):
            part = all_ref[pl.ds(2 * k + c, 1)][0]
            dst[:, k * 128 : (k + 1) * 128] = part[:, 0:128]
            dst[:, 256 + k * 128 : 256 + (k + 1) * 128] = part[:, 128:256]
            dst[:, 512 + k * 512 : 512 + (k + 1) * 512] = part[:, 256:768]


def centred(z, total, pixels):
    return keep_inside(z - total / pixels).astype(BF)


def reduce_kernel(ids, xo, xt, w, pre_out, centred_out, stat_out):
    core = ids[1]
    parts = []
    for c in (core, 1 - core):
        for k in range(2):
            for j in range(2):
                p = 2 * (2 * k + c) + j
                parts.append(lanes([w[place(ids, 0, p)], w[place(ids, 1, p)]]))
    pre = dot(lanes([xo[...], xt[...]]), rows(parts))
    total = jnp.sum(pre, 0, keepdims=True)
    stats = pack_rows(total, jnp.sum(pre * pre, 0, keepdims=True))
    pre_out[...] = pre
    centred_out[...] = centred(pre, total, NIMG * SIDE * SIDE)
    stat_out[...] = jnp.broadcast_to(stats[None], stat_out.shape)


def both_halves(ids, stat, pre, other, own_prm, oth_prm, lo, population, moments_out):
    x, core, wide = ids[0], ids[1], ids[2]
    own = stat[:, pl.ds(core, 1)]
    oth = stat[:, pl.ds(1 - core, 1)]
    own_sum = jnp.sum(own, axis=(0, 1, 2))
    oth_sum = jnp.sum(oth, axis=(0, 1, 2))
    local = stat[pl.ds(x, 1), pl.ds(1 - core, 1), pl.ds(wide, 1)].reshape(4, 128)
    mean, inverse = mean_inverse(own_sum, population)
    moments_out[...] = rows([mean, inverse, jnp.zeros((6, mean.shape[1]), F32)])
    hid_own = silu(own_prm[0:1, lo : lo + 256] * (pre[...] - mean) * inverse + own_prm[1:2, lo : lo + 256])
    mean_t, inverse_t = mean_inverse(oth_sum, population)
    local_mean = unpack_rows(local)[0] / (NIMG * SIDE * SIDE)
    hid_oth = silu(
        oth_prm[0:1, lo : lo + 256] * (other[...].astype(F32) + (local_mean - mean_t)) * inverse_t
        + oth_prm[1:2, lo : lo + 256]
    )
    hid_own = keep_inside(hid_own)
    hid_oth = keep_inside(hid_oth)
    first = core == 0
    parts = []
    for k in range(2):
        a = hid_own[:, k * 128 : (k + 1) * 128]
        b = hid_oth[:, k * 128 : (k + 1) * 128]
        parts += [jnp.where(first, a, b), jnp.where(first, b, a)]
    return lanes(parts)


def fill_shifts(dst, v, sign):
    for d in range(3):
        shifted = v if d == 1 else pltpu.roll(v, (sign * (d - 1)) % v.shape[0], 0)
        shifted = shifted.astype(BF)
        dst[d, 0:LINE] = jnp.zeros((LINE, v.shape[1]), BF)
        for i in range(NIMG):
            at = LINE + i * (IMG + LINE)
            dst[d, at : at + IMG] = shifted[i * IMG : (i + 1) * IMG]
            dst[d, at + IMG : at + IMG + LINE] = jnp.zeros((LINE, v.shape[1]), BF)


def squeeze(v):
    return rows([v[i * (IMG + LINE) : i * (IMG + LINE) + IMG] for i in range(NIMG)])


def tap_segments(tap, depth):
    lo, hi = tap * 512, (tap + 1) * 512
    found = []
    while lo < hi:
        piece = lo // depth
        end = min(hi, (piece + 1) * depth)
        found.append((piece, lo - piece * depth, end - piece * depth))
        lo = end
    return found


def tap_weights(ids, w, tap):
    return lanes(
        [
            rows([w[place(ids, h, p), a:b] for p, a, b in tap_segments(tap, w.shape[1])])
            for h in range(2)
        ]
    )


def spatial_kernel(
    population, ids, stat, pre, other, own_prm, oth_prm, w, hid_out, moments_out, pre_out, centred_out, stat_out, shifts
):
    hid = both_halves(ids, stat, pre, other, own_prm, oth_prm, 0, population, moments_out)
    fill_shifts(shifts, hid, -1)
    hid_out[...] = shifts[1, LINE : LINE + SPAN]
    acc = None
    for tap in range(9):
        at = (tap // 3) * LINE
        part = dot(shifts[tap % 3, at : at + SPAN], tap_weights(ids, w, tap))
        acc = part if acc is None else acc + part
    pre2 = keep_inside(squeeze(acc))
    total = jnp.sum(pre2, 0, keepdims=True)
    stats = pack_rows(total, jnp.sum(pre2 * pre2, 0, keepdims=True))
    pre_out[...] = pre2
    centred_out[...] = centred(pre2, total, NIMG * SIDE * SIDE)
    stat_out[...] = jnp.broadcast_to(stats[None], stat_out.shape)


def expand_kernel(population, ids, stat, pre, other, own_prm, oth_prm, w, hid_out, moments_out, pre_out, stat_out):
    hid = both_halves(ids, stat, pre, other, own_prm, oth_prm, 256, population, moments_out).astype(BF)
    hid_out[...] = hid
    total = []
    square = []
    for h in range(2):
        pre3 = dot(hid, rows([w[place(ids, h, p)] for p in range(PIECES)]))
        pre_out[:, h * 512 : (h + 1) * 512] = pre3
        total.append(jnp.sum(pre3, 0, keepdims=True))
        square.append(jnp.sum(pre3 * pre3, 0, keepdims=True))
    stats = pack_rows(lanes(total), lanes(square))
    stat_out[...] = jnp.broadcast_to(stats[None], stat_out.shape)


def close_kernel(population, stat, pre, stream, own_prm, moments_out, out, low_out):
    mean, inverse = mean_inverse(jnp.sum(stat[...], 0), population)
    moments_out[...] = rows([mean, inverse, jnp.zeros((6, mean.shape[1]), F32)])
    v = own_prm[0:1, 512:] * (pre[...] - mean) * inverse + own_prm[1:2, 512:] + stream[...].astype(F32)
    result = keep_inside(silu(v))
    out[...] = result
    low_out[...] = result.astype(BF)


def last_kernel(population, stat, pre, stream, own_prm, grad, moments_out, out, outside_out, stat_out):
    mean, inverse = mean_inverse(jnp.sum(stat[...], 0), population)
    moments_out[...] = rows([mean, inverse, jnp.zeros((6, mean.shape[1]), F32)])
    normed = (pre[...] - mean) * inverse
    v = own_prm[0:1, 512:] * normed + own_prm[1:2, 512:] + stream[...].astype(F32)
    s = sigmoid(v)
    out[...] = v * s
    outside = keep_inside(grad[...].astype(F32) * (s * (1.0 + v * (1.0 - s))))
    outside_out[...] = outside
    stat_out[...] = jnp.broadcast_to(column_sums(outside, outside * normed)[None], stat_out.shape)


def outer_back_kernel(moments, pre, stream, own_prm, outside_after, own_part, recv_part, outside_out, stat_out):
    mean = moments[0:1]
    inverse = moments[1:2]
    normed = (pre[...] - mean) * inverse
    v = own_prm[0:1, 512:] * normed + own_prm[1:2, 512:] + stream[...].astype(F32)
    upstream = outside_after[...] + own_part[...] + recv_part[...].astype(F32)
    outside = keep_inside(upstream * silu_slope(v))
    outside_out[...] = outside
    stat_out[...] = jnp.broadcast_to(column_sums(outside, outside * normed)[None], stat_out.shape)


def norm_back(sums, population, moments, pre, upstream, gain):
    shift_grad, gain_grad = unpack_rows(sums)
    mean = moments[0:1]
    inverse = moments[1:2]
    normed = (pre[...] - mean) * inverse
    lowered = gain * inverse * (upstream[...] - shift_grad / population - normed * (gain_grad / population))
    return keep_inside(lowered)


def split_cores(ids, parts, own_out, send_out):
    first = ids[1] == 0
    width = parts[0].shape[1]
    for k in range(2):
        a, b = parts[2 * k], parts[2 * k + 1]
        own_out[:, k * width : (k + 1) * width] = jnp.where(first, a, b)
        send_out[:, k * width : (k + 1) * width] = jnp.where(first, b, a).astype(BF)


def expand_back_kernel(population, ids, stat, moments, pre, outside, own_prm, w, low_out, own_out, send_out, sums_out):
    sums = jnp.sum(stat[...], 0)
    sums_out[...] = sums
    low = norm_back(sums, population, moments, pre, outside, own_prm[0:1, 512:]).astype(BF)
    low_out[...] = low
    acc = None
    for h in range(2):
        part = dot_nt(low[:, h * 512 : (h + 1) * 512], rows([w[place(ids, h, p)] for p in range(PIECES)]))
        acc = part if acc is None else acc + part
    split_cores(ids, [acc[:, n * 128 : (n + 1) * 128] for n in range(4)], own_out, send_out)


def expand_grad_kernel(ids, hid, low, out):
    grad = dot_tn(hid[...], low[...])
    depth = out.shape[1]
    for h in range(2):
        for p in range(PIECES):
            out[place(ids, h, p)] = grad[p * depth : (p + 1) * depth, h * 512 : (h + 1) * 512].astype(out.dtype)


def inner_back_kernel(lo, own_part, recv_part, moments, pre, own_prm, out, stat_out):
    normed = (pre[...] - moments[0:1]) * moments[1:2]
    v = own_prm[0:1, lo : lo + 256] * normed + own_prm[1:2, lo : lo + 256]
    upstream = (own_part[...] + recv_part[...].astype(F32)) * silu_slope(v)
    upstream = keep_inside(upstream)
    out[...] = upstream
    stat_out[...] = jnp.broadcast_to(column_sums(upstream, upstream * normed)[None], stat_out.shape)


def spatial_back_kernel(population, ids, stat, moments, pre, upstream, own_prm, w, shifts, own_out, send_out, sums_out):
    sums = jnp.sum(stat[...], 0)
    sums_out[...] = sums
    low = norm_back(sums, population, moments, pre, upstream, own_prm[0:1, 256:512])
    fill_shifts(shifts, low, 1)
    acc = None
    for tap in range(9):
        at = LINE * (2 - tap // 3)
        part = dot_nt(shifts[tap % 3, at : at + SPAN], tap_weights(ids, w, tap))
        acc = part if acc is None else acc + part
    acc = squeeze(acc)
    split_cores(ids, [acc[:, n * 128 : (n + 1) * 128] for n in range(4)], own_out, send_out)


def spatial_grad_kernel(ids, hid, shifts, out):
    turned = hid[...].T
    depth = out.shape[1]
    for tap in range(9):
        at = LINE * (2 - tap // 3)
        grad = dot(turned, shifts[tap % 3, at : at + SPAN])
        row = 0
        for p, a, b in tap_segments(tap, depth):
            for h in range(2):
                out[place(ids, h, p), a:b] = grad[row : row + b - a, h * 128 : (h + 1) * 128].astype(out.dtype)
            row += b - a


def reduce_back_kernel(population, ids, stat, moments, pre, upstream, own_prm, w, low_out, own_out, send_out, sums_out):
    sums = jnp.sum(stat[...], 0)
    sums_out[...] = sums
    low = norm_back(sums, population, moments, pre, upstream, own_prm[0:1, 0:256]).astype(BF)
    low_out[...] = low
    core = ids[1]
    for c, dst in ((1 - core, send_out), (core, own_out)):
        for k in range(2):
            for j in range(2):
                p = 2 * (2 * k + c) + j
                part = dot_nt(low, lanes([w[place(ids, 0, p)], w[place(ids, 1, p)]]))
                at = k * 512 + j * 256
                dst[:, at : at + 256] = part.astype(dst.dtype)


def reduce_grad_kernel(ids, xo, xt, low, out):
    core = ids[1]
    for c, src in ((core, xo), (1 - core, xt)):
        grad = dot_tn(src[...], low[...])
        for k in range(2):
            for j in range(2):
                p = 2 * (2 * k + c) + j
                at = k * 512 + j * 256
                for h in range(2):
                    out[place(ids, h, p)] = grad[at : at + 256, h * 128 : (h + 1) * 128].astype(out.dtype)


def leave_kernel(ids, full, keep_out, send_out):
    first = ids[0] == 0
    a = full[:, :512]
    b = full[:, 512:]
    keep_out[...] = jnp.where(first, a, b)
    send_out[...] = jnp.where(first, b, a).astype(BF)


def leave_sum_kernel(ids, outside, own_part, recv_part, keep_out, send_out):
    first = ids[0] == 0
    full = outside[...] + own_part[...] + recv_part[...].astype(F32)
    a = full[:, :512]
    b = full[:, 512:]
    keep_out[...] = jnp.where(first, a, b)
    send_out[...] = jnp.where(first, b, a).astype(BF)


def arrive_kernel(ids, keep, recv, out):
    x = ids[0]
    for src, owner in ((keep, x), (recv, 1 - x)):
        for i in range(NIMG):
            img = src[i * IMG : (i + 1) * IMG].astype(F32).reshape(SIDE, LINE, src.shape[1])
            out[owner * NIMG + i] = img[:, :SIDE, :]


def moments_step(first, second, gradient):
    first_new = FIRST_DECAY * first + (1.0 - FIRST_DECAY) * gradient
    second_new = SECOND_DECAY * second + (1.0 - SECOND_DECAY) * gradient * gradient
    update = (first_new / (1.0 - FIRST_DECAY**STEP)) / (
        jnp.sqrt(second_new / (1.0 - SECOND_DECAY**STEP)) + ADAM_EPSILON
    )
    return second_new, update


def cell(v, lane):
    return jnp.where(lax.broadcasted_iota(jnp.int32, (1, 128), 1) == lane, jnp.sum(v), 0.0)


def lamb_kernel(blocks, *refs):
    grads, masters, firsts, seconds = refs[0:3], refs[3:6], refs[6:9], refs[9:12]
    squares, updates, stat_out = refs[12:15], refs[15:18], refs[18]
    line = jnp.zeros((1, 128), F32)
    for b in range(blocks):
        for m in range(3):
            master = masters[m][b]
            second_new, update = moments_step(firsts[m][b], seconds[m][b], grads[m][b])
            update = update + WEIGHT_DECAY * master
            squares[m][b] = second_new
            updates[m][b] = update
            line = line + cell(master * master, (b * 3 + m) * 2) + cell(update * update, (b * 3 + m) * 2 + 1)
    stat_out[...] = jnp.broadcast_to(line[None], stat_out.shape)


def renew_kernel(blocks, stat, *refs):
    masters, updates, outs, norms_out = refs[0:3], refs[3:6], refs[6:9], refs[9]
    norms = jnp.sqrt(jnp.sum(stat[...], 0))
    norms_out[...] = norms
    for b in range(blocks):
        for m in range(3):
            at = (b * 3 + m) * 2
            ratio = norms[:, at : at + 1] / norms[:, at + 1 : at + 2]
            outs[m][b] = masters[m][b] - MATRIX_RATE * ratio * updates[m][b]


def norm_kernel(blocks, ids, *refs):
    sums = refs[: 3 * blocks]
    params, first, second = refs[3 * blocks : 3 * blocks + 3]
    grads_out, square_out, new_out = refs[3 * blocks + 3 :]
    front = ids[0] == 0
    for b in range(blocks):
        parts = [[], []]
        for n in range(3):
            pair = unpack_rows(sums[3 * b + n][...])
            for kind in range(2):
                v = pair[1 - kind]
                half = v.shape[1] // 2
                parts[kind].append(jnp.where(front, v[:, :half], v[:, half:]))
        for kind in range(2):
            g = lanes(parts[kind])
            second_new, update = moments_step(first[b, kind], second[b, kind], g)
            grads_out[b, kind] = g
            square_out[b, kind] = second_new
            new_out[b, kind] = params[b, kind] - NORM_RATE * update


def body(
    wide,
    block_input,
    out_grad,
    conv_reduce,
    conv_spatial,
    conv_expand,
    first_reduce,
    first_spatial,
    first_expand,
    second_reduce,
    second_spatial,
    second_expand,
    norm_params,
    norm_first,
    norm_second,
):
    blocks = conv_reduce.shape[0]
    population = float(block_input.shape[0] * SIDE * SIDE * wide)
    count = 4 * wide
    x = lax.axis_index("x").astype(jnp.int32)
    core = lax.axis_index("core").astype(jnp.int32)
    w = lax.axis_index("wide").astype(jnp.int32)
    natural = jnp.arange(2 * PIECES, dtype=jnp.int32)
    ids = jnp.concatenate([jnp.stack([x, core, w, jnp.zeros((), jnp.int32)]), natural])

    swap = [(0, 1), (1, 0)]

    def over_core(v):
        return lax.ppermute(v, "core", swap)

    def over_x(v):
        return lax.ppermute(v, "x", swap)

    def share(v, axes):
        return lax.all_to_all(v, axes, 0, 0)

    def run(kernel, outs, *args, **kw):
        return call(kernel, outs, ids, *args, smem=(0,), **kw)

    def gather(shard):
        low = shard.astype(BF)
        return lax.all_gather(low, CROSS, axis=0, tiled=True)

    weights = []
    for b in range(blocks):
        weights.append(
            (
                gather(conv_reduce[b]).reshape(2 * PIECES, -1, 128),
                gather(conv_spatial[b]).reshape(2 * PIECES, -1, 128),
                gather(conv_expand[b]).reshape(2 * PIECES, -1, 512),
            )
        )

    wide_row = norm_params.shape[-1]
    params_all = share(
        jnp.broadcast_to(norm_params.reshape(1, 2 * blocks, wide_row), (4, 2 * blocks, wide_row)), ("x", "core")
    )
    own_all, oth_all = run(
        params_kernel, [((2 * blocks, 2 * wide_row), F32)] * 2, params_all, name="norm_rows"
    )
    own_prm = [own_all[2 * b : 2 * b + 2] for b in range(blocks)]
    oth_prm = [oth_all[2 * b : 2 * b + 2] for b in range(blocks)]

    act = (ROWS, 512)
    keep_x, send_x, keep_g, send_g = run(enter_kernel, [(act, BF)] * 4, block_input, out_grad, name="enter")
    recv_x = over_x(send_x)
    recv_g = over_x(send_g)
    stream, grad = run(join_kernel, [((ROWS, 1024), BF)] * 2, keep_x, recv_x, keep_g, recv_g, name="join")
    low_stream = stream

    inner = (count, 4, 128)
    outer = (2 * wide, 16, 128)
    saved = []
    for b in range(blocks):
        w_reduce, w_spatial, w_expand = weights[b]
        other = over_core(low_stream)
        pre1, low1, stat = run(
            reduce_kernel,
            [((ROWS, 256), F32), ((ROWS, 256), BF), (inner, F32)],
            low_stream,
            other,
            w_reduce,
            name="reduce",
        )
        low1 = over_core(low1)
        stat = share(stat, ALL).reshape(2, 2, wide, 4, 128)
        hid1, moments1, pre2, low2, stat = run(
            functools.partial(spatial_kernel, population),
            [((SPAN, 512), BF), ((8, 256), F32), ((ROWS, 256), F32), ((ROWS, 256), BF), (inner, F32)],
            stat,
            pre1,
            low1,
            own_prm[b],
            oth_prm[b],
            w_spatial,
            scratch=[pltpu.VMEM((3, SPAN + 2 * LINE, 512), BF)],
            name="spatial",
        )
        low2 = over_core(low2)
        stat = share(stat, ALL).reshape(2, 2, wide, 4, 128)
        hid2, moments2, pre3, stat = run(
            functools.partial(expand_kernel, population),
            [((ROWS, 512), BF), ((8, 256), F32), ((ROWS, 1024), F32), (outer, F32)],
            stat,
            pre2,
            low2,
            own_prm[b],
            oth_prm[b],
            w_expand,
            name="expand",
        )
        stat = share(stat, CROSS)
        item = dict(
            xo=low_stream, xt=other, stream=stream, pre1=pre1, hid1=hid1, m1=moments1, pre2=pre2, hid2=hid2, m2=moments2, pre3=pre3
        )
        if b < blocks - 1:
            item["m3"], stream, low_stream = call(
                functools.partial(close_kernel, population),
                [((8, 1024), F32), ((ROWS, 1024), F32), ((ROWS, 1024), BF)],
                stat,
                pre3,
                stream,
                own_prm[b],
                name="close",
            )
        else:
            item["m3"], result, outside, stat = call(
                functools.partial(last_kernel, population),
                [((8, 1024), F32), ((ROWS, 1024), F32), ((ROWS, 1024), F32), (outer, F32)],
                stat,
                pre3,
                stream,
                own_prm[b],
                grad,
                name="last",
            )
        saved.append(item)

    keep, send = run(leave_kernel, [(act, F32), (act, BF)], result, name="leave")
    block_output = run(arrive_kernel, [(block_input.shape, F32)], keep, over_x(send), name="arrive")[0]

    sums = [None] * (3 * blocks)
    local = [None] * blocks
    after = None
    for b in reversed(range(blocks)):
        item = saved[b]
        w_reduce, w_spatial, w_expand = weights[b]
        if after is not None:
            outside, stat = call(
                outer_back_kernel,
                [((ROWS, 1024), F32), (outer, F32)],
                item["m3"],
                item["pre3"],
                item["stream"],
                own_prm[b],
                *after,
                name="outer_back",
            )
        stat = share(stat, CROSS)
        low3, own_part, send, sums[3 * b + 2] = run(
            functools.partial(expand_back_kernel, population),
            [((ROWS, 1024), BF), ((ROWS, 256), F32), ((ROWS, 256), BF), ((16, 128), F32)],
            stat,
            item["m3"],
            item["pre3"],
            outside,
            own_prm[b],
            w_expand,
            name="expand_back",
        )
        recv = over_core(send)
        grad_expand = run(expand_grad_kernel, [(w_expand.shape, BF)], item["hid2"], low3, name="expand_grad")[0]
        upstream, stat = call(
            functools.partial(inner_back_kernel, 256),
            [((ROWS, 256), F32), ((2 * wide, 4, 128), F32)],
            own_part,
            recv,
            item["m2"],
            item["pre2"],
            own_prm[b],
            name="inner_back",
        )
        stat = share(stat, CROSS)
        shifts, own_part, send, sums[3 * b + 1] = run(
            functools.partial(spatial_back_kernel, population),
            [((3, SPAN + 2 * LINE, 256), BF), ((ROWS, 256), F32), ((ROWS, 256), BF), ((4, 128), F32)],
            stat,
            item["m2"],
            item["pre2"],
            upstream,
            own_prm[b],
            w_spatial,
            name="spatial_back",
        )
        recv = over_core(send)
        grad_spatial = run(spatial_grad_kernel, [(w_spatial.shape, BF)], item["hid1"], shifts, name="spatial_grad")[0]
        upstream, stat = call(
            functools.partial(inner_back_kernel, 0),
            [((ROWS, 256), F32), ((2 * wide, 4, 128), F32)],
            own_part,
            recv,
            item["m1"],
            item["pre1"],
            own_prm[b],
            name="inner_back",
        )
        stat = share(stat, CROSS)
        low1, own_part, send, sums[3 * b] = run(
            functools.partial(reduce_back_kernel, population),
            [((ROWS, 256), BF), ((ROWS, 1024), F32), ((ROWS, 1024), BF), ((4, 128), F32)],
            stat,
            item["m1"],
            item["pre1"],
            upstream,
            own_prm[b],
            w_reduce,
            name="reduce_back",
        )
        recv = over_core(send)
        grad_reduce = run(
            reduce_grad_kernel, [(w_reduce.shape, BF)], item["xo"], item["xt"], low1, name="reduce_grad"
        )[0]
        after = (outside, own_part, recv)
        local[b] = (grad_reduce, grad_spatial, grad_expand)

    keep, send = run(leave_sum_kernel, [(act, F32), (act, BF)], *after, name="leave_sum")
    input_grad = run(arrive_kernel, [(block_input.shape, F32)], keep, over_x(send), name="arrive")[0]

    def scatter(parts):
        flat = parts.reshape(-1, parts.shape[-1])
        return lax.psum_scatter(flat, CROSS, scatter_dimension=0, tiled=True).astype(F32)

    gradients = tuple(jnp.stack([scatter(local[b][m]) for b in range(blocks)]) for m in range(3))
    masters = (conv_reduce, conv_spatial, conv_expand)
    firsts = (first_reduce, first_spatial, first_expand)
    seconds = (second_reduce, second_spatial, second_expand)
    shapes = [(m.shape, F32) for m in masters]
    found = call(
        functools.partial(lamb_kernel, blocks),
        shapes + shapes + [((count, 1, 128), F32)],
        *gradients,
        *masters,
        *firsts,
        *seconds,
        name="lamb",
    )
    squares, updates, stat = found[:3], found[3:6], found[6]
    stat = share(stat, ALL)
    renewed = call(
        functools.partial(renew_kernel, blocks), shapes + [((1, 128), F32)], stat, *masters, *updates, name="renew"
    )
    layer_norms = renewed[3][0, : 6 * blocks].reshape(blocks, 3, 2)
    norm_shape = (norm_params.shape, F32)
    norm_grads, norm_square, norm_new = run(
        functools.partial(norm_kernel, blocks), [norm_shape] * 3, *sums, norm_params, norm_first, norm_second, name="norms"
    )
    return (
        block_output,
        input_grad,
        *gradients,
        *squares,
        *renewed[:3],
        norm_grads,
        norm_square,
        norm_new,
        layer_norms,
    )


def solution(mesh):
    wide = mesh.shape["wide"]
    fine = Mesh(np.asarray(mesh.devices).reshape(2, 2, wide), ALL)
    narrow = ("x", "core")
    image = P("wide", None, None, narrow)
    matrix = P(None, "wide", narrow)
    row = P(None, None, narrow, None)
    return jax.shard_map(
        functools.partial(body, wide),
        mesh=fine,
        in_specs=(image,) * 2 + (matrix,) * 9 + (row,) * 3,
        out_specs=(image,) * 2 + (matrix,) * 9 + (row,) * 3 + (P(),),
        check_vma=False,
    )
```

```python
import functools

import jax
import jax.numpy as jnp
import numpy as np
from jax import lax
from jax.experimental import pallas as pl
from jax.experimental.pallas import tpu as pltpu
from jax.sharding import Mesh
from jax.sharding import PartitionSpec as P

STEP = 10
BN_EPS = 1e-05
FIRST_DECAY = 0.9
SECOND_DECAY = 0.999
ADAM_EPSILON = 1e-06
WEIGHT_DECAY = 0.01
MATRIX_RATE = 0.5
NORM_RATE = 0.3

ALL = ("x", "core", "wide")
CROSS = ("x", "wide")
BF = jnp.bfloat16
F32 = jnp.float32

SIDE = 14
LINE = 16
IMG = SIDE * LINE
NIMG = 2
ROWS = NIMG * IMG
SPAN = ROWS + LINE * (NIMG - 1)
PIECES = 8


def dot(a, b):
    return lax.dot_general(a, b, (((1,), (0,)), ((), ())), preferred_element_type=F32)


def dot_nt(a, b):
    return lax.dot_general(a, b, (((1,), (1,)), ((), ())), preferred_element_type=F32)


def dot_tn(a, b):
    return lax.dot_general(a, b, (((0,), (0,)), ((), ())), preferred_element_type=F32)


def lanes(parts):
    return jnp.concatenate(parts, axis=1)


def rows(parts):
    return jnp.concatenate(parts, axis=0)


def sigmoid(v):
    return 0.5 * jnp.tanh(0.5 * v) + 0.5


def silu(v):
    return v * sigmoid(v)


def silu_slope(v):
    s = sigmoid(v)
    return s * (1.0 + v * (1.0 - s))


def inside(shape):
    return (lax.broadcasted_iota(jnp.int32, shape, 0) & (LINE - 1)) < SIDE


def keep_inside(v):
    return jnp.where(inside(v.shape), v, 0.0)


def pack_rows(total, other):
    n = total.shape[1] // 128
    return rows([v[:, i * 128 : (i + 1) * 128] for v in (total, other) for i in range(n)])


def unpack_rows(block):
    n = block.shape[0] // 2
    return tuple(lanes([block[k * n + i : k * n + i + 1] for i in range(n)]) for k in range(2))


def column_sums(a, b):
    return pack_rows(jnp.sum(a, 0, keepdims=True), jnp.sum(b, 0, keepdims=True))


def mean_inverse(block, population):
    total, square = unpack_rows(block)
    mean = total / population
    return mean, lax.rsqrt(square / population - mean * mean + BN_EPS)


class Late:
    def __init__(self, buf, copy):
        self.buf = buf
        self.copy = copy
        self.shape = buf.shape
        self.waited = False
        copy.start()

    def wait(self):
        if not self.waited:
            self.copy.wait()
            self.waited = True

    def __getitem__(self, at):
        self.wait()
        return self.buf[at]


class Pair:
    def __init__(self, near, far):
        self.near = near
        self.far = far
        self.shape = near.shape

    def __getitem__(self, at):
        piece, rest = (at[0], at[1:]) if isinstance(at, tuple) else (at, ())
        inner = (piece & (PIECES - 1),) + rest
        return jnp.where(piece < PIECES, self.near[inner], self.far[inner])


def call(kernel, outs, *args, scratch=(), name=None, smem=(), limit=16, weight=None):
    vmem = pl.BlockSpec(memory_space=pltpu.VMEM)
    in_specs = [pl.BlockSpec(memory_space=pltpu.SMEM) if i in smem else vmem for i in range(len(args))]
    count = len(args)
    ins = list(args)
    scratch = list(scratch)
    cut = False
    if weight is not None:
        parts, (lo, hi) = weight
        ins += parts
        cut = parts[0].shape[1] != hi - lo
        in_specs += [pl.BlockSpec(memory_space=pl.ANY) if cut else vmem] * len(parts)
        if cut:
            scratch += [pltpu.VMEM((2 * PIECES, hi - lo, parts[0].shape[2]), BF), pltpu.SemaphoreType.DMA]
    total = len(ins)

    def whole(*refs):
        operands, results = refs[:count], refs[total:]
        if weight is None:
            return kernel(*operands, *results)
        held = refs[count:total]
        if not cut:
            return kernel(*operands, Pair(*held) if len(held) == 2 else held[0], *results)
        buf, sem = results[-2:]
        late = Late(buf, pltpu.make_async_copy(held[0].at[:, lo:hi], buf, sem))
        kernel(*operands, late, *results[:-2])
        late.wait()

    return pl.pallas_call(
        whole,
        out_shape=[jax.ShapeDtypeStruct(shape, dtype) for shape, dtype in outs],
        in_specs=in_specs,
        out_specs=[vmem] * len(outs),
        scratch_shapes=scratch,
        compiler_params=pltpu.CompilerParams(vmem_limit_bytes=limit * 1024 * 1024),
        name=name,
    )(*ins)


def place(ids, half, piece):
    return ids[4 + PIECES * half + piece]


def origin(ids, at):
    return ids[4 + 2 * PIECES + at]


def piece_of(ids, w, half, piece):
    return w[place(ids, half, piece)]


def expand_weights(ids, w, half):
    def piece(at):
        if w.shape[2] == 512:
            return w[at]
        depth = w.shape[1] // 4
        return lanes([w[at, i * depth : (i + 1) * depth] for i in range(4)])

    return rows([piece(place(ids, half, p)) for p in range(PIECES)])


def deal(ids, held, near, far):
    for start, dst in ((PIECES, far), (0, near)):
        for at in range(PIECES):
            dst[at] = held[origin(ids, start + at)]


def enter_kernel(ids, image_ref, grad_ref, keep_x, send_x, keep_g, send_g):
    x = ids[0]
    for src, keep, send in ((image_ref, keep_x, send_x), (grad_ref, keep_g, send_g)):
        for dst, owner in ((keep, x), (send, 1 - x)):
            for i in range(NIMG):
                img = src[owner * NIMG + i]
                pad = jnp.zeros((SIDE, LINE - SIDE, img.shape[2]), img.dtype)
                full = jnp.concatenate([img, pad], axis=1)
                dst[i * IMG : (i + 1) * IMG] = full.reshape(IMG, img.shape[2])


def join_kernel(ids, keep, recv, out):
    first = ids[0] == 0
    a = keep[...]
    b = recv[...]
    n = a.shape[1]
    out[:, :n] = jnp.where(first, a, b)
    out[:, n:] = jnp.where(first, b, a)


def params_kernel(ids, near_ref, far_ref, own_ref, oth_ref):
    first = ids[0] == 0
    for n, dst in ((0, own_ref), (1, oth_ref)):
        for lo, hi in ((0, 128), (128, 256), (256, 768)):
            a = near_ref[n, :, lo:hi]
            c = far_ref[n, :, lo:hi]
            dst[:, 2 * lo : lo + hi] = jnp.where(first, a, c)
            dst[:, lo + hi : 2 * hi] = jnp.where(first, c, a)


def centred(z, total, pixels):
    return keep_inside(z - total / pixels).astype(BF)


def reduce_kernel(ids, xo, xt, w, pre_out, centred_out, stat_out):
    core = ids[1]
    parts = []
    for c in (core, 1 - core):
        for k in range(2):
            for j in range(2):
                p = 2 * (2 * k + c) + j
                parts.append(lanes([piece_of(ids, w, 0, p), piece_of(ids, w, 1, p)]))
    pre = dot(lanes([xo[...], xt[...]]), rows(parts))
    total = jnp.sum(pre, 0, keepdims=True)
    stats = pack_rows(total, jnp.sum(pre * pre, 0, keepdims=True))
    pre_out[...] = pre
    centred_out[...] = centred(pre, total, NIMG * SIDE * SIDE)
    stat_out[...] = jnp.broadcast_to(stats[None], stat_out.shape)


def both_halves(ids, stat, pre, other, own_prm, oth_prm, lo, population, moments_out):
    x, core, wide = ids[0], ids[1], ids[2]
    own = stat[:, pl.ds(core, 1)]
    oth = stat[:, pl.ds(1 - core, 1)]
    own_sum = jnp.sum(own, axis=(0, 1, 2))
    oth_sum = jnp.sum(oth, axis=(0, 1, 2))
    local = stat[pl.ds(x, 1), pl.ds(1 - core, 1), pl.ds(wide, 1)].reshape(4, 128)
    mean, inverse = mean_inverse(own_sum, population)
    moments_out[...] = rows([mean, inverse, jnp.zeros((6, mean.shape[1]), F32)])
    hid_own = silu(own_prm[0:1, lo : lo + 256] * (pre[...] - mean) * inverse + own_prm[1:2, lo : lo + 256])
    mean_t, inverse_t = mean_inverse(oth_sum, population)
    local_mean = unpack_rows(local)[0] / (NIMG * SIDE * SIDE)
    hid_oth = silu(
        oth_prm[0:1, lo : lo + 256] * (other[...].astype(F32) + (local_mean - mean_t)) * inverse_t
        + oth_prm[1:2, lo : lo + 256]
    )
    hid_own = keep_inside(hid_own)
    hid_oth = keep_inside(hid_oth)
    first = core == 0
    parts = []
    for k in range(2):
        a = hid_own[:, k * 128 : (k + 1) * 128]
        b = hid_oth[:, k * 128 : (k + 1) * 128]
        parts += [jnp.where(first, a, b), jnp.where(first, b, a)]
    return lanes(parts)


def fill_shifts(dst, v, sign):
    for d in range(3):
        shifted = v if d == 1 else pltpu.roll(v, (sign * (d - 1)) % v.shape[0], 0)
        shifted = shifted.astype(BF)
        dst[d, 0:LINE] = jnp.zeros((LINE, v.shape[1]), BF)
        for i in range(NIMG):
            at = LINE + i * (IMG + LINE)
            dst[d, at : at + IMG] = shifted[i * IMG : (i + 1) * IMG]
            dst[d, at + IMG : at + IMG + LINE] = jnp.zeros((LINE, v.shape[1]), BF)


def squeeze(v):
    return rows([v[i * (IMG + LINE) : i * (IMG + LINE) + IMG] for i in range(NIMG)])


def tap_segments(tap, depth):
    lo, hi = tap * 512, (tap + 1) * 512
    found = []
    while lo < hi:
        piece = lo // depth
        end = min(hi, (piece + 1) * depth)
        found.append((piece, lo - piece * depth, end - piece * depth))
        lo = end
    return found


def tap_weights(ids, w, tap):
    return lanes(
        [
            rows([w[place(ids, h, p), a:b] for p, a, b in tap_segments(tap, w.shape[1])])
            for h in range(2)
        ]
    )


def spatial_kernel(
    population, ids, stat, pre, other, own_prm, oth_prm, w, hid_out, moments_out, pre_out, centred_out, stat_out, shifts
):
    hid = both_halves(ids, stat, pre, other, own_prm, oth_prm, 0, population, moments_out)
    fill_shifts(shifts, hid, -1)
    hid_out[...] = shifts[1, LINE : LINE + SPAN]
    acc = None
    for tap in range(9):
        at = (tap // 3) * LINE
        part = dot(shifts[tap % 3, at : at + SPAN], tap_weights(ids, w, tap))
        acc = part if acc is None else acc + part
    pre2 = keep_inside(squeeze(acc))
    total = jnp.sum(pre2, 0, keepdims=True)
    stats = pack_rows(total, jnp.sum(pre2 * pre2, 0, keepdims=True))
    pre_out[...] = pre2
    centred_out[...] = centred(pre2, total, NIMG * SIDE * SIDE)
    stat_out[...] = jnp.broadcast_to(stats[None], stat_out.shape)


def expand_kernel(population, ids, stat, pre, other, own_prm, oth_prm, w, hid_out, moments_out, pre_out, stat_out):
    hid = both_halves(ids, stat, pre, other, own_prm, oth_prm, 256, population, moments_out).astype(BF)
    hid_out[...] = hid
    total = []
    square = []
    for h in range(2):
        pre3 = dot(hid, expand_weights(ids, w, h))
        pre_out[:, h * 512 : (h + 1) * 512] = pre3
        total.append(jnp.sum(pre3, 0, keepdims=True))
        square.append(jnp.sum(pre3 * pre3, 0, keepdims=True))
    stats = pack_rows(lanes(total), lanes(square))
    stat_out[...] = jnp.broadcast_to(stats[None], stat_out.shape)


def close_kernel(population, stat, pre, stream, own_prm, moments_out, out, low_out):
    mean, inverse = mean_inverse(jnp.sum(stat[...], 0), population)
    moments_out[...] = rows([mean, inverse, jnp.zeros((6, mean.shape[1]), F32)])
    v = own_prm[0:1, 512:] * (pre[...] - mean) * inverse + own_prm[1:2, 512:] + stream[...].astype(F32)
    result = keep_inside(silu(v))
    out[...] = result
    low_out[...] = result.astype(BF)


def last_kernel(population, ids, stat, pre, stream, own_prm, keep_g, recv_g, moments_out, out, outside_out, stat_out):
    mean, inverse = mean_inverse(jnp.sum(stat[...], 0), population)
    moments_out[...] = rows([mean, inverse, jnp.zeros((6, mean.shape[1]), F32)])
    normed = (pre[...] - mean) * inverse
    v = own_prm[0:1, 512:] * normed + own_prm[1:2, 512:] + stream[...].astype(F32)
    s = sigmoid(v)
    out[...] = v * s
    first = ids[0] == 0
    a = keep_g[...]
    b = recv_g[...]
    grad = lanes([jnp.where(first, a, b), jnp.where(first, b, a)]).astype(F32)
    outside = keep_inside(grad * (s * (1.0 + v * (1.0 - s))))
    outside_out[...] = outside
    stat_out[...] = jnp.broadcast_to(column_sums(outside, outside * normed)[None], stat_out.shape)


def outer_back_kernel(moments, pre, stream, own_prm, outside_after, own_part, recv_part, outside_out, stat_out):
    mean = moments[0:1]
    inverse = moments[1:2]
    normed = (pre[...] - mean) * inverse
    v = own_prm[0:1, 512:] * normed + own_prm[1:2, 512:] + stream[...].astype(F32)
    upstream = outside_after[...] + own_part[...] + recv_part[...].astype(F32)
    outside = keep_inside(upstream * silu_slope(v))
    outside_out[...] = outside
    stat_out[...] = jnp.broadcast_to(column_sums(outside, outside * normed)[None], stat_out.shape)


def norm_back(sums, population, moments, pre, upstream, gain):
    shift_grad, gain_grad = unpack_rows(sums)
    mean = moments[0:1]
    inverse = moments[1:2]
    normed = (pre[...] - mean) * inverse
    lowered = gain * inverse * (upstream[...] - shift_grad / population - normed * (gain_grad / population))
    return keep_inside(lowered)


def split_cores(ids, parts, own_out, send_out):
    first = ids[1] == 0
    width = parts[0].shape[1]
    for k in range(2):
        a, b = parts[2 * k], parts[2 * k + 1]
        own_out[:, k * width : (k + 1) * width] = jnp.where(first, a, b)
        send_out[:, k * width : (k + 1) * width] = jnp.where(first, b, a).astype(BF)


def expand_back_kernel(population, ids, stat, moments, pre, outside, own_prm, w, low_out, own_out, send_out, sums_out):
    sums = jnp.sum(stat[...], 0)
    sums_out[...] = sums
    low = norm_back(sums, population, moments, pre, outside, own_prm[0:1, 512:]).astype(BF)
    low_out[...] = low
    acc = None
    for h in range(2):
        part = dot_nt(low[:, h * 512 : (h + 1) * 512], expand_weights(ids, w, h))
        acc = part if acc is None else acc + part
    split_cores(ids, [acc[:, n * 128 : (n + 1) * 128] for n in range(4)], own_out, send_out)


def expand_grad(ids, hid, low, held):
    grad = dot_tn(hid[...], low[...])
    lane_blocks = 512 // held.shape[2]
    depth = held.shape[1] // lane_blocks
    for h in range(2):
        for p in range(PIECES):
            piece = grad[p * depth : (p + 1) * depth, h * 512 : (h + 1) * 512].astype(BF)
            if lane_blocks == 1:
                held[h * PIECES + p] = piece
            else:
                for i in range(lane_blocks):
                    held[h * PIECES + p, i * depth : (i + 1) * depth] = piece[:, i * 128 : (i + 1) * 128]


def inner_back_kernel(lo, own_part, recv_part, moments, pre, own_prm, out, stat_out):
    normed = (pre[...] - moments[0:1]) * moments[1:2]
    v = own_prm[0:1, lo : lo + 256] * normed + own_prm[1:2, lo : lo + 256]
    upstream = (own_part[...] + recv_part[...].astype(F32)) * silu_slope(v)
    upstream = keep_inside(upstream)
    out[...] = upstream
    stat_out[...] = jnp.broadcast_to(column_sums(upstream, upstream * normed)[None], stat_out.shape)


def spatial_back_kernel(population, ids, stat, moments, pre, upstream, own_prm, w, shifts, own_out, send_out, sums_out):
    sums = jnp.sum(stat[...], 0)
    sums_out[...] = sums
    low = norm_back(sums, population, moments, pre, upstream, own_prm[0:1, 256:512])
    fill_shifts(shifts, low, 1)
    acc = None
    for tap in range(9):
        at = LINE * (2 - tap // 3)
        part = dot_nt(shifts[tap % 3, at : at + SPAN], tap_weights(ids, w, tap))
        acc = part if acc is None else acc + part
    acc = squeeze(acc)
    split_cores(ids, [acc[:, n * 128 : (n + 1) * 128] for n in range(4)], own_out, send_out)


def spatial_grad(ids, hid, shifts, held):
    turned = hid[...].T
    depth = held.shape[1]
    for tap in range(9):
        at = LINE * (2 - tap // 3)
        grad = dot(turned, shifts[tap % 3, at : at + SPAN]).astype(BF)
        row = 0
        for p, a, b in tap_segments(tap, depth):
            for h in range(2):
                held[h * PIECES + p, a:b] = grad[row : row + b - a, h * 128 : (h + 1) * 128]
            row += b - a


def reduce_back_kernel(population, ids, stat, moments, pre, upstream, own_prm, w, low_out, own_out, send_out, sums_out):
    sums = jnp.sum(stat[...], 0)
    sums_out[...] = sums
    low = norm_back(sums, population, moments, pre, upstream, own_prm[0:1, 0:256]).astype(BF)
    low_out[...] = low
    core = ids[1]
    for c, dst in ((1 - core, send_out), (core, own_out)):
        for k in range(2):
            for j in range(2):
                p = 2 * (2 * k + c) + j
                part = dot_nt(low, lanes([piece_of(ids, w, 0, p), piece_of(ids, w, 1, p)]))
                at = k * 512 + j * 256
                dst[:, at : at + 256] = part.astype(dst.dtype)


def reduce_grad(ids, xo, xt, low, held):
    core = ids[1]
    for c, src in ((core, xo), (1 - core, xt)):
        grad = dot_tn(src[...], low[...]).astype(BF)
        for k in range(2):
            for j in range(2):
                p = 2 * (2 * k + c) + j
                at = k * 512 + j * 256
                for h in range(2):
                    held[h * PIECES + p] = grad[at : at + 256, h * 128 : (h + 1) * 128]


def leave_kernel(ids, full, keep_out, send_out):
    first = ids[0] == 0
    a = full[:, :512]
    b = full[:, 512:]
    keep_out[...] = jnp.where(first, a, b)
    send_out[...] = jnp.where(first, b, a).astype(BF)


def leave_sum_kernel(ids, outside, own_part, recv_part, keep_out, send_out):
    first = ids[0] == 0
    full = outside[...] + own_part[...] + recv_part[...].astype(F32)
    a = full[:, :512]
    b = full[:, 512:]
    keep_out[...] = jnp.where(first, a, b)
    send_out[...] = jnp.where(first, b, a).astype(BF)


def arrive_kernel(ids, keep, recv, out):
    x = ids[0]
    for src, owner in ((keep, x), (recv, 1 - x)):
        for i in range(NIMG):
            img = src[i * IMG : (i + 1) * IMG].astype(F32).reshape(SIDE, LINE, src.shape[1])
            out[owner * NIMG + i] = img[:, :SIDE, :]


def moments_step(first, second, gradient):
    first_new = FIRST_DECAY * first + (1.0 - FIRST_DECAY) * gradient
    second_new = SECOND_DECAY * second + (1.0 - SECOND_DECAY) * gradient * gradient
    update = (first_new / (1.0 - FIRST_DECAY**STEP)) / (
        jnp.sqrt(second_new / (1.0 - SECOND_DECAY**STEP)) + ADAM_EPSILON
    )
    return second_new, update


def cell(v, lane):
    return jnp.where(lax.broadcasted_iota(jnp.int32, (1, 128), 1) == lane, jnp.sum(v), 0.0)


def lamb_kernel(items, lines, *refs):
    count = len(items)
    grads, masters, firsts, seconds = (refs[i * count : (i + 1) * count] for i in range(4))
    before = refs[4 * count : 4 * count + lines]
    outs = refs[len(refs) - 3 * count - 1 :]
    line = jnp.zeros((1, 128), F32)
    for ref in before:
        line = line + ref[...]
    for i, (b, m) in enumerate(items):
        grad = grads[i][...]
        master = masters[i][0]
        if grad.shape != master.shape:
            depth = master.shape[0]
            grad = lanes([grad[n * depth : (n + 1) * depth] for n in range(grad.shape[0] // depth)])
        second_new, update = moments_step(firsts[i][0], seconds[i][0], grad)
        update = update + WEIGHT_DECAY * master
        outs[3 * i][0] = grad
        outs[3 * i + 1][0] = second_new
        outs[3 * i + 2][0] = update
        line = line + cell(master * master, (b * 3 + m) * 2) + cell(update * update, (b * 3 + m) * 2 + 1)
    outs[-1][...] = jnp.broadcast_to(line[None], outs[-1].shape) if len(outs[-1].shape) == 3 else line


def lamb(items, grads, masters, firsts, seconds, filled, lines, count):
    whole = pl.BlockSpec(memory_space=pltpu.VMEM)
    args, specs, outs, out_specs, aliases = list(grads), [whole] * len(items), [], [], {}

    def one(b, m):
        return pl.BlockSpec((1,) + masters[m].shape[1:], lambda _: (b, 0, 0))

    for source in (masters, firsts, seconds):
        for b, m in items:
            args.append(source[m])
            specs.append(one(b, m))
    for line in lines:
        args.append(line)
        specs.append(whole)
    for b, m in items:
        for k in range(3):
            if filled[m] is not None:
                aliases[len(args)] = len(outs)
                args.append(filled[m][k])
                specs.append(pl.BlockSpec(memory_space=pl.ANY))
            outs.append(jax.ShapeDtypeStruct(masters[m].shape, F32))
            out_specs.append(one(b, m))
    outs.append(jax.ShapeDtypeStruct((count, 1, 128) if count else (1, 128), F32))
    out_specs.append(whole)
    found = pl.pallas_call(
        functools.partial(lamb_kernel, items, len(lines)),
        out_shape=outs,
        grid=(1,),
        in_specs=specs,
        out_specs=out_specs,
        input_output_aliases=aliases,
        compiler_params=pltpu.CompilerParams(vmem_limit_bytes=16 * 1024 * 1024),
        name="lamb",
    )(*args)
    for i, (b, m) in enumerate(items):
        filled[m] = tuple(found[3 * i : 3 * i + 3])
    return found[-1]


def renew_kernel(blocks, stat, *refs):
    masters, updates, outs, norms_out = refs[0:3], refs[3:6], refs[6:9], refs[9]
    norms = jnp.sqrt(jnp.sum(stat[...], 0))
    norms_out[...] = norms
    for b in range(blocks):
        for m in range(3):
            at = (b * 3 + m) * 2
            ratio = norms[:, at : at + 1] / norms[:, at + 1 : at + 2]
            outs[m][b] = masters[m][b] - MATRIX_RATE * ratio * updates[m][b]


def norm_kernel(blocks, ids, *refs):
    sums = refs[: 3 * blocks]
    params, first, second = refs[3 * blocks : 3 * blocks + 3]
    grads_out, square_out, new_out = refs[3 * blocks + 3 :]
    front = ids[0] == 0
    for b in range(blocks):
        parts = [[], []]
        for n in range(3):
            pair = unpack_rows(sums[3 * b + n][...])
            for kind in range(2):
                v = pair[1 - kind]
                half = v.shape[1] // 2
                parts[kind].append(jnp.where(front, v[:, :half], v[:, half:]))
        for kind in range(2):
            g = lanes(parts[kind])
            second_new, update = moments_step(first[b, kind], second[b, kind], g)
            grads_out[b, kind] = g
            square_out[b, kind] = second_new
            new_out[b, kind] = params[b, kind] - NORM_RATE * update


def exchange(step):
    pairs = []
    for i in range(32):
        core = (i >> 3) & 1
        pairs.append((i, i ^ (4, 2, 16 if core else 1, 1 if core else 16)[step]))
    return pairs


class Gather:
    def __init__(self, held):
        self.parts = (held,)

    def step(self, step, *after):
        if after:
            self.wait(*after)
        held = self.held()
        self.parts = (held, lax.ppermute(held, ALL, exchange(step)))

    def wait(self, *after):
        self.parts = order(self.parts, *after)

    def held(self):
        return self.parts[0] if len(self.parts) == 1 else jnp.concatenate(self.parts, 0)

    def last(self):
        return self.parts[-1]

    def weight(self):
        return list(self.parts), (0, self.parts[0].shape[1])


def order(value, *before):
    return lax.optimization_barrier((value, before))[0]


class Scatter:
    def __init__(self, near=None, far=None, parts=()):
        self.terms = [] if near is None else [near]
        self.far = far
        self.parts = parts

    def wait(self, *after):
        for part in self.parts:
            part.wait(*after)
        if self.terms:
            self.terms = list(lax.optimization_barrier(tuple(self.terms) + after)[: len(self.terms)])

    def total(self, lo, hi):
        found = [term[lo:hi].astype(F32) for term in self.terms]
        if self.parts:
            found.append(jnp.concatenate([part.total(lo, hi) for part in self.parts], axis=1))
        return functools.reduce(jnp.add, found)

    def step(self, step, *after):
        if step == 3:
            send = self.far
        else:
            if after:
                self.wait(*after)
            size = 1 << step
            send = self.total(size, 2 * size).astype(BF)
        self.terms.append(lax.ppermute(send, ALL, exchange(step)))
        return send


def body(
    wide,
    block_input,
    out_grad,
    conv_reduce,
    conv_spatial,
    conv_expand,
    first_reduce,
    first_spatial,
    first_expand,
    second_reduce,
    second_spatial,
    second_expand,
    norm_params,
    norm_first,
    norm_second,
):
    blocks = conv_reduce.shape[0]
    population = float(block_input.shape[0] * SIDE * SIDE * wide)
    count = 4 * wide
    x = lax.axis_index("x").astype(jnp.int32)
    core = lax.axis_index("core").astype(jnp.int32)
    w = lax.axis_index("wide").astype(jnp.int32)
    fast = wide == PIECES
    here = jnp.stack([x, core, w, jnp.zeros((), jnp.int32)])
    count_up = jnp.arange(2 * PIECES, dtype=jnp.int32)
    ids = jnp.concatenate([here, count_up, count_up])
    to_x = count_up // PIECES
    to_w = count_up % PIECES

    apart_x = to_x ^ x
    apart_w = to_w ^ w
    back = jnp.where(core == 0, apart_w & 1, apart_x)
    front = jnp.where(core == 0, apart_x, apart_w & 1)
    places = front * 8 + back * 4 + ((apart_w & 2) | (apart_w >> 2))
    bit3, bit2 = count_up >> 3, (count_up >> 2) & 1
    from_x = x ^ jnp.where(core == 0, bit3, bit2)
    from_w = w ^ (jnp.where(core == 0, bit2, bit3) | (count_up & 2) | ((count_up & 1) << 2))
    relative = jnp.concatenate([here, places, from_x * PIECES + from_w])

    swap = [(0, 1), (1, 0)]

    def over_core(v):
        return lax.ppermute(v, "core", swap)

    def over_x(v):
        return lax.ppermute(v, "x", swap)

    def share(v, axes):
        return lax.all_to_all(v, axes, 0, 0)

    def run(kernel, outs, *args, places=None, **kw):
        return call(kernel, outs, ids if places is None else places, *args, smem=(0,), **kw)

    wide_row = norm_params.shape[-1]
    near = norm_params.reshape(2 * blocks, wide_row)
    both = jnp.stack([near, over_core(near)])
    far = over_x(both)
    own_all, oth_all = run(
        params_kernel, [((2 * blocks, 2 * wide_row), F32)] * 2, both, far, name="norm_rows"
    )
    own_prm = [own_all[2 * b : 2 * b + 2] for b in range(blocks)]
    oth_prm = [oth_all[2 * b : 2 * b + 2] for b in range(blocks)]

    act = (ROWS, 512)
    keep_x, send_x, keep_g, send_g = run(enter_kernel, [(act, BF)] * 4, block_input, out_grad, name="enter")
    recv_x = over_x(send_x)
    low_stream = stream = run(join_kernel, [((ROWS, 1024), BF)], keep_x, recv_x, name="join")[0]

    def gather(shard, columns):
        whole = lax.all_gather(shard.astype(BF), CROSS, axis=0, tiled=True).reshape(2 * PIECES, -1, columns)
        return [whole], (0, whole.shape[1])

    table = relative if fast else ids
    tables = [table] + [ids] * (blocks - 1)
    gathers = []
    weights = None
    if fast:
        depth = conv_expand.shape[1]

        def shards(b):
            blocked = conv_expand[b].astype(BF).reshape(depth, 4, 128).swapaxes(0, 1).reshape(4 * depth, 128)
            return [conv_reduce[b].astype(BF), conv_spatial[b].astype(BF), blocked]

        gathers = [Gather(shard[None]) for shard in shards(0)]
        gathers[0].step(0, send_x)
        gathers[0].step(1)
        gathers[1].step(0, gathers[0].parts[0])
        gathers[0].step(2, recv_x, far)
        gathers[1].step(1, gathers[0].parts[0])
        gathers[2].step(0, gathers[1].parts[0])
        gathers[2].step(1)
        gathers[0].step(3)
        wholes = [lax.all_gather(jnp.concatenate(shards(b)), CROSS, axis=0, tiled=False) for b in range(1, blocks)]
        one = conv_reduce.shape[1]
        two = one + conv_spatial.shape[1]
        cuts = ((0, one), (one, two), (two, two + 4 * depth))
    else:
        weights = [
            (gather(conv_reduce[b], 128), gather(conv_spatial[b], 128), gather(conv_expand[b], 512)) for b in range(blocks)
        ]

    def weight_of(b, m):
        if not fast:
            return weights[b][m]
        return gathers[m].weight() if b == 0 else ([wholes[b - 1]], cuts[m])

    def advance(stage, stat, out):
        if not fast:
            return
        if stage == 1:
            gathers[1].step(2, out)
            gathers[1].step(3, stat)
        elif stage == 2:
            gathers[2].step(2, gathers[1].last())
            gathers[2].step(3, out)

    inner = (count, 4, 128)
    outer = (2 * wide, 16, 128)
    saved = []
    for b in range(blocks):
        other = over_core(low_stream)
        pre1, low1, stat = run(
            reduce_kernel,
            [((ROWS, 256), F32), ((ROWS, 256), BF), (inner, F32)],
            low_stream,
            other,
            weight=weight_of(b, 0),
            places=tables[b],
            name="reduce",
        )
        low1 = over_core(low1)
        stat = share(stat, ALL)
        advance(3 * b + 1, stat, pre1)
        stat = stat.reshape(2, 2, wide, 4, 128)
        hid1, moments1, pre2, low2, stat = run(
            functools.partial(spatial_kernel, population),
            [((SPAN, 512), BF), ((8, 256), F32), ((ROWS, 256), F32), ((ROWS, 256), BF), (inner, F32)],
            stat,
            pre1,
            low1,
            own_prm[b],
            oth_prm[b],
            weight=weight_of(b, 1),
            scratch=[pltpu.VMEM((3, SPAN + 2 * LINE, 512), BF)],
            places=tables[b],
            name="spatial",
        )
        low2 = over_core(low2)
        stat = share(stat, ALL)
        advance(3 * b + 2, stat, pre2)
        if fast and b == 0:
            stat, *wholes = lax.optimization_barrier((stat, *wholes))
        stat = stat.reshape(2, 2, wide, 4, 128)
        before = stat
        hid2, moments2, pre3, stat = run(
            functools.partial(expand_kernel, population),
            [((ROWS, 512), BF), ((8, 256), F32), ((ROWS, 1024), F32), (outer, F32)],
            stat,
            pre2,
            low2,
            own_prm[b],
            oth_prm[b],
            weight=weight_of(b, 2),
            places=tables[b],
            name="expand",
        )
        if b == blocks - 1:
            recv_g = over_x(order(send_g, before))
        stat = share(stat, CROSS)
        advance(3 * b + 3, stat, pre3)
        item = dict(
            xo=low_stream, xt=other, stream=stream, pre1=pre1, hid1=hid1, m1=moments1, pre2=pre2, hid2=hid2, m2=moments2, pre3=pre3
        )
        if b < blocks - 1:
            item["m3"], stream, low_stream = call(
                functools.partial(close_kernel, population),
                [((8, 1024), F32), ((ROWS, 1024), F32), ((ROWS, 1024), BF)],
                stat,
                pre3,
                stream,
                own_prm[b],
                name="close",
            )
        else:
            item["m3"], result, outside, stat = run(
                functools.partial(last_kernel, population),
                [((8, 1024), F32), ((ROWS, 1024), F32), ((ROWS, 1024), F32), (outer, F32)],
                stat,
                pre3,
                stream,
                own_prm[b],
                keep_g,
                recv_g,
                name="last",
            )
        saved.append(item)

    tasks = {}

    def hook(kind, b, grads, stat):
        if not fast:
            return []
        tasks[kind, b] = Scatter(*grads)
        sends = [tasks[kind, b].step(3)]

        def more(step, *names):
            for name in names:
                sends.append(tasks[name].step(step, stat))

        if b == 1 and kind == "reduce":
            more(2, ("expand", 1), ("spatial", 1))
        if b == 0 and kind == "expand":
            tasks["big", 1] = Scatter(parts=(tasks["expand", 1], tasks["spatial", 1]))
            more(2, ("reduce", 1))
            more(1, ("big", 1))
        if b == 0 and kind == "spatial":
            more(2, ("expand", 0))
            more(1, ("reduce", 1))
            more(0, ("big", 1))
        return sends

    def pinned(value, *names):
        for name in names:
            if name in tasks:
                value, tasks[name].terms[-1] = lax.optimization_barrier((value, tasks[name].terms[-1]))
        return value

    def hurry(stat):
        if not fast:
            return stat
        return order(
            stat,
            tasks["spatial", 0].step(2, stat),
            tasks["expand", 0].step(1, stat),
            tasks["reduce", 1].step(0, stat),
        )

    def finish():
        tasks["expand", 0].step(0)
        gate = tasks["reduce", 0].step(2)
        tasks["spatial", 0].step(1)
        tasks["spatial", 0].step(0)
        tasks["reduce", 0].step(1)
        tasks["reduce", 0].step(0)
        batches = []
        big = tasks["big", 1].total(0, 1)[0]
        cut = big.shape[0] - conv_spatial.shape[1]
        batches.append((((1, 1), (1, 2)), (big[cut:], big[:cut])))
        batches.append((((1, 0),), (tasks["reduce", 1].total(0, 1)[0],)))
        batches.append((((0, 2),), (tasks["expand", 0].total(0, 1)[0],)))
        batches.append((((0, 1),), (tasks["spatial", 0].total(0, 1)[0],)))
        batches.append((((0, 0),), (tasks["reduce", 0].total(0, 1)[0],)))
        return batches, gate

    def gradient(b, m, kernel, *args, name):
        parts, (lo, hi) = weight_of(b, m)
        shape = (hi - lo, parts[0].shape[2])
        whole = pltpu.VMEM((2 * PIECES,) + shape, BF)
        half = ((PIECES,) + shape, BF)

        def halves(ids, *refs):
            kernel(ids, *refs[:-3], refs[-1])
            deal(ids, refs[-1], refs[-3], refs[-2])

        return run(halves, [half] * 2, *args, scratch=[whole], places=table, name=name)

    sums = [None] * (3 * blocks)
    local = [None] * blocks
    after = None
    for b in reversed(range(blocks)):
        item = saved[b]
        w_reduce, w_spatial, w_expand = (weight_of(b, m) for m in range(3))
        if after is not None:
            outside, stat = call(
                outer_back_kernel,
                [((ROWS, 1024), F32), (outer, F32)],
                item["m3"],
                item["pre3"],
                item["stream"],
                own_prm[b],
                *after,
                name="outer_back",
            )
        stat = share(stat, CROSS)
        low3, own_part, send, sums[3 * b + 2] = run(
            functools.partial(expand_back_kernel, population),
            [((ROWS, 1024), BF), ((ROWS, 256), F32), ((ROWS, 256), BF), ((16, 128), F32)],
            stat,
            item["m3"],
            item["pre3"],
            outside,
            own_prm[b],
            weight=w_expand,
            places=tables[b],
            name="expand_back",
        )
        recv = over_core(send)
        grad_expand = gradient(b, 2, expand_grad, item["hid2"], low3, name="expand_grad")
        own_part = order(own_part, *grad_expand, *hook("expand", b, grad_expand, stat))
        upstream, stat = call(
            functools.partial(inner_back_kernel, 256),
            [((ROWS, 256), F32), ((2 * wide, 4, 128), F32)],
            own_part,
            recv,
            item["m2"],
            item["pre2"],
            own_prm[b],
            name="inner_back",
        )
        stat = pinned(share(stat, CROSS), ("expand", b))
        shifts, own_part, send, sums[3 * b + 1] = run(
            functools.partial(spatial_back_kernel, population),
            [((3, SPAN + 2 * LINE, 256), BF), ((ROWS, 256), F32), ((ROWS, 256), BF), ((4, 128), F32)],
            stat,
            item["m2"],
            item["pre2"],
            upstream,
            own_prm[b],
            weight=w_spatial,
            places=tables[b],
            name="spatial_back",
        )
        recv = over_core(send)
        grad_spatial = gradient(b, 1, spatial_grad, item["hid1"], shifts, name="spatial_grad")
        own_part = order(own_part, *grad_spatial, *hook("spatial", b, grad_spatial, stat))
        upstream, stat = call(
            functools.partial(inner_back_kernel, 0),
            [((ROWS, 256), F32), ((2 * wide, 4, 128), F32)],
            own_part,
            recv,
            item["m1"],
            item["pre1"],
            own_prm[b],
            name="inner_back",
        )
        stat = share(stat, CROSS)
        if b == 0:
            stat = hurry(pinned(stat, ("spatial", 0)))
        low1, own_part, send, sums[3 * b] = run(
            functools.partial(reduce_back_kernel, population),
            [((ROWS, 256), BF), ((ROWS, 1024), F32), ((ROWS, 1024), BF), ((4, 128), F32)],
            stat,
            item["m1"],
            item["pre1"],
            upstream,
            own_prm[b],
            weight=w_reduce,
            places=tables[b],
            name="reduce_back",
        )
        recv = over_core(send)
        grad_reduce = gradient(b, 0, reduce_grad, item["xo"], item["xt"], low1, name="reduce_grad")
        own_part = order(own_part, *grad_reduce, *hook("reduce", b, grad_reduce, stat))
        after = (outside, own_part, recv)
        local[b] = (grad_reduce, grad_spatial, grad_expand)

    def scatter(pair):
        flat = jnp.concatenate(pair).reshape(-1, pair[0].shape[-1])
        return lax.psum_scatter(flat, CROSS, scatter_dimension=0, tiled=True).astype(F32)

    masters = (conv_reduce, conv_spatial, conv_expand)
    firsts = (first_reduce, first_spatial, first_expand)
    seconds = (second_reduce, second_spatial, second_expand)
    filled = [None] * 3
    lines = []
    if fast:
        batches, gate = finish()
    else:
        batches = [(((b, m),), (scatter(local[b][m]),)) for b in range(blocks) for m in range(3)]
        gate = after[1]
    keep_out, send = run(leave_kernel, [(act, F32), (act, BF)], order(result, gate), name="leave")
    recv_out = over_x(send)
    keep_in, send = run(leave_sum_kernel, [(act, F32), (act, BF)], *order(after, gate), name="leave_sum")
    recv_in = over_x(send)
    for n, (items, grads) in enumerate(batches):
        last = n == len(batches) - 1
        line = lamb(items, grads, masters, firsts, seconds, filled, lines if last else [], count if last else 0)
        lines.append(line)
    gradients = [filled[m][0] for m in range(3)]
    squares = [filled[m][1] for m in range(3)]
    updates = [filled[m][2] for m in range(3)]
    line = order(lines[-1], recv_out, recv_in)
    stat = share(line, ALL)
    keep_out = order(keep_out, line)
    keep_in = order(keep_in, line)
    block_output = run(arrive_kernel, [(block_input.shape, F32)], keep_out, recv_out, name="arrive")[0]
    input_grad = run(arrive_kernel, [(block_input.shape, F32)], keep_in, recv_in, name="arrive")[0]
    shapes = [(m.shape, F32) for m in masters]
    renewed = call(
        functools.partial(renew_kernel, blocks), shapes + [((1, 128), F32)], stat, *masters, *updates, name="renew"
    )
    layer_norms = renewed[3][0, : 6 * blocks].reshape(blocks, 3, 2)
    norm_shape = (norm_params.shape, F32)
    norm_grads, norm_square, norm_new = run(
        functools.partial(norm_kernel, blocks), [norm_shape] * 3, *sums, norm_params, norm_first, norm_second, name="norms"
    )
    return (
        block_output,
        input_grad,
        *gradients,
        *squares,
        *renewed[:3],
        norm_grads,
        norm_square,
        norm_new,
        layer_norms,
    )


def solution(mesh):
    wide = mesh.shape["wide"]
    fine = Mesh(np.asarray(mesh.devices).reshape(2, 2, wide), ALL)
    narrow = ("x", "core")
    image = P("wide", None, None, narrow)
    matrix = P(None, "wide", narrow)
    row = P(None, None, narrow, None)
    return jax.shard_map(
        functools.partial(body, wide),
        mesh=fine,
        in_specs=(image,) * 2 + (matrix,) * 9 + (row,) * 3,
        out_specs=(image,) * 2 + (matrix,) * 9 + (row,) * 3 + (P(),),
        check_vma=False,
    )
```

```python
import functools

import jax
import jax.numpy as jnp
import numpy as np
from jax import lax
from jax.experimental import pallas as pl
from jax.experimental.pallas import tpu as pltpu
from jax.sharding import Mesh
from jax.sharding import PartitionSpec as P

STEP = 10
BN_EPS = 1e-05
FIRST_DECAY = 0.9
SECOND_DECAY = 0.999
ADAM_EPSILON = 1e-06
WEIGHT_DECAY = 0.01
MATRIX_RATE = 0.5
NORM_RATE = 0.3

ALL = ("x", "core", "wide")
CROSS = ("x", "wide")
BF = jnp.bfloat16
F32 = jnp.float32

SIDE = 14
LINE = 16
IMG = SIDE * LINE
NIMG = 2
ROWS = NIMG * IMG
SPAN = ROWS + LINE * (NIMG - 1)
PIECES = 8


def dot(a, b):
    return lax.dot_general(a, b, (((1,), (0,)), ((), ())), preferred_element_type=F32)


def dot_nt(a, b):
    return lax.dot_general(a, b, (((1,), (1,)), ((), ())), preferred_element_type=F32)


def dot_tn(a, b):
    return lax.dot_general(a, b, (((0,), (0,)), ((), ())), preferred_element_type=F32)


def lanes(parts):
    return jnp.concatenate(parts, axis=1)


def rows(parts):
    return jnp.concatenate(parts, axis=0)


def sigmoid(v):
    return 0.5 * jnp.tanh(0.5 * v) + 0.5


def silu(v):
    return v * sigmoid(v)


def silu_slope(v):
    s = sigmoid(v)
    return s * (1.0 + v * (1.0 - s))


def inside(shape):
    return (lax.broadcasted_iota(jnp.int32, shape, 0) & (LINE - 1)) < SIDE


def keep_inside(v):
    return jnp.where(inside(v.shape), v, 0.0)


def pack_rows(total, other):
    n = total.shape[1] // 128
    return rows([v[:, i * 128 : (i + 1) * 128] for v in (total, other) for i in range(n)])


def unpack_rows(block):
    n = block.shape[0] // 2
    return tuple(lanes([block[k * n + i : k * n + i + 1] for i in range(n)]) for k in range(2))


def column_sums(a, b):
    return pack_rows(jnp.sum(a, 0, keepdims=True), jnp.sum(b, 0, keepdims=True))


def mean_inverse(block, population):
    total, square = unpack_rows(block)
    mean = total / population
    return mean, lax.rsqrt(square / population - mean * mean + BN_EPS)


class Late:
    def __init__(self, buf, copy):
        self.buf = buf
        self.copy = copy
        self.shape = buf.shape
        self.waited = False
        copy.start()

    def wait(self):
        if not self.waited:
            self.copy.wait()
            self.waited = True

    def __getitem__(self, at):
        self.wait()
        return self.buf[at]


class Pair:
    def __init__(self, near, far):
        self.near = near
        self.far = far
        self.shape = near.shape

    def __getitem__(self, at):
        piece, rest = (at[0], at[1:]) if isinstance(at, tuple) else (at, ())
        inner = (piece & (PIECES - 1),) + rest
        return jnp.where(piece < PIECES, self.near[inner], self.far[inner])


def call(kernel, outs, *args, scratch=(), name=None, smem=(), limit=16, weight=None):
    vmem = pl.BlockSpec(memory_space=pltpu.VMEM)
    in_specs = [pl.BlockSpec(memory_space=pltpu.SMEM) if i in smem else vmem for i in range(len(args))]
    count = len(args)
    ins = list(args)
    scratch = list(scratch)
    cut = False
    if weight is not None:
        parts, (lo, hi) = weight
        ins += parts
        cut = parts[0].shape[1] != hi - lo
        in_specs += [pl.BlockSpec(memory_space=pl.ANY) if cut else vmem] * len(parts)
        if cut:
            scratch += [pltpu.VMEM((2 * PIECES, hi - lo, parts[0].shape[2]), BF), pltpu.SemaphoreType.DMA]
    total = len(ins)

    def whole(*refs):
        operands, results = refs[:count], refs[total:]
        if weight is None:
            return kernel(*operands, *results)
        held = refs[count:total]
        if not cut:
            return kernel(*operands, Pair(*held) if len(held) == 2 else held[0], *results)
        buf, sem = results[-2:]
        late = Late(buf, pltpu.make_async_copy(held[0].at[:, lo:hi], buf, sem))
        kernel(*operands, late, *results[:-2])
        late.wait()

    return pl.pallas_call(
        whole,
        out_shape=[jax.ShapeDtypeStruct(shape, dtype) for shape, dtype in outs],
        in_specs=in_specs,
        out_specs=[vmem] * len(outs),
        scratch_shapes=scratch,
        compiler_params=pltpu.CompilerParams(vmem_limit_bytes=limit * 1024 * 1024),
        name=name,
    )(*ins)


def place(ids, half, piece):
    return ids[4 + PIECES * half + piece]


def origin(ids, at):
    return ids[4 + 2 * PIECES + at]


def piece_of(ids, w, half, piece):
    return w[place(ids, half, piece)]


def expand_weights(ids, w, half):
    def piece(at):
        if w.shape[2] == 512:
            return w[at]
        depth = w.shape[1] // 4
        return lanes([w[at, i * depth : (i + 1) * depth] for i in range(4)])

    return rows([piece(place(ids, half, p)) for p in range(PIECES)])


def deal(ids, held, near, far):
    for start, dst in ((PIECES, far), (0, near)):
        for at in range(PIECES):
            dst[at] = held[origin(ids, start + at)]


def enter_kernel(ids, image_ref, grad_ref, keep_x, send_x, keep_g, send_g):
    x = ids[0]
    for src, keep, send in ((image_ref, keep_x, send_x), (grad_ref, keep_g, send_g)):
        for dst, owner in ((keep, x), (send, 1 - x)):
            for i in range(NIMG):
                img = src[owner * NIMG + i]
                pad = jnp.zeros((SIDE, LINE - SIDE, img.shape[2]), img.dtype)
                full = jnp.concatenate([img, pad], axis=1)
                dst[i * IMG : (i + 1) * IMG] = full.reshape(IMG, img.shape[2])


def join_kernel(ids, keep, recv, out):
    first = ids[0] == 0
    a = keep[...]
    b = recv[...]
    n = a.shape[1]
    out[:, :n] = jnp.where(first, a, b)
    out[:, n:] = jnp.where(first, b, a)


def params_kernel(ids, near_ref, far_ref, own_ref, oth_ref):
    first = ids[0] == 0
    for n, dst in ((0, own_ref), (1, oth_ref)):
        for lo, hi in ((0, 128), (128, 256), (256, 768)):
            a = near_ref[n, :, lo:hi]
            c = far_ref[n, :, lo:hi]
            dst[:, 2 * lo : lo + hi] = jnp.where(first, a, c)
            dst[:, lo + hi : 2 * hi] = jnp.where(first, c, a)


def centred(z, total, pixels):
    return keep_inside(z - total / pixels).astype(BF)


def reduce_kernel(ids, xo, xt, w, pre_out, centred_out, stat_out):
    core = ids[1]
    parts = []
    for c in (core, 1 - core):
        for k in range(2):
            for j in range(2):
                p = 2 * (2 * k + c) + j
                parts.append(lanes([piece_of(ids, w, 0, p), piece_of(ids, w, 1, p)]))
    pre = dot(lanes([xo[...], xt[...]]), rows(parts))
    total = jnp.sum(pre, 0, keepdims=True)
    stats = pack_rows(total, jnp.sum(pre * pre, 0, keepdims=True))
    pre_out[...] = pre
    centred_out[...] = centred(pre, total, NIMG * SIDE * SIDE)
    stat_out[...] = jnp.broadcast_to(stats[None], stat_out.shape)


def both_halves(ids, stat, pre, other, own_prm, oth_prm, lo, population, moments_out):
    x, core, wide = ids[0], ids[1], ids[2]
    own = stat[:, pl.ds(core, 1)]
    oth = stat[:, pl.ds(1 - core, 1)]
    own_sum = jnp.sum(own, axis=(0, 1, 2))
    oth_sum = jnp.sum(oth, axis=(0, 1, 2))
    local = stat[pl.ds(x, 1), pl.ds(1 - core, 1), pl.ds(wide, 1)].reshape(4, 128)
    mean, inverse = mean_inverse(own_sum, population)
    moments_out[...] = rows([mean, inverse, jnp.zeros((6, mean.shape[1]), F32)])
    hid_own = silu(own_prm[0:1, lo : lo + 256] * (pre[...] - mean) * inverse + own_prm[1:2, lo : lo + 256])
    mean_t, inverse_t = mean_inverse(oth_sum, population)
    local_mean = unpack_rows(local)[0] / (NIMG * SIDE * SIDE)
    hid_oth = silu(
        oth_prm[0:1, lo : lo + 256] * (other[...].astype(F32) + (local_mean - mean_t)) * inverse_t
        + oth_prm[1:2, lo : lo + 256]
    )
    hid_own = keep_inside(hid_own)
    hid_oth = keep_inside(hid_oth)
    first = core == 0
    parts = []
    for k in range(2):
        a = hid_own[:, k * 128 : (k + 1) * 128]
        b = hid_oth[:, k * 128 : (k + 1) * 128]
        parts += [jnp.where(first, a, b), jnp.where(first, b, a)]
    return lanes(parts)


def fill_shifts(dst, v, sign):
    for d in range(3):
        shifted = v if d == 1 else pltpu.roll(v, (sign * (d - 1)) % v.shape[0], 0)
        shifted = shifted.astype(BF)
        dst[d, 0:LINE] = jnp.zeros((LINE, v.shape[1]), BF)
        for i in range(NIMG):
            at = LINE + i * (IMG + LINE)
            dst[d, at : at + IMG] = shifted[i * IMG : (i + 1) * IMG]
            dst[d, at + IMG : at + IMG + LINE] = jnp.zeros((LINE, v.shape[1]), BF)


def squeeze(v):
    return rows([v[i * (IMG + LINE) : i * (IMG + LINE) + IMG] for i in range(NIMG)])


def tap_segments(tap, depth):
    lo, hi = tap * 512, (tap + 1) * 512
    found = []
    while lo < hi:
        piece = lo // depth
        end = min(hi, (piece + 1) * depth)
        found.append((piece, lo - piece * depth, end - piece * depth))
        lo = end
    return found


def tap_weights(ids, w, tap):
    return lanes(
        [
            rows([w[place(ids, h, p), a:b] for p, a, b in tap_segments(tap, w.shape[1])])
            for h in range(2)
        ]
    )


def spatial_kernel(
    population, ids, stat, pre, other, own_prm, oth_prm, w, hid_out, moments_out, pre_out, centred_out, stat_out, shifts
):
    hid = both_halves(ids, stat, pre, other, own_prm, oth_prm, 0, population, moments_out)
    fill_shifts(shifts, hid, -1)
    hid_out[...] = shifts[1, LINE : LINE + SPAN]
    acc = None
    for tap in range(9):
        at = (tap // 3) * LINE
        part = dot(shifts[tap % 3, at : at + SPAN], tap_weights(ids, w, tap))
        acc = part if acc is None else acc + part
    pre2 = keep_inside(squeeze(acc))
    total = jnp.sum(pre2, 0, keepdims=True)
    stats = pack_rows(total, jnp.sum(pre2 * pre2, 0, keepdims=True))
    pre_out[...] = pre2
    centred_out[...] = centred(pre2, total, NIMG * SIDE * SIDE)
    stat_out[...] = jnp.broadcast_to(stats[None], stat_out.shape)


def expand_kernel(population, ids, stat, pre, other, own_prm, oth_prm, w, hid_out, moments_out, pre_out, stat_out):
    hid = both_halves(ids, stat, pre, other, own_prm, oth_prm, 256, population, moments_out).astype(BF)
    hid_out[...] = hid
    total = []
    square = []
    for h in range(2):
        pre3 = dot(hid, expand_weights(ids, w, h))
        pre_out[:, h * 512 : (h + 1) * 512] = pre3
        total.append(jnp.sum(pre3, 0, keepdims=True))
        square.append(jnp.sum(pre3 * pre3, 0, keepdims=True))
    stats = pack_rows(lanes(total), lanes(square))
    stat_out[...] = jnp.broadcast_to(stats[None], stat_out.shape)


def close_kernel(population, stat, pre, stream, own_prm, moments_out, out, low_out):
    mean, inverse = mean_inverse(jnp.sum(stat[...], 0), population)
    moments_out[...] = rows([mean, inverse, jnp.zeros((6, mean.shape[1]), F32)])
    v = own_prm[0:1, 512:] * (pre[...] - mean) * inverse + own_prm[1:2, 512:] + stream[...].astype(F32)
    result = keep_inside(silu(v))
    out[...] = result
    low_out[...] = result.astype(BF)


def last_kernel(population, ids, stat, pre, stream, own_prm, keep_g, recv_g, moments_out, out, outside_out, stat_out):
    mean, inverse = mean_inverse(jnp.sum(stat[...], 0), population)
    moments_out[...] = rows([mean, inverse, jnp.zeros((6, mean.shape[1]), F32)])
    normed = (pre[...] - mean) * inverse
    v = own_prm[0:1, 512:] * normed + own_prm[1:2, 512:] + stream[...].astype(F32)
    s = sigmoid(v)
    out[...] = v * s
    first = ids[0] == 0
    a = keep_g[...]
    b = recv_g[...]
    grad = lanes([jnp.where(first, a, b), jnp.where(first, b, a)]).astype(F32)
    outside = keep_inside(grad * (s * (1.0 + v * (1.0 - s))))
    outside_out[...] = outside
    stat_out[...] = jnp.broadcast_to(column_sums(outside, outside * normed)[None], stat_out.shape)


def outer_back_kernel(moments, pre, stream, own_prm, outside_after, own_part, recv_part, outside_out, stat_out):
    mean = moments[0:1]
    inverse = moments[1:2]
    normed = (pre[...] - mean) * inverse
    v = own_prm[0:1, 512:] * normed + own_prm[1:2, 512:] + stream[...].astype(F32)
    upstream = outside_after[...] + own_part[...] + recv_part[...].astype(F32)
    outside = keep_inside(upstream * silu_slope(v))
    outside_out[...] = outside
    stat_out[...] = jnp.broadcast_to(column_sums(outside, outside * normed)[None], stat_out.shape)


def norm_back(sums, population, moments, pre, upstream, gain):
    shift_grad, gain_grad = unpack_rows(sums)
    mean = moments[0:1]
    inverse = moments[1:2]
    normed = (pre[...] - mean) * inverse
    lowered = gain * inverse * (upstream[...] - shift_grad / population - normed * (gain_grad / population))
    return keep_inside(lowered)


def split_cores(ids, parts, own_out, send_out):
    first = ids[1] == 0
    width = parts[0].shape[1]
    for k in range(2):
        a, b = parts[2 * k], parts[2 * k + 1]
        own_out[:, k * width : (k + 1) * width] = jnp.where(first, a, b)
        send_out[:, k * width : (k + 1) * width] = jnp.where(first, b, a).astype(BF)


def expand_back_kernel(population, ids, stat, moments, pre, outside, own_prm, w, low_out, own_out, send_out, sums_out):
    sums = jnp.sum(stat[...], 0)
    sums_out[...] = sums
    low = norm_back(sums, population, moments, pre, outside, own_prm[0:1, 512:]).astype(BF)
    low_out[...] = low
    acc = None
    for h in range(2):
        part = dot_nt(low[:, h * 512 : (h + 1) * 512], expand_weights(ids, w, h))
        acc = part if acc is None else acc + part
    split_cores(ids, [acc[:, n * 128 : (n + 1) * 128] for n in range(4)], own_out, send_out)


def expand_grad(ids, hid, low, held):
    grad = dot_tn(hid[...], low[...])
    lane_blocks = 512 // held.shape[2]
    depth = held.shape[1] // lane_blocks
    for h in range(2):
        for p in range(PIECES):
            piece = grad[p * depth : (p + 1) * depth, h * 512 : (h + 1) * 512].astype(BF)
            if lane_blocks == 1:
                held[h * PIECES + p] = piece
            else:
                for i in range(lane_blocks):
                    held[h * PIECES + p, i * depth : (i + 1) * depth] = piece[:, i * 128 : (i + 1) * 128]


def inner_back_kernel(lo, own_part, recv_part, moments, pre, own_prm, out, stat_out):
    normed = (pre[...] - moments[0:1]) * moments[1:2]
    v = own_prm[0:1, lo : lo + 256] * normed + own_prm[1:2, lo : lo + 256]
    upstream = (own_part[...] + recv_part[...].astype(F32)) * silu_slope(v)
    upstream = keep_inside(upstream)
    out[...] = upstream
    stat_out[...] = jnp.broadcast_to(column_sums(upstream, upstream * normed)[None], stat_out.shape)


def spatial_back_kernel(population, ids, stat, moments, pre, upstream, own_prm, w, shifts, own_out, send_out, sums_out):
    sums = jnp.sum(stat[...], 0)
    sums_out[...] = sums
    low = norm_back(sums, population, moments, pre, upstream, own_prm[0:1, 256:512])
    fill_shifts(shifts, low, 1)
    acc = None
    for tap in range(9):
        at = LINE * (2 - tap // 3)
        part = dot_nt(shifts[tap % 3, at : at + SPAN], tap_weights(ids, w, tap))
        acc = part if acc is None else acc + part
    acc = squeeze(acc)
    split_cores(ids, [acc[:, n * 128 : (n + 1) * 128] for n in range(4)], own_out, send_out)


def spatial_grad(ids, hid, shifts, held):
    turned = hid[...].T
    depth = held.shape[1]
    for tap in range(9):
        at = LINE * (2 - tap // 3)
        grad = dot(turned, shifts[tap % 3, at : at + SPAN]).astype(BF)
        row = 0
        for p, a, b in tap_segments(tap, depth):
            for h in range(2):
                held[h * PIECES + p, a:b] = grad[row : row + b - a, h * 128 : (h + 1) * 128]
            row += b - a


def reduce_back_kernel(population, ids, stat, moments, pre, upstream, own_prm, w, low_out, own_out, send_out, sums_out):
    sums = jnp.sum(stat[...], 0)
    sums_out[...] = sums
    low = norm_back(sums, population, moments, pre, upstream, own_prm[0:1, 0:256]).astype(BF)
    low_out[...] = low
    core = ids[1]
    for c, dst in ((1 - core, send_out), (core, own_out)):
        for k in range(2):
            for j in range(2):
                p = 2 * (2 * k + c) + j
                part = dot_nt(low, lanes([piece_of(ids, w, 0, p), piece_of(ids, w, 1, p)]))
                at = k * 512 + j * 256
                dst[:, at : at + 256] = part.astype(dst.dtype)


def reduce_grad(ids, xo, xt, low, held):
    core = ids[1]
    for c, src in ((core, xo), (1 - core, xt)):
        grad = dot_tn(src[...], low[...]).astype(BF)
        for k in range(2):
            for j in range(2):
                p = 2 * (2 * k + c) + j
                at = k * 512 + j * 256
                for h in range(2):
                    held[h * PIECES + p] = grad[at : at + 256, h * 128 : (h + 1) * 128]


def leave_kernel(ids, full, keep_out, send_out):
    first = ids[0] == 0
    a = full[:, :512]
    b = full[:, 512:]
    keep_out[...] = jnp.where(first, a, b)
    send_out[...] = jnp.where(first, b, a).astype(BF)


def leave_sum_kernel(ids, outside, own_part, recv_part, keep_out, send_out):
    first = ids[0] == 0
    full = outside[...] + own_part[...] + recv_part[...].astype(F32)
    a = full[:, :512]
    b = full[:, 512:]
    keep_out[...] = jnp.where(first, a, b)
    send_out[...] = jnp.where(first, b, a).astype(BF)


def arrive_kernel(ids, keep, recv, out):
    x = ids[0]
    for src, owner in ((keep, x), (recv, 1 - x)):
        for i in range(NIMG):
            img = src[i * IMG : (i + 1) * IMG].astype(F32).reshape(SIDE, LINE, src.shape[1])
            out[owner * NIMG + i] = img[:, :SIDE, :]


def moments_step(first, second, gradient):
    first_new = FIRST_DECAY * first + (1.0 - FIRST_DECAY) * gradient
    second_new = SECOND_DECAY * second + (1.0 - SECOND_DECAY) * gradient * gradient
    update = (first_new / (1.0 - FIRST_DECAY**STEP)) / (
        jnp.sqrt(second_new / (1.0 - SECOND_DECAY**STEP)) + ADAM_EPSILON
    )
    return second_new, update


def cell(v, lane):
    return jnp.where(lax.broadcasted_iota(jnp.int32, (1, 128), 1) == lane, jnp.sum(v), 0.0)


def lamb_kernel(plans, cuts, lines, arrays, *refs):
    blocks = iter(refs[:arrays])
    refs = refs[arrays:]
    count = sum(len(cut) for cut in cuts)
    masters, firsts, seconds = (refs[i * count : (i + 1) * count] for i in range(3))
    before = refs[3 * count : 3 * count + lines]
    outs = refs[len(refs) - 3 * count - 1 :]
    line = jnp.zeros((1, 128), F32)
    for ref in before:
        line = line + ref[...]
    i = 0
    for plan, cut in zip(plans, cuts):
        total = evaluate(plan, blocks)[0]
        for (b, m), lo, hi in cut:
            grad = total[lo:hi]
            master = masters[i][0]
            if grad.shape != master.shape:
                depth = master.shape[0]
                grad = lanes([grad[n * depth : (n + 1) * depth] for n in range(grad.shape[0] // depth)])
            second_new, update = moments_step(firsts[i][0], seconds[i][0], grad)
            update = update + WEIGHT_DECAY * master
            outs[3 * i][0] = grad
            outs[3 * i + 1][0] = second_new
            outs[3 * i + 2][0] = update
            line = line + cell(master * master, (b * 3 + m) * 2) + cell(update * update, (b * 3 + m) * 2 + 1)
            i += 1
    outs[-1][...] = jnp.broadcast_to(line[None], outs[-1].shape) if len(outs[-1].shape) == 3 else line


def lamb(sources, masters, firsts, seconds, filled, lines, count):
    whole = pl.BlockSpec(memory_space=pltpu.VMEM)
    tasks = [task for task, _ in sources]
    cuts = [cut for _, cut in sources]
    items = [item for cut in cuts for item, _, _ in cut]
    args, specs = slices(tasks, 1, 0)
    arrays = len(args)
    outs, out_specs, aliases = [], [], {}

    def one(b, m):
        return pl.BlockSpec((1,) + masters[m].shape[1:], lambda _: (b, 0, 0))

    for source in (masters, firsts, seconds):
        for b, m in items:
            args.append(source[m])
            specs.append(one(b, m))
    for line in lines:
        args.append(line)
        specs.append(whole)
    for b, m in items:
        for k in range(3):
            if filled[m] is not None:
                aliases[len(args)] = len(outs)
                args.append(filled[m][k])
                specs.append(pl.BlockSpec(memory_space=pl.ANY))
            outs.append(jax.ShapeDtypeStruct(masters[m].shape, F32))
            out_specs.append(one(b, m))
    outs.append(jax.ShapeDtypeStruct((count, 1, 128) if count else (1, 128), F32))
    out_specs.append(whole)
    found = pl.pallas_call(
        functools.partial(lamb_kernel, [task.plan() for task in tasks], cuts, len(lines), arrays),
        out_shape=outs,
        grid=(1,),
        in_specs=specs,
        out_specs=out_specs,
        input_output_aliases=aliases,
        compiler_params=pltpu.CompilerParams(vmem_limit_bytes=16 * 1024 * 1024),
        name="lamb",
    )(*args)
    for i, (b, m) in enumerate(items):
        filled[m] = tuple(found[3 * i : 3 * i + 3])
    return found[-1]


def renew_kernel(blocks, stat, *refs):
    masters, updates, outs, norms_out = refs[0:3], refs[3:6], refs[6:9], refs[9]
    norms = jnp.sqrt(jnp.sum(stat[...], 0))
    norms_out[...] = norms
    for b in range(blocks):
        for m in range(3):
            at = (b * 3 + m) * 2
            ratio = norms[:, at : at + 1] / norms[:, at + 1 : at + 2]
            outs[m][b] = masters[m][b] - MATRIX_RATE * ratio * updates[m][b]


def norm_kernel(blocks, ids, *refs):
    sums = refs[: 3 * blocks]
    params, first, second = refs[3 * blocks : 3 * blocks + 3]
    grads_out, square_out, new_out = refs[3 * blocks + 3 :]
    front = ids[0] == 0
    for b in range(blocks):
        parts = [[], []]
        for n in range(3):
            pair = unpack_rows(sums[3 * b + n][...])
            for kind in range(2):
                v = pair[1 - kind]
                half = v.shape[1] // 2
                parts[kind].append(jnp.where(front, v[:, :half], v[:, half:]))
        for kind in range(2):
            g = lanes(parts[kind])
            second_new, update = moments_step(first[b, kind], second[b, kind], g)
            grads_out[b, kind] = g
            square_out[b, kind] = second_new
            new_out[b, kind] = params[b, kind] - NORM_RATE * update


def exchange(step):
    pairs = []
    for i in range(32):
        core = (i >> 3) & 1
        pairs.append((i, i ^ (4, 2, 16 if core else 1, 1 if core else 16)[step]))
    return pairs


class Gather:
    def __init__(self, held):
        self.parts = (held,)

    def step(self, step, *after):
        if after:
            self.wait(*after)
        held = self.held()
        self.parts = (held, lax.ppermute(held, ALL, exchange(step)))

    def wait(self, *after):
        self.parts = order(self.parts, *after)

    def held(self):
        return self.parts[0] if len(self.parts) == 1 else jnp.concatenate(self.parts, 0)

    def last(self):
        return self.parts[-1]

    def weight(self):
        return list(self.parts), (0, self.parts[0].shape[1])


def order(value, *before):
    return lax.optimization_barrier((value, before))[0]


class Scatter:
    def __init__(self, near=None, far=None, parts=()):
        self.terms = [] if near is None else [near]
        self.far = far
        self.parts = parts

    def wait(self, *after):
        for part in self.parts:
            part.wait(*after)
        if self.terms:
            self.terms = list(order(tuple(self.terms), *after))

    def arrays(self):
        return [array for part in self.parts for array in part.arrays()] + self.terms

    def rows(self):
        return self.terms[0].shape[1] if self.terms else sum(part.rows() for part in self.parts)

    def plan(self):
        return [part.plan() for part in self.parts], len(self.terms)

    def send(self, step, value):
        self.terms.append(lax.ppermute(value, ALL, exchange(step)))


def evaluate(plan, refs):
    parts, count = plan
    found = [jnp.concatenate([evaluate(part, refs) for part in parts], axis=1)] if parts else []
    found += [next(refs)[...].astype(F32) for _ in range(count)]
    return functools.reduce(jnp.add, found)


def slices(tasks, size, at):
    arrays = [array for task in tasks for array in task.arrays()]
    return arrays, [pl.BlockSpec((size,) + array.shape[1:], lambda _: (at, 0, 0)) for array in arrays]


def add_up_kernel(plans, *refs):
    blocks = iter(refs[: len(refs) - len(plans)])
    for plan, out in zip(plans, refs[len(refs) - len(plans) :]):
        out[...] = evaluate(plan, blocks).astype(out.dtype)


def advance_sums(steps, *after):
    arrays, specs, outs, plans = [], [], [], []
    for task, step in steps:
        task.wait(*after)
    for task, step in steps:
        size = 1 << step
        more, blocks = slices([task], size, 1)
        arrays += more
        specs += blocks
        outs.append(jax.ShapeDtypeStruct((size, task.rows(), 128), BF))
        plans.append(task.plan())
    sends = pl.pallas_call(
        functools.partial(add_up_kernel, plans),
        out_shape=outs,
        grid=(1,),
        in_specs=specs,
        out_specs=[pl.BlockSpec(memory_space=pltpu.VMEM)] * len(outs),
        compiler_params=pltpu.CompilerParams(vmem_limit_bytes=16 * 1024 * 1024),
        name="add_up",
    )(*arrays)
    for (task, step), value in zip(steps, sends):
        task.send(step, value)
    return sends


def body(
    wide,
    block_input,
    out_grad,
    conv_reduce,
    conv_spatial,
    conv_expand,
    first_reduce,
    first_spatial,
    first_expand,
    second_reduce,
    second_spatial,
    second_expand,
    norm_params,
    norm_first,
    norm_second,
):
    blocks = conv_reduce.shape[0]
    population = float(block_input.shape[0] * SIDE * SIDE * wide)
    count = 4 * wide
    x = lax.axis_index("x").astype(jnp.int32)
    core = lax.axis_index("core").astype(jnp.int32)
    w = lax.axis_index("wide").astype(jnp.int32)
    fast = wide == PIECES
    here = jnp.stack([x, core, w, jnp.zeros((), jnp.int32)])
    count_up = jnp.arange(2 * PIECES, dtype=jnp.int32)
    ids = jnp.concatenate([here, count_up, count_up])
    to_x = count_up // PIECES
    to_w = count_up % PIECES

    apart_x = to_x ^ x
    apart_w = to_w ^ w
    back = jnp.where(core == 0, apart_w & 1, apart_x)
    front = jnp.where(core == 0, apart_x, apart_w & 1)
    places = front * 8 + back * 4 + ((apart_w & 2) | (apart_w >> 2))
    bit3, bit2 = count_up >> 3, (count_up >> 2) & 1
    from_x = x ^ jnp.where(core == 0, bit3, bit2)
    from_w = w ^ (jnp.where(core == 0, bit2, bit3) | (count_up & 2) | ((count_up & 1) << 2))
    relative = jnp.concatenate([here, places, from_x * PIECES + from_w])

    swap = [(0, 1), (1, 0)]

    def over_core(v):
        return lax.ppermute(v, "core", swap)

    def over_x(v):
        return lax.ppermute(v, "x", swap)

    def share(v, axes):
        return lax.all_to_all(v, axes, 0, 0)

    def run(kernel, outs, *args, places=None, **kw):
        return call(kernel, outs, ids if places is None else places, *args, smem=(0,), **kw)

    wide_row = norm_params.shape[-1]
    near = norm_params.reshape(2 * blocks, wide_row)
    both = jnp.stack([near, over_core(near)])
    far = over_x(both)
    own_all, oth_all = run(
        params_kernel, [((2 * blocks, 2 * wide_row), F32)] * 2, both, far, name="norm_rows"
    )
    own_prm = [own_all[2 * b : 2 * b + 2] for b in range(blocks)]
    oth_prm = [oth_all[2 * b : 2 * b + 2] for b in range(blocks)]

    act = (ROWS, 512)
    keep_x, send_x, keep_g, send_g = run(enter_kernel, [(act, BF)] * 4, block_input, out_grad, name="enter")
    recv_x = over_x(send_x)
    low_stream = stream = run(join_kernel, [((ROWS, 1024), BF)], keep_x, recv_x, name="join")[0]

    def gather(shard, columns):
        whole = lax.all_gather(shard.astype(BF), CROSS, axis=0, tiled=True).reshape(2 * PIECES, -1, columns)
        return [whole], (0, whole.shape[1])

    table = relative if fast else ids
    tables = [table] + [ids] * (blocks - 1)
    gathers = []
    weights = None
    if fast:
        depth = conv_expand.shape[1]

        def shards(b):
            blocked = conv_expand[b].astype(BF).reshape(depth, 4, 128).swapaxes(0, 1).reshape(4 * depth, 128)
            return [conv_reduce[b].astype(BF), conv_spatial[b].astype(BF), blocked]

        gathers = [Gather(shard[None]) for shard in shards(0)]
        gathers[0].step(0, send_x)
        gathers[0].step(1)
        gathers[1].step(0, gathers[0].parts[0])
        gathers[0].step(2, recv_x, far)
        gathers[1].step(1, gathers[0].parts[0])
        gathers[2].step(0, gathers[1].parts[0])
        gathers[2].step(1)
        gathers[0].step(3)
        wholes = [lax.all_gather(jnp.concatenate(shards(b)), CROSS, axis=0, tiled=False) for b in range(1, blocks)]
        one = conv_reduce.shape[1]
        two = one + conv_spatial.shape[1]
        cuts = ((0, one), (one, two), (two, two + 4 * depth))
    else:
        weights = [
            (gather(conv_reduce[b], 128), gather(conv_spatial[b], 128), gather(conv_expand[b], 512)) for b in range(blocks)
        ]

    def weight_of(b, m):
        if not fast:
            return weights[b][m]
        return gathers[m].weight() if b == 0 else ([wholes[b - 1]], cuts[m])

    def advance(stage, stat, out):
        if not fast:
            return
        if stage == 1:
            gathers[1].step(2, out)
            gathers[1].step(3, stat)
        elif stage == 2:
            gathers[2].step(2, gathers[1].last())
            gathers[2].step(3, out)

    inner = (count, 4, 128)
    outer = (2 * wide, 16, 128)
    saved = []
    for b in range(blocks):
        other = over_core(low_stream)
        pre1, low1, stat = run(
            reduce_kernel,
            [((ROWS, 256), F32), ((ROWS, 256), BF), (inner, F32)],
            low_stream,
            other,
            weight=weight_of(b, 0),
            places=tables[b],
            name="reduce",
        )
        low1 = over_core(low1)
        stat = share(stat, ALL)
        advance(3 * b + 1, stat, pre1)
        stat = stat.reshape(2, 2, wide, 4, 128)
        hid1, moments1, pre2, low2, stat = run(
            functools.partial(spatial_kernel, population),
            [((SPAN, 512), BF), ((8, 256), F32), ((ROWS, 256), F32), ((ROWS, 256), BF), (inner, F32)],
            stat,
            pre1,
            low1,
            own_prm[b],
            oth_prm[b],
            weight=weight_of(b, 1),
            scratch=[pltpu.VMEM((3, SPAN + 2 * LINE, 512), BF)],
            places=tables[b],
            name="spatial",
        )
        low2 = over_core(low2)
        if b > 0:
            stat = order(stat, low2)
        stat = share(stat, ALL)
        advance(3 * b + 2, stat, pre2)
        if fast and b == 0:
            stat, *wholes = lax.optimization_barrier((stat, *wholes))
        stat = stat.reshape(2, 2, wide, 4, 128)
        before = stat
        hid2, moments2, pre3, stat = run(
            functools.partial(expand_kernel, population),
            [((ROWS, 512), BF), ((8, 256), F32), ((ROWS, 1024), F32), (outer, F32)],
            stat,
            pre2,
            low2,
            own_prm[b],
            oth_prm[b],
            weight=weight_of(b, 2),
            places=tables[b],
            name="expand",
        )
        if b == blocks - 1:
            recv_g = over_x(order(send_g, before))
        stat = share(stat, CROSS)
        advance(3 * b + 3, stat, pre3)
        item = dict(
            xo=low_stream, xt=other, stream=stream, pre1=pre1, hid1=hid1, m1=moments1, pre2=pre2, hid2=hid2, m2=moments2, pre3=pre3
        )
        if b < blocks - 1:
            item["m3"], stream, low_stream = call(
                functools.partial(close_kernel, population),
                [((8, 1024), F32), ((ROWS, 1024), F32), ((ROWS, 1024), BF)],
                stat,
                pre3,
                stream,
                own_prm[b],
                name="close",
            )
        else:
            item["m3"], result, outside, stat = run(
                functools.partial(last_kernel, population),
                [((8, 1024), F32), ((ROWS, 1024), F32), ((ROWS, 1024), F32), (outer, F32)],
                stat,
                pre3,
                stream,
                own_prm[b],
                keep_g,
                recv_g,
                name="last",
            )
        saved.append(item)

    tasks = {}

    def hook(kind, b, grads):
        if not fast:
            return []
        near, far = grads
        tasks[kind, b] = Scatter(near)
        tasks[kind, b].send(3, far)
        return [far]

    def ahead(kind, b, stat):
        if not fast:
            return stat
        steps = []
        if b == 1 and kind == "spatial":
            stat = order(stat, tasks["expand", 1].terms[-1])
        if b == 0 and kind == "reduce":
            stat = order(stat, tasks["big"].terms[-1])
        if b == 1 and kind == "reduce":
            tasks["big"] = Scatter(parts=(tasks["expand", 1], tasks["spatial", 1]))
            steps = [(tasks["big"], 2)]
        if b == 0 and kind == "expand":
            steps = [(tasks["reduce", 1], 2), (tasks["big"], 1)]
        if b == 0 and kind == "spatial":
            steps = [(tasks["expand", 0], 2), (tasks["reduce", 1], 1), (tasks["big"], 0)]
        if b == 0 and kind == "reduce":
            steps = [(tasks["spatial", 0], 2), (tasks["expand", 0], 1), (tasks["reduce", 1], 0)]
        return order(stat, *advance_sums(steps, stat)) if steps else stat

    def whole(task, b, m):
        return task, [((b, m), 0, task.rows())]

    def step_of(sources, last=False):
        line = lamb(sources, masters, firsts, seconds, filled, lines if last else [], count if last else 0)
        lines.append(line)
        return line

    images = []

    def finish_images(gate):
        keep_out, send = run(leave_kernel, [(act, F32), (act, BF)], order(result, gate), name="leave")
        recv_out = over_x(send)
        keep_in, send = run(leave_sum_kernel, [(act, F32), (act, BF)], *order(after, gate), name="leave_sum")
        recv_in = over_x(send)
        images.extend(run(arrive_kernel, [(block_input.shape, F32)], keep_out, recv_out, name="arrive"))
        images.extend(run(arrive_kernel, [(block_input.shape, F32)], keep_in, recv_in, name="arrive"))

    def finish():
        small, middle, large = (tasks[kind, 0] for kind in ("expand", "reduce", "spatial"))
        big = tasks["big"]
        cut = 4 * conv_expand.shape[1]
        line = step_of([(big, [((1, 2), 0, cut), ((1, 1), cut, big.rows())])])
        sent = advance_sums([(large, 1)], line, norm_grads)
        sent = advance_sums([(middle, 2), (small, 0)], sent, tasks["reduce", 1].terms[-1])
        finish_images(sent[0])
        sent = advance_sums([(middle, 1)], sent)
        line = step_of([whole(tasks["reduce", 1], 1, 0)])
        sent = advance_sums([(large, 0)], sent, small.terms[-1], line)
        advance_sums([(middle, 0)], sent)
        line = step_of([whole(small, 0, 2)])
        for task in (large, middle):
            task.wait(line, *images)
        return [[whole(large, 0, 1), whole(middle, 0, 0)]]

    def gradient(b, m, kernel, *args, name):
        parts, (lo, hi) = weight_of(b, m)
        shape = (hi - lo, parts[0].shape[2])
        whole = pltpu.VMEM((2 * PIECES,) + shape, BF)
        half = ((PIECES,) + shape, BF)

        def halves(ids, *refs):
            kernel(ids, *refs[:-3], refs[-1])
            deal(ids, refs[-1], refs[-3], refs[-2])

        return run(halves, [half] * 2, *args, scratch=[whole], places=table, name=name)

    sums = [None] * (3 * blocks)
    local = [None] * blocks
    after = None
    for b in reversed(range(blocks)):
        item = saved[b]
        w_reduce, w_spatial, w_expand = (weight_of(b, m) for m in range(3))
        if after is not None:
            outside, stat = call(
                outer_back_kernel,
                [((ROWS, 1024), F32), (outer, F32)],
                item["m3"],
                item["pre3"],
                item["stream"],
                own_prm[b],
                *after,
                name="outer_back",
            )
        stat = ahead("expand", b, share(stat, CROSS))
        low3, own_part, send, sums[3 * b + 2] = run(
            functools.partial(expand_back_kernel, population),
            [((ROWS, 1024), BF), ((ROWS, 256), F32), ((ROWS, 256), BF), ((16, 128), F32)],
            stat,
            item["m3"],
            item["pre3"],
            outside,
            own_prm[b],
            weight=w_expand,
            places=tables[b],
            name="expand_back",
        )
        recv = over_core(send)
        grad_expand = gradient(b, 2, expand_grad, item["hid2"], low3, name="expand_grad")
        own_part = order(own_part, *grad_expand, *hook("expand", b, grad_expand))
        upstream, stat = call(
            functools.partial(inner_back_kernel, 256),
            [((ROWS, 256), F32), ((2 * wide, 4, 128), F32)],
            own_part,
            recv,
            item["m2"],
            item["pre2"],
            own_prm[b],
            name="inner_back",
        )
        stat = ahead("spatial", b, share(stat, CROSS))
        shifts, own_part, send, sums[3 * b + 1] = run(
            functools.partial(spatial_back_kernel, population),
            [((3, SPAN + 2 * LINE, 256), BF), ((ROWS, 256), F32), ((ROWS, 256), BF), ((4, 128), F32)],
            stat,
            item["m2"],
            item["pre2"],
            upstream,
            own_prm[b],
            weight=w_spatial,
            places=tables[b],
            name="spatial_back",
        )
        recv = over_core(send)
        grad_spatial = gradient(b, 1, spatial_grad, item["hid1"], shifts, name="spatial_grad")
        own_part = order(own_part, *grad_spatial, *hook("spatial", b, grad_spatial))
        upstream, stat = call(
            functools.partial(inner_back_kernel, 0),
            [((ROWS, 256), F32), ((2 * wide, 4, 128), F32)],
            own_part,
            recv,
            item["m1"],
            item["pre1"],
            own_prm[b],
            name="inner_back",
        )
        stat = ahead("reduce", b, share(stat, CROSS))
        low1, own_part, send, sums[3 * b] = run(
            functools.partial(reduce_back_kernel, population),
            [((ROWS, 256), BF), ((ROWS, 1024), F32), ((ROWS, 1024), BF), ((4, 128), F32)],
            stat,
            item["m1"],
            item["pre1"],
            upstream,
            own_prm[b],
            weight=w_reduce,
            places=tables[b],
            name="reduce_back",
        )
        recv = over_core(send)
        grad_reduce = gradient(b, 0, reduce_grad, item["xo"], item["xt"], low1, name="reduce_grad")
        own_part = order(own_part, *grad_reduce, *hook("reduce", b, grad_reduce))
        after = (outside, own_part, recv)
        local[b] = (grad_reduce, grad_spatial, grad_expand)

    def scatter(pair):
        flat = jnp.concatenate(pair).reshape(-1, pair[0].shape[-1])
        return lax.psum_scatter(flat, CROSS, scatter_dimension=0, tiled=True).astype(F32)

    norm_shape = (norm_params.shape, F32)
    norm_grads, norm_square, norm_new = run(
        functools.partial(norm_kernel, blocks), [norm_shape] * 3, *sums, norm_params, norm_first, norm_second, name="norms"
    )
    masters = (conv_reduce, conv_spatial, conv_expand)
    firsts = (first_reduce, first_spatial, first_expand)
    seconds = (second_reduce, second_spatial, second_expand)
    filled = [None] * 3
    lines = []
    if fast:
        batches = finish()
    else:
        finish_images(after[1])
        batches = []
        for b in range(blocks):
            for m in range(3):
                part = scatter(local[b][m])
                batches.append([(Scatter(part[None]), [((b, m), 0, part.shape[0])])])
    for n, sources in enumerate(batches):
        step_of(sources, n == len(batches) - 1)
    block_output, input_grad = images
    gradients = [filled[m][0] for m in range(3)]
    squares = [filled[m][1] for m in range(3)]
    updates = [filled[m][2] for m in range(3)]
    line = order(lines[-1], block_output, input_grad, norm_grads, norm_square, norm_new)
    stat = share(line, ALL)
    shapes = [(m.shape, F32) for m in masters]
    renewed = call(
        functools.partial(renew_kernel, blocks), shapes + [((1, 128), F32)], stat, *masters, *updates, name="renew"
    )
    layer_norms = renewed[3][0, : 6 * blocks].reshape(blocks, 3, 2)
    return (
        block_output,
        input_grad,
        *gradients,
        *squares,
        *renewed[:3],
        norm_grads,
        norm_square,
        norm_new,
        layer_norms,
    )


def solution(mesh):
    wide = mesh.shape["wide"]
    fine = Mesh(np.asarray(mesh.devices).reshape(2, 2, wide), ALL)
    narrow = ("x", "core")
    image = P("wide", None, None, narrow)
    matrix = P(None, "wide", narrow)
    row = P(None, None, narrow, None)
    return jax.shard_map(
        functools.partial(body, wide),
        mesh=fine,
        in_specs=(image,) * 2 + (matrix,) * 9 + (row,) * 3,
        out_specs=(image,) * 2 + (matrix,) * 9 + (row,) * 3 + (P(),),
        check_vma=False,
    )
```

```python
import functools

import jax
import jax.numpy as jnp
import numpy as np
from jax import lax
from jax.experimental import pallas as pl
from jax.experimental.pallas import tpu as pltpu
from jax.sharding import Mesh
from jax.sharding import PartitionSpec as P

STEP = 10
BN_EPS = 1e-05
FIRST_DECAY = 0.9
SECOND_DECAY = 0.999
ADAM_EPSILON = 1e-06
WEIGHT_DECAY = 0.01
MATRIX_RATE = 0.5
NORM_RATE = 0.3

ALL = ("x", "core", "wide")
CROSS = ("x", "wide")
BF = jnp.bfloat16
F32 = jnp.float32

SIDE = 14
LINE = 16
IMG = SIDE * LINE
NIMG = 2
ROWS = NIMG * IMG
SPAN = ROWS + LINE * (NIMG - 1)
PIECES = 8


def dot(a, b):
    return lax.dot_general(a, b, (((1,), (0,)), ((), ())), preferred_element_type=F32)


def dot_nt(a, b):
    return lax.dot_general(a, b, (((1,), (1,)), ((), ())), preferred_element_type=F32)


def dot_tn(a, b):
    return lax.dot_general(a, b, (((0,), (0,)), ((), ())), preferred_element_type=F32)


def lanes(parts):
    return jnp.concatenate(parts, axis=1)


def rows(parts):
    return jnp.concatenate(parts, axis=0)


def sigmoid(v):
    return 0.5 * jnp.tanh(0.5 * v) + 0.5


def silu(v):
    return v * sigmoid(v)


def silu_slope(v):
    s = sigmoid(v)
    return s * (1.0 + v * (1.0 - s))


def inside(shape):
    return (lax.broadcasted_iota(jnp.int32, shape, 0) & (LINE - 1)) < SIDE


def keep_inside(v):
    return jnp.where(inside(v.shape), v, 0.0)


def pack_rows(total, other):
    n = total.shape[1] // 128
    return rows([v[:, i * 128 : (i + 1) * 128] for v in (total, other) for i in range(n)])


def unpack_rows(block):
    n = block.shape[0] // 2
    return tuple(lanes([block[k * n + i : k * n + i + 1] for i in range(n)]) for k in range(2))


def column_sums(a, b):
    return pack_rows(jnp.sum(a, 0, keepdims=True), jnp.sum(b, 0, keepdims=True))


def mean_inverse(block, population):
    total, square = unpack_rows(block)
    mean = total / population
    return mean, lax.rsqrt(square / population - mean * mean + BN_EPS)


class Late:
    def __init__(self, buf, copy):
        self.buf = buf
        self.copy = copy
        self.shape = buf.shape
        self.waited = False
        copy.start()

    def wait(self):
        if not self.waited:
            self.copy.wait()
            self.waited = True

    def __getitem__(self, at):
        self.wait()
        return self.buf[at]


class Pair:
    def __init__(self, near, far):
        self.near = near
        self.far = far
        self.shape = near.shape

    def __getitem__(self, at):
        piece, rest = (at[0], at[1:]) if isinstance(at, tuple) else (at, ())
        inner = (piece & (PIECES - 1),) + rest
        return jnp.where(piece < PIECES, self.near[inner], self.far[inner])


def call(kernel, outs, *args, scratch=(), name=None, smem=(), limit=16, weight=None):
    vmem = pl.BlockSpec(memory_space=pltpu.VMEM)
    in_specs = [pl.BlockSpec(memory_space=pltpu.SMEM) if i in smem else vmem for i in range(len(args))]
    count = len(args)
    ins = list(args)
    scratch = list(scratch)
    cut = False
    if weight is not None:
        parts, (lo, hi) = weight
        ins += parts
        cut = parts[0].shape[1] != hi - lo
        in_specs += [pl.BlockSpec(memory_space=pl.ANY) if cut else vmem] * len(parts)
        if cut:
            scratch += [pltpu.VMEM((2 * PIECES, hi - lo, parts[0].shape[2]), BF), pltpu.SemaphoreType.DMA]
    total = len(ins)

    def whole(*refs):
        operands, results = refs[:count], refs[total:]
        if weight is None:
            return kernel(*operands, *results)
        held = refs[count:total]
        if not cut:
            return kernel(*operands, Pair(*held) if len(held) == 2 else held[0], *results)
        buf, sem = results[-2:]
        late = Late(buf, pltpu.make_async_copy(held[0].at[:, lo:hi], buf, sem))
        kernel(*operands, late, *results[:-2])
        late.wait()

    return pl.pallas_call(
        whole,
        out_shape=[jax.ShapeDtypeStruct(shape, dtype) for shape, dtype in outs],
        in_specs=in_specs,
        out_specs=[vmem] * len(outs),
        scratch_shapes=scratch,
        compiler_params=pltpu.CompilerParams(vmem_limit_bytes=limit * 1024 * 1024),
        name=name,
    )(*ins)


def place(ids, half, piece):
    return ids[4 + PIECES * half + piece]


def origin(ids, at):
    return ids[4 + 2 * PIECES + at]


def piece_of(ids, w, half, piece):
    return w[place(ids, half, piece)]


def expand_weights(ids, w, half):
    def piece(at):
        if w.shape[2] == 512:
            return w[at]
        depth = w.shape[1] // 4
        return lanes([w[at, i * depth : (i + 1) * depth] for i in range(4)])

    return rows([piece(place(ids, half, p)) for p in range(PIECES)])


def deal(ids, held, near, far):
    for start, dst in ((PIECES, far), (0, near)):
        for at in range(PIECES):
            dst[at] = held[origin(ids, start + at)]


def enter_kernel(ids, image_ref, grad_ref, keep_x, send_x, keep_g, send_g):
    x = ids[0]
    for src, keep, send in ((image_ref, keep_x, send_x), (grad_ref, keep_g, send_g)):
        for dst, owner in ((keep, x), (send, 1 - x)):
            for i in range(NIMG):
                img = src[owner * NIMG + i]
                pad = jnp.zeros((SIDE, LINE - SIDE, img.shape[2]), img.dtype)
                full = jnp.concatenate([img, pad], axis=1)
                dst[i * IMG : (i + 1) * IMG] = full.reshape(IMG, img.shape[2])


def join_kernel(ids, keep, recv, out):
    first = ids[0] == 0
    a = keep[...]
    b = recv[...]
    n = a.shape[1]
    out[:, :n] = jnp.where(first, a, b)
    out[:, n:] = jnp.where(first, b, a)


def params_kernel(ids, near_ref, far_ref, own_ref, oth_ref):
    first = ids[0] == 0
    for n, dst in ((0, own_ref), (1, oth_ref)):
        for lo, hi in ((0, 128), (128, 256), (256, 768)):
            a = near_ref[n, :, lo:hi]
            c = far_ref[n, :, lo:hi]
            dst[:, 2 * lo : lo + hi] = jnp.where(first, a, c)
            dst[:, lo + hi : 2 * hi] = jnp.where(first, c, a)


def centred(z, total, pixels):
    return keep_inside(z - total / pixels).astype(BF)


def reduce_kernel(ids, xo, xt, w, pre_out, centred_out, stat_out):
    core = ids[1]
    parts = []
    for c in (core, 1 - core):
        for k in range(2):
            for j in range(2):
                p = 2 * (2 * k + c) + j
                parts.append(lanes([piece_of(ids, w, 0, p), piece_of(ids, w, 1, p)]))
    pre = dot(lanes([xo[...], xt[...]]), rows(parts))
    total = jnp.sum(pre, 0, keepdims=True)
    stats = pack_rows(total, jnp.sum(pre * pre, 0, keepdims=True))
    pre_out[...] = pre
    centred_out[...] = centred(pre, total, NIMG * SIDE * SIDE)
    stat_out[...] = jnp.broadcast_to(stats[None], stat_out.shape)


def both_halves(ids, stat, pre, other, own_prm, oth_prm, lo, population, moments_out):
    x, core, wide = ids[0], ids[1], ids[2]
    own = stat[:, pl.ds(core, 1)]
    oth = stat[:, pl.ds(1 - core, 1)]
    own_sum = jnp.sum(own, axis=(0, 1, 2))
    oth_sum = jnp.sum(oth, axis=(0, 1, 2))
    local = stat[pl.ds(x, 1), pl.ds(1 - core, 1), pl.ds(wide, 1)].reshape(4, 128)
    mean, inverse = mean_inverse(own_sum, population)
    moments_out[...] = rows([mean, inverse, jnp.zeros((6, mean.shape[1]), F32)])
    hid_own = silu(own_prm[0:1, lo : lo + 256] * (pre[...] - mean) * inverse + own_prm[1:2, lo : lo + 256])
    mean_t, inverse_t = mean_inverse(oth_sum, population)
    local_mean = unpack_rows(local)[0] / (NIMG * SIDE * SIDE)
    hid_oth = silu(
        oth_prm[0:1, lo : lo + 256] * (other[...].astype(F32) + (local_mean - mean_t)) * inverse_t
        + oth_prm[1:2, lo : lo + 256]
    )
    hid_own = keep_inside(hid_own)
    hid_oth = keep_inside(hid_oth)
    first = core == 0
    parts = []
    for k in range(2):
        a = hid_own[:, k * 128 : (k + 1) * 128]
        b = hid_oth[:, k * 128 : (k + 1) * 128]
        parts += [jnp.where(first, a, b), jnp.where(first, b, a)]
    return lanes(parts)


def fill_shifts(dst, v, sign):
    for d in range(3):
        shifted = v if d == 1 else pltpu.roll(v, (sign * (d - 1)) % v.shape[0], 0)
        shifted = shifted.astype(BF)
        dst[d, 0:LINE] = jnp.zeros((LINE, v.shape[1]), BF)
        for i in range(NIMG):
            at = LINE + i * (IMG + LINE)
            dst[d, at : at + IMG] = shifted[i * IMG : (i + 1) * IMG]
            dst[d, at + IMG : at + IMG + LINE] = jnp.zeros((LINE, v.shape[1]), BF)


def squeeze(v):
    return rows([v[i * (IMG + LINE) : i * (IMG + LINE) + IMG] for i in range(NIMG)])


def tap_segments(tap, depth):
    lo, hi = tap * 512, (tap + 1) * 512
    found = []
    while lo < hi:
        piece = lo // depth
        end = min(hi, (piece + 1) * depth)
        found.append((piece, lo - piece * depth, end - piece * depth))
        lo = end
    return found


def tap_weights(ids, w, tap):
    return lanes(
        [
            rows([w[place(ids, h, p), a:b] for p, a, b in tap_segments(tap, w.shape[1])])
            for h in range(2)
        ]
    )


def spatial_kernel(
    population, ids, stat, pre, other, own_prm, oth_prm, w, hid_out, moments_out, pre_out, centred_out, stat_out, shifts
):
    hid = both_halves(ids, stat, pre, other, own_prm, oth_prm, 0, population, moments_out)
    fill_shifts(shifts, hid, -1)
    hid_out[...] = shifts[1, LINE : LINE + SPAN]
    acc = None
    for tap in range(9):
        at = (tap // 3) * LINE
        part = dot(shifts[tap % 3, at : at + SPAN], tap_weights(ids, w, tap))
        acc = part if acc is None else acc + part
    pre2 = keep_inside(squeeze(acc))
    total = jnp.sum(pre2, 0, keepdims=True)
    stats = pack_rows(total, jnp.sum(pre2 * pre2, 0, keepdims=True))
    pre_out[...] = pre2
    centred_out[...] = centred(pre2, total, NIMG * SIDE * SIDE)
    stat_out[...] = jnp.broadcast_to(stats[None], stat_out.shape)


def expand_kernel(population, ids, stat, pre, other, own_prm, oth_prm, w, hid_out, moments_out, pre_out, stat_out):
    hid = both_halves(ids, stat, pre, other, own_prm, oth_prm, 256, population, moments_out).astype(BF)
    hid_out[...] = hid
    total = []
    square = []
    for h in range(2):
        pre3 = dot(hid, expand_weights(ids, w, h))
        pre_out[:, h * 512 : (h + 1) * 512] = pre3
        total.append(jnp.sum(pre3, 0, keepdims=True))
        square.append(jnp.sum(pre3 * pre3, 0, keepdims=True))
    stats = pack_rows(lanes(total), lanes(square))
    stat_out[...] = jnp.broadcast_to(stats[None], stat_out.shape)


def close_kernel(population, stat, pre, stream, own_prm, moments_out, out, low_out):
    mean, inverse = mean_inverse(jnp.sum(stat[...], 0), population)
    moments_out[...] = rows([mean, inverse, jnp.zeros((6, mean.shape[1]), F32)])
    v = own_prm[0:1, 512:] * (pre[...] - mean) * inverse + own_prm[1:2, 512:] + stream[...].astype(F32)
    result = keep_inside(silu(v))
    out[...] = result
    low_out[...] = result.astype(BF)


def last_kernel(population, ids, stat, pre, stream, own_prm, keep_g, recv_g, moments_out, out, outside_out, stat_out):
    mean, inverse = mean_inverse(jnp.sum(stat[...], 0), population)
    moments_out[...] = rows([mean, inverse, jnp.zeros((6, mean.shape[1]), F32)])
    normed = (pre[...] - mean) * inverse
    v = own_prm[0:1, 512:] * normed + own_prm[1:2, 512:] + stream[...].astype(F32)
    s = sigmoid(v)
    out[...] = v * s
    first = ids[0] == 0
    a = keep_g[...]
    b = recv_g[...]
    grad = lanes([jnp.where(first, a, b), jnp.where(first, b, a)]).astype(F32)
    outside = keep_inside(grad * (s * (1.0 + v * (1.0 - s))))
    outside_out[...] = outside
    stat_out[...] = jnp.broadcast_to(column_sums(outside, outside * normed)[None], stat_out.shape)


def outer_back_kernel(moments, pre, stream, own_prm, outside_after, own_part, recv_part, outside_out, stat_out):
    mean = moments[0:1]
    inverse = moments[1:2]
    normed = (pre[...] - mean) * inverse
    v = own_prm[0:1, 512:] * normed + own_prm[1:2, 512:] + stream[...].astype(F32)
    upstream = outside_after[...] + own_part[...] + recv_part[...].astype(F32)
    outside = keep_inside(upstream * silu_slope(v))
    outside_out[...] = outside
    stat_out[...] = jnp.broadcast_to(column_sums(outside, outside * normed)[None], stat_out.shape)


def norm_back(sums, population, moments, pre, upstream, gain):
    shift_grad, gain_grad = unpack_rows(sums)
    mean = moments[0:1]
    inverse = moments[1:2]
    normed = (pre[...] - mean) * inverse
    lowered = gain * inverse * (upstream[...] - shift_grad / population - normed * (gain_grad / population))
    return keep_inside(lowered)


def split_cores(ids, parts, own_out, send_out):
    first = ids[1] == 0
    width = parts[0].shape[1]
    for k in range(2):
        a, b = parts[2 * k], parts[2 * k + 1]
        own_out[:, k * width : (k + 1) * width] = jnp.where(first, a, b)
        send_out[:, k * width : (k + 1) * width] = jnp.where(first, b, a).astype(BF)


def expand_back_kernel(population, ids, stat, moments, pre, outside, own_prm, w, low_out, own_out, send_out, sums_out):
    sums = jnp.sum(stat[...], 0)
    sums_out[...] = sums
    low = norm_back(sums, population, moments, pre, outside, own_prm[0:1, 512:]).astype(BF)
    low_out[...] = low
    acc = None
    for h in range(2):
        part = dot_nt(low[:, h * 512 : (h + 1) * 512], expand_weights(ids, w, h))
        acc = part if acc is None else acc + part
    split_cores(ids, [acc[:, n * 128 : (n + 1) * 128] for n in range(4)], own_out, send_out)


def expand_grad(ids, hid, low, held):
    grad = dot_tn(hid[...], low[...])
    lane_blocks = 512 // held.shape[2]
    depth = held.shape[1] // lane_blocks
    for h in range(2):
        for p in range(PIECES):
            piece = grad[p * depth : (p + 1) * depth, h * 512 : (h + 1) * 512].astype(BF)
            if lane_blocks == 1:
                held[h * PIECES + p] = piece
            else:
                for i in range(lane_blocks):
                    held[h * PIECES + p, i * depth : (i + 1) * depth] = piece[:, i * 128 : (i + 1) * 128]


def inner_back_kernel(lo, own_part, recv_part, moments, pre, own_prm, out, stat_out):
    normed = (pre[...] - moments[0:1]) * moments[1:2]
    v = own_prm[0:1, lo : lo + 256] * normed + own_prm[1:2, lo : lo + 256]
    upstream = (own_part[...] + recv_part[...].astype(F32)) * silu_slope(v)
    upstream = keep_inside(upstream)
    out[...] = upstream
    stat_out[...] = jnp.broadcast_to(column_sums(upstream, upstream * normed)[None], stat_out.shape)


def spatial_back_kernel(population, ids, stat, moments, pre, upstream, own_prm, w, shifts, own_out, send_out, sums_out):
    sums = jnp.sum(stat[:, pl.ds(ids[1], 1)], axis=(0, 1, 2))
    sums_out[...] = sums
    low = norm_back(sums, population, moments, pre, upstream, own_prm[0:1, 256:512])
    fill_shifts(shifts, low, 1)
    acc = None
    for tap in range(9):
        at = LINE * (2 - tap // 3)
        part = dot_nt(shifts[tap % 3, at : at + SPAN], tap_weights(ids, w, tap))
        acc = part if acc is None else acc + part
    acc = squeeze(acc)
    split_cores(ids, [acc[:, n * 128 : (n + 1) * 128] for n in range(4)], own_out, send_out)


def spatial_grad(ids, hid, shifts, held):
    turned = hid[...].T
    depth = held.shape[1]
    for tap in range(9):
        at = LINE * (2 - tap // 3)
        grad = dot(turned, shifts[tap % 3, at : at + SPAN]).astype(BF)
        row = 0
        for p, a, b in tap_segments(tap, depth):
            for h in range(2):
                held[h * PIECES + p, a:b] = grad[row : row + b - a, h * 128 : (h + 1) * 128]
            row += b - a


def reduce_back_kernel(population, ids, stat, moments, pre, upstream, own_prm, w, low_out, own_out, send_out, sums_out):
    sums = jnp.sum(stat[:, pl.ds(ids[1], 1)], axis=(0, 1, 2))
    sums_out[...] = sums
    low = norm_back(sums, population, moments, pre, upstream, own_prm[0:1, 0:256]).astype(BF)
    low_out[...] = low
    core = ids[1]
    for c, dst in ((1 - core, send_out), (core, own_out)):
        for k in range(2):
            for j in range(2):
                p = 2 * (2 * k + c) + j
                part = dot_nt(low, lanes([piece_of(ids, w, 0, p), piece_of(ids, w, 1, p)]))
                at = k * 512 + j * 256
                dst[:, at : at + 256] = part.astype(dst.dtype)


def reduce_grad(ids, xo, xt, low, held):
    core = ids[1]
    for c, src in ((core, xo), (1 - core, xt)):
        grad = dot_tn(src[...], low[...]).astype(BF)
        for k in range(2):
            for j in range(2):
                p = 2 * (2 * k + c) + j
                at = k * 512 + j * 256
                for h in range(2):
                    held[h * PIECES + p] = grad[at : at + 256, h * 128 : (h + 1) * 128]


def leave_kernel(ids, full, keep_out, send_out):
    first = ids[0] == 0
    a = full[:, :512]
    b = full[:, 512:]
    keep_out[...] = jnp.where(first, a, b)
    send_out[...] = jnp.where(first, b, a).astype(BF)


def leave_sum_kernel(ids, outside, own_part, recv_part, keep_out, send_out):
    first = ids[0] == 0
    full = outside[...] + own_part[...] + recv_part[...].astype(F32)
    a = full[:, :512]
    b = full[:, 512:]
    keep_out[...] = jnp.where(first, a, b)
    send_out[...] = jnp.where(first, b, a).astype(BF)


def arrive_kernel(ids, keep, recv, out):
    x = ids[0]
    for src, owner in ((keep, x), (recv, 1 - x)):
        for i in range(NIMG):
            img = src[i * IMG : (i + 1) * IMG].astype(F32).reshape(SIDE, LINE, src.shape[1])
            out[owner * NIMG + i] = img[:, :SIDE, :]


def moments_step(first, second, gradient):
    first_new = FIRST_DECAY * first + (1.0 - FIRST_DECAY) * gradient
    second_new = SECOND_DECAY * second + (1.0 - SECOND_DECAY) * gradient * gradient
    update = (first_new / (1.0 - FIRST_DECAY**STEP)) / (
        jnp.sqrt(second_new / (1.0 - SECOND_DECAY**STEP)) + ADAM_EPSILON
    )
    return second_new, update


def cell(v, lane):
    return jnp.where(lax.broadcasted_iota(jnp.int32, (1, 128), 1) == lane, jnp.sum(v), 0.0)


def lamb_kernel(plans, cuts, lines, arrays, *refs):
    blocks = iter(refs[:arrays])
    refs = refs[arrays:]
    count = sum(len(cut) for cut in cuts)
    masters, firsts, seconds = (refs[i * count : (i + 1) * count] for i in range(3))
    before = refs[3 * count : 3 * count + lines]
    outs = refs[len(refs) - 3 * count - 1 :]
    line = jnp.zeros((1, 128), F32)
    for ref in before:
        line = line + ref[...]
    i = 0
    for plan, cut in zip(plans, cuts):
        total = evaluate(plan, blocks)[0]
        for (b, m), lo, hi in cut:
            grad = total[lo:hi]
            master = masters[i][0]
            if grad.shape != master.shape:
                depth = master.shape[0]
                grad = lanes([grad[n * depth : (n + 1) * depth] for n in range(grad.shape[0] // depth)])
            second_new, update = moments_step(firsts[i][0], seconds[i][0], grad)
            update = update + WEIGHT_DECAY * master
            outs[3 * i][0] = grad
            outs[3 * i + 1][0] = second_new
            outs[3 * i + 2][0] = update
            line = line + cell(master * master, (b * 3 + m) * 2) + cell(update * update, (b * 3 + m) * 2 + 1)
            i += 1
    outs[-1][...] = jnp.broadcast_to(line[None], outs[-1].shape) if len(outs[-1].shape) == 3 else line


def lamb(sources, masters, firsts, seconds, filled, lines, count):
    whole = pl.BlockSpec(memory_space=pltpu.VMEM)
    tasks = [task for task, _ in sources]
    cuts = [cut for _, cut in sources]
    items = [item for cut in cuts for item, _, _ in cut]
    args, specs = slices(tasks, 1, 0)
    arrays = len(args)
    outs, out_specs, aliases = [], [], {}

    def one(b, m):
        return pl.BlockSpec((1,) + masters[m].shape[1:], lambda _: (b, 0, 0))

    for source in (masters, firsts, seconds):
        for b, m in items:
            args.append(source[m])
            specs.append(one(b, m))
    for line in lines:
        args.append(line)
        specs.append(whole)
    for b, m in items:
        for k in range(3):
            if filled[m] is not None:
                aliases[len(args)] = len(outs)
                args.append(filled[m][k])
                specs.append(pl.BlockSpec(memory_space=pl.ANY))
            outs.append(jax.ShapeDtypeStruct(masters[m].shape, F32))
            out_specs.append(one(b, m))
    outs.append(jax.ShapeDtypeStruct((count, 1, 128) if count else (1, 128), F32))
    out_specs.append(whole)
    found = pl.pallas_call(
        functools.partial(lamb_kernel, [task.plan() for task in tasks], cuts, len(lines), arrays),
        out_shape=outs,
        grid=(1,),
        in_specs=specs,
        out_specs=out_specs,
        input_output_aliases=aliases,
        compiler_params=pltpu.CompilerParams(vmem_limit_bytes=16 * 1024 * 1024),
        name="lamb",
    )(*args)
    for i, (b, m) in enumerate(items):
        filled[m] = tuple(found[3 * i : 3 * i + 3])
    return found[-1]


def renew_kernel(blocks, stat, *refs):
    masters, updates, outs, norms_out = refs[0:3], refs[3:6], refs[6:9], refs[9]
    norms = jnp.sqrt(jnp.sum(stat[...], 0))
    norms_out[...] = norms
    for b in range(blocks):
        for m in range(3):
            at = (b * 3 + m) * 2
            ratio = norms[:, at : at + 1] / norms[:, at + 1 : at + 2]
            outs[m][b] = masters[m][b] - MATRIX_RATE * ratio * updates[m][b]


def norm_kernel(blocks, ids, *refs):
    sums = refs[: 3 * blocks]
    params, first, second = refs[3 * blocks : 3 * blocks + 3]
    grads_out, square_out, new_out = refs[3 * blocks + 3 :]
    front = ids[0] == 0
    for b in range(blocks):
        parts = [[], []]
        for n in range(3):
            pair = unpack_rows(sums[3 * b + n][...])
            for kind in range(2):
                v = pair[1 - kind]
                half = v.shape[1] // 2
                parts[kind].append(jnp.where(front, v[:, :half], v[:, half:]))
        for kind in range(2):
            g = lanes(parts[kind])
            second_new, update = moments_step(first[b, kind], second[b, kind], g)
            grads_out[b, kind] = g
            square_out[b, kind] = second_new
            new_out[b, kind] = params[b, kind] - NORM_RATE * update


def exchange(step):
    pairs = []
    for i in range(32):
        core = (i >> 3) & 1
        pairs.append((i, i ^ (4, 2, 16 if core else 1, 1 if core else 16)[step]))
    return pairs


class Gather:
    def __init__(self, held):
        self.parts = (held,)

    def step(self, step, *after):
        if after:
            self.wait(*after)
        held = self.held()
        self.parts = (held, lax.ppermute(held, ALL, exchange(step)))

    def wait(self, *after):
        self.parts = order(self.parts, *after)

    def held(self):
        return self.parts[0] if len(self.parts) == 1 else jnp.concatenate(self.parts, 0)

    def last(self):
        return self.parts[-1]

    def weight(self):
        return list(self.parts), (0, self.parts[0].shape[1])


def order(value, *before):
    return lax.optimization_barrier((value, before))[0]


class Scatter:
    def __init__(self, near=None, far=None, parts=()):
        self.terms = [] if near is None else [near]
        self.far = far
        self.parts = parts

    def wait(self, *after):
        for part in self.parts:
            part.wait(*after)
        if self.terms:
            self.terms = list(order(tuple(self.terms), *after))

    def arrays(self):
        return [array for part in self.parts for array in part.arrays()] + self.terms

    def rows(self):
        return self.terms[0].shape[1] if self.terms else sum(part.rows() for part in self.parts)

    def plan(self):
        return [part.plan() for part in self.parts], len(self.terms)

    def send(self, step, value):
        self.terms.append(lax.ppermute(value, ALL, exchange(step)))


def evaluate(plan, refs):
    parts, count = plan
    found = [jnp.concatenate([evaluate(part, refs) for part in parts], axis=1)] if parts else []
    found += [next(refs)[...].astype(F32) for _ in range(count)]
    return functools.reduce(jnp.add, found)


def slices(tasks, size, at):
    arrays = [array for task in tasks for array in task.arrays()]
    return arrays, [pl.BlockSpec((size,) + array.shape[1:], lambda _: (at, 0, 0)) for array in arrays]


def add_up_kernel(plans, *refs):
    blocks = iter(refs[: len(refs) - len(plans)])
    for plan, out in zip(plans, refs[len(refs) - len(plans) :]):
        out[...] = evaluate(plan, blocks).astype(out.dtype)


def advance_sums(steps, *after):
    arrays, specs, outs, plans = [], [], [], []
    for task, step in steps:
        task.wait(*after)
    for task, step in steps:
        size = 1 << step
        more, blocks = slices([task], size, 1)
        arrays += more
        specs += blocks
        outs.append(jax.ShapeDtypeStruct((size, task.rows(), 128), BF))
        plans.append(task.plan())
    sends = pl.pallas_call(
        functools.partial(add_up_kernel, plans),
        out_shape=outs,
        grid=(1,),
        in_specs=specs,
        out_specs=[pl.BlockSpec(memory_space=pltpu.VMEM)] * len(outs),
        compiler_params=pltpu.CompilerParams(vmem_limit_bytes=16 * 1024 * 1024),
        name="add_up",
    )(*arrays)
    for (task, step), value in zip(steps, sends):
        task.send(step, value)
    return sends


def body(
    wide,
    block_input,
    out_grad,
    conv_reduce,
    conv_spatial,
    conv_expand,
    first_reduce,
    first_spatial,
    first_expand,
    second_reduce,
    second_spatial,
    second_expand,
    norm_params,
    norm_first,
    norm_second,
):
    blocks = conv_reduce.shape[0]
    population = float(block_input.shape[0] * SIDE * SIDE * wide)
    count = 4 * wide
    x = lax.axis_index("x").astype(jnp.int32)
    core = lax.axis_index("core").astype(jnp.int32)
    w = lax.axis_index("wide").astype(jnp.int32)
    fast = wide == PIECES
    here = jnp.stack([x, core, w, jnp.zeros((), jnp.int32)])
    count_up = jnp.arange(2 * PIECES, dtype=jnp.int32)
    ids = jnp.concatenate([here, count_up, count_up])
    to_x = count_up // PIECES
    to_w = count_up % PIECES

    apart_x = to_x ^ x
    apart_w = to_w ^ w
    back = jnp.where(core == 0, apart_w & 1, apart_x)
    front = jnp.where(core == 0, apart_x, apart_w & 1)
    places = front * 8 + back * 4 + ((apart_w & 2) | (apart_w >> 2))
    bit3, bit2 = count_up >> 3, (count_up >> 2) & 1
    from_x = x ^ jnp.where(core == 0, bit3, bit2)
    from_w = w ^ (jnp.where(core == 0, bit2, bit3) | (count_up & 2) | ((count_up & 1) << 2))
    relative = jnp.concatenate([here, places, from_x * PIECES + from_w])

    swap = [(0, 1), (1, 0)]

    def over_core(v):
        return lax.ppermute(v, "core", swap)

    def over_x(v):
        return lax.ppermute(v, "x", swap)

    def share(v, axes):
        return lax.all_to_all(v, axes, 0, 0)

    def run(kernel, outs, *args, places=None, **kw):
        return call(kernel, outs, ids if places is None else places, *args, smem=(0,), **kw)

    wide_row = norm_params.shape[-1]
    near = norm_params.reshape(2 * blocks, wide_row)
    both = jnp.stack([near, over_core(near)])
    far = over_x(both)
    own_all, oth_all = run(
        params_kernel, [((2 * blocks, 2 * wide_row), F32)] * 2, both, far, name="norm_rows"
    )
    own_prm = [own_all[2 * b : 2 * b + 2] for b in range(blocks)]
    oth_prm = [oth_all[2 * b : 2 * b + 2] for b in range(blocks)]

    act = (ROWS, 512)
    keep_x, send_x, keep_g, send_g = run(enter_kernel, [(act, BF)] * 4, block_input, out_grad, name="enter")
    recv_x = over_x(send_x)
    low_stream = stream = run(join_kernel, [((ROWS, 1024), BF)], keep_x, recv_x, name="join")[0]

    def gather(shard, columns):
        whole = lax.all_gather(shard.astype(BF), CROSS, axis=0, tiled=True).reshape(2 * PIECES, -1, columns)
        return [whole], (0, whole.shape[1])

    table = relative if fast else ids
    tables = [table] + [ids] * (blocks - 1)
    gathers = []
    weights = None
    if fast:
        depth = conv_expand.shape[1]

        def shards(b):
            blocked = conv_expand[b].astype(BF).reshape(depth, 4, 128).swapaxes(0, 1).reshape(4 * depth, 128)
            return [conv_reduce[b].astype(BF), conv_spatial[b].astype(BF), blocked]

        gathers = [Gather(shard[None]) for shard in shards(0)]
        gathers[0].step(0, send_x)
        gathers[0].step(1)
        gathers[1].step(0, gathers[0].parts[0])
        gathers[0].step(2, recv_x, far)
        gathers[1].step(1, gathers[0].parts[0])
        gathers[2].step(0, gathers[1].parts[0])
        gathers[2].step(1)
        gathers[0].step(3)
        wholes = [lax.all_gather(jnp.concatenate(shards(b)), CROSS, axis=0, tiled=False) for b in range(1, blocks)]
        one = conv_reduce.shape[1]
        two = one + conv_spatial.shape[1]
        cuts = ((0, one), (one, two), (two, two + 4 * depth))
    else:
        weights = [
            (gather(conv_reduce[b], 128), gather(conv_spatial[b], 128), gather(conv_expand[b], 512)) for b in range(blocks)
        ]

    def weight_of(b, m):
        if not fast:
            return weights[b][m]
        return gathers[m].weight() if b == 0 else ([wholes[b - 1]], cuts[m])

    def advance(stage, stat, out):
        if not fast:
            return
        if stage == 1:
            gathers[1].step(2, out)
            gathers[1].step(3, stat)
        elif stage == 2:
            gathers[2].step(2, gathers[1].last())
            gathers[2].step(3, out)

    inner = (count, 4, 128)
    outer = (2 * wide, 16, 128)
    saved = []
    for b in range(blocks):
        other = over_core(low_stream)
        pre1, low1, stat = run(
            reduce_kernel,
            [((ROWS, 256), F32), ((ROWS, 256), BF), (inner, F32)],
            low_stream,
            other,
            weight=weight_of(b, 0),
            places=tables[b],
            name="reduce",
        )
        low1 = over_core(low1)
        stat = share(stat, ALL)
        advance(3 * b + 1, stat, pre1)
        stat = stat.reshape(2, 2, wide, 4, 128)
        hid1, moments1, pre2, low2, stat = run(
            functools.partial(spatial_kernel, population),
            [((SPAN, 512), BF), ((8, 256), F32), ((ROWS, 256), F32), ((ROWS, 256), BF), (inner, F32)],
            stat,
            pre1,
            low1,
            own_prm[b],
            oth_prm[b],
            weight=weight_of(b, 1),
            scratch=[pltpu.VMEM((3, SPAN + 2 * LINE, 512), BF)],
            places=tables[b],
            name="spatial",
        )
        low2 = over_core(low2)
        if b > 0:
            stat = order(stat, low2)
        stat = share(stat, ALL)
        advance(3 * b + 2, stat, pre2)
        if fast and b == 0:
            stat, *wholes = lax.optimization_barrier((stat, *wholes))
        stat = stat.reshape(2, 2, wide, 4, 128)
        before = stat
        hid2, moments2, pre3, stat = run(
            functools.partial(expand_kernel, population),
            [((ROWS, 512), BF), ((8, 256), F32), ((ROWS, 1024), F32), (outer, F32)],
            stat,
            pre2,
            low2,
            own_prm[b],
            oth_prm[b],
            weight=weight_of(b, 2),
            places=tables[b],
            name="expand",
        )
        if b == blocks - 1:
            recv_g = over_x(order(send_g, before))
        stat = share(stat, CROSS)
        advance(3 * b + 3, stat, pre3)
        item = dict(
            xo=low_stream, xt=other, stream=stream, pre1=pre1, hid1=hid1, m1=moments1, pre2=pre2, hid2=hid2, m2=moments2, pre3=pre3
        )
        if b < blocks - 1:
            item["m3"], stream, low_stream = call(
                functools.partial(close_kernel, population),
                [((8, 1024), F32), ((ROWS, 1024), F32), ((ROWS, 1024), BF)],
                stat,
                pre3,
                stream,
                own_prm[b],
                name="close",
            )
        else:
            item["m3"], result, outside, stat = run(
                functools.partial(last_kernel, population),
                [((8, 1024), F32), ((ROWS, 1024), F32), ((ROWS, 1024), F32), (outer, F32)],
                stat,
                pre3,
                stream,
                own_prm[b],
                keep_g,
                recv_g,
                name="last",
            )
        saved.append(item)

    tasks = {}

    def hook(kind, b, grads):
        if not fast:
            return []
        near, far = grads
        tasks[kind, b] = Scatter(near, far)
        if (kind, b) != ("reduce", 1):
            tasks[kind, b].send(3, far)
        return [far]

    def ahead(kind, b, stat):
        if not fast:
            return stat
        steps = []
        if b == 1 and kind == "spatial":
            stat = order(stat, tasks["expand", 1].terms[-1])
        if b == 0 and kind == "reduce":
            stat = order(stat, *(tasks[name].terms[-1] for name in ("big", ("expand", 0), ("reduce", 1))))
        if b == 1 and kind == "reduce":
            tasks["big"] = Scatter(parts=(tasks["expand", 1], tasks["spatial", 1]))
            steps = [(tasks["big"], 2)]
        if b == 0 and kind == "expand":
            tasks["reduce", 1].send(3, order(tasks["reduce", 1].far, stat))
            steps = [(tasks["big"], 1)]
        if b == 0 and kind == "spatial":
            steps = [(tasks["expand", 0], 2), (tasks["reduce", 1], 2), (tasks["big"], 0)]
        if b == 0 and kind == "reduce":
            steps = [(tasks["spatial", 0], 2)]
        return order(stat, *advance_sums(steps, stat)) if steps else stat

    def whole(task, b, m):
        return task, [((b, m), 0, task.rows())]

    def step_of(sources, last=False):
        line = lamb(sources, masters, firsts, seconds, filled, lines if last else [], count if last else 0)
        lines.append(line)
        return line

    images = []

    def finish_images(full, gate, kernel, name):
        keep, send = run(kernel, [(act, F32), (act, BF)], *order(full, gate), name=name)
        images.extend(run(arrive_kernel, [(block_input.shape, F32)], keep, over_x(send), name="arrive"))
        return send

    def finish():
        small, middle, large = (tasks[kind, 0] for kind in ("expand", "reduce", "spatial"))
        advance_sums([(small, 1), (tasks["reduce", 1], 1)], middle.terms[0])
        leaving = finish_images((result,), middle.terms[0], leave_kernel, "leave")
        big = tasks["big"]
        cut = 4 * conv_expand.shape[1]
        sent = advance_sums([(large, 1)], small.terms[-1], tasks["reduce", 1].terms[-1], leaving)
        rest = Scatter(parts=(small, tasks["reduce", 1]))
        sent = advance_sums([(middle, 2), (rest, 0)], sent)
        finish_images(after, sent[0], leave_sum_kernel, "leave_sum")
        line = step_of([(big, [((1, 2), 0, cut), ((1, 1), cut, big.rows())])])
        sent = advance_sums([(middle, 1)], sent, line, norm_grads)
        sent = advance_sums([(large, 0)], sent, rest.terms[-1])
        advance_sums([(middle, 0)], sent)
        line = step_of([(rest, [((0, 2), 0, cut), ((1, 0), cut, rest.rows())])])
        for task in (large, middle):
            task.wait(line, *images)
        return [[whole(large, 0, 1), whole(middle, 0, 0)]]

    def gradient(b, m, kernel, *args, name):
        parts, (lo, hi) = weight_of(b, m)
        shape = (hi - lo, parts[0].shape[2])
        whole = pltpu.VMEM((2 * PIECES,) + shape, BF)
        half = ((PIECES,) + shape, BF)

        def halves(ids, *refs):
            kernel(ids, *refs[:-3], refs[-1])
            deal(ids, refs[-1], refs[-3], refs[-2])

        return run(halves, [half] * 2, *args, scratch=[whole], places=table, name=name)

    sums = [None] * (3 * blocks)
    local = [None] * blocks
    after = None
    for b in reversed(range(blocks)):
        item = saved[b]
        w_reduce, w_spatial, w_expand = (weight_of(b, m) for m in range(3))
        if after is not None:
            outside, stat = call(
                outer_back_kernel,
                [((ROWS, 1024), F32), (outer, F32)],
                item["m3"],
                item["pre3"],
                item["stream"],
                own_prm[b],
                *after,
                name="outer_back",
            )
        stat = ahead("expand", b, share(stat, CROSS))
        low3, own_part, send, sums[3 * b + 2] = run(
            functools.partial(expand_back_kernel, population),
            [((ROWS, 1024), BF), ((ROWS, 256), F32), ((ROWS, 256), BF), ((16, 128), F32)],
            stat,
            item["m3"],
            item["pre3"],
            outside,
            own_prm[b],
            weight=w_expand,
            places=tables[b],
            name="expand_back",
        )
        recv = over_core(send)
        grad_expand = gradient(b, 2, expand_grad, item["hid2"], low3, name="expand_grad")
        own_part = order(own_part, *grad_expand, *hook("expand", b, grad_expand))
        upstream, stat = call(
            functools.partial(inner_back_kernel, 256),
            [((ROWS, 256), F32), (inner, F32)],
            own_part,
            recv,
            item["m2"],
            item["pre2"],
            own_prm[b],
            name="inner_back",
        )
        stat = ahead("spatial", b, share(stat, ALL)).reshape(2, 2, wide, 4, 128)
        shifts, own_part, send, sums[3 * b + 1] = run(
            functools.partial(spatial_back_kernel, population),
            [((3, SPAN + 2 * LINE, 256), BF), ((ROWS, 256), F32), ((ROWS, 256), BF), ((4, 128), F32)],
            stat,
            item["m2"],
            item["pre2"],
            upstream,
            own_prm[b],
            weight=w_spatial,
            places=tables[b],
            name="spatial_back",
        )
        recv = over_core(send)
        grad_spatial = gradient(b, 1, spatial_grad, item["hid1"], shifts, name="spatial_grad")
        own_part = order(own_part, *grad_spatial, *hook("spatial", b, grad_spatial))
        upstream, stat = call(
            functools.partial(inner_back_kernel, 0),
            [((ROWS, 256), F32), (inner, F32)],
            own_part,
            recv,
            item["m1"],
            item["pre1"],
            own_prm[b],
            name="inner_back",
        )
        stat = ahead("reduce", b, share(stat, ALL)).reshape(2, 2, wide, 4, 128)
        low1, own_part, send, sums[3 * b] = run(
            functools.partial(reduce_back_kernel, population),
            [((ROWS, 256), BF), ((ROWS, 1024), F32), ((ROWS, 1024), BF), ((4, 128), F32)],
            stat,
            item["m1"],
            item["pre1"],
            upstream,
            own_prm[b],
            weight=w_reduce,
            places=tables[b],
            name="reduce_back",
        )
        recv = over_core(send)
        grad_reduce = gradient(b, 0, reduce_grad, item["xo"], item["xt"], low1, name="reduce_grad")
        own_part = order(own_part, *grad_reduce, *hook("reduce", b, grad_reduce))
        after = (outside, own_part, recv)
        local[b] = (grad_reduce, grad_spatial, grad_expand)

    def scatter(pair):
        flat = jnp.concatenate(pair).reshape(-1, pair[0].shape[-1])
        return lax.psum_scatter(flat, CROSS, scatter_dimension=0, tiled=True).astype(F32)

    norm_shape = (norm_params.shape, F32)
    norm_grads, norm_square, norm_new = run(
        functools.partial(norm_kernel, blocks), [norm_shape] * 3, *sums, norm_params, norm_first, norm_second, name="norms"
    )
    masters = (conv_reduce, conv_spatial, conv_expand)
    firsts = (first_reduce, first_spatial, first_expand)
    seconds = (second_reduce, second_spatial, second_expand)
    filled = [None] * 3
    lines = []
    if fast:
        batches = finish()
    else:
        finish_images((result,), after[1], leave_kernel, "leave")
        finish_images(after, after[1], leave_sum_kernel, "leave_sum")
        batches = []
        for b in range(blocks):
            for m in range(3):
                part = scatter(local[b][m])
                batches.append([(Scatter(part[None]), [((b, m), 0, part.shape[0])])])
    for n, sources in enumerate(batches):
        step_of(sources, n == len(batches) - 1)
    block_output, input_grad = images
    gradients = [filled[m][0] for m in range(3)]
    squares = [filled[m][1] for m in range(3)]
    updates = [filled[m][2] for m in range(3)]
    line = order(lines[-1], block_output, input_grad, norm_grads, norm_square, norm_new)
    stat = share(line, ALL)
    shapes = [(m.shape, F32) for m in masters]
    renewed = call(
        functools.partial(renew_kernel, blocks), shapes + [((1, 128), F32)], stat, *masters, *updates, name="renew"
    )
    layer_norms = renewed[3][0, : 6 * blocks].reshape(blocks, 3, 2)
    return (
        block_output,
        input_grad,
        *gradients,
        *squares,
        *renewed[:3],
        norm_grads,
        norm_square,
        norm_new,
        layer_norms,
    )


def solution(mesh):
    wide = mesh.shape["wide"]
    fine = Mesh(np.asarray(mesh.devices).reshape(2, 2, wide), ALL)
    narrow = ("x", "core")
    image = P("wide", None, None, narrow)
    matrix = P(None, "wide", narrow)
    row = P(None, None, narrow, None)
    return jax.shard_map(
        functools.partial(body, wide),
        mesh=fine,
        in_specs=(image,) * 2 + (matrix,) * 9 + (row,) * 3,
        out_specs=(image,) * 2 + (matrix,) * 9 + (row,) * 3 + (P(),),
        check_vma=False,
    )
```

```python
import functools

import jax
import jax.numpy as jnp
import numpy as np
from jax import lax
from jax.experimental import pallas as pl
from jax.experimental.pallas import tpu as pltpu
from jax.sharding import Mesh
from jax.sharding import PartitionSpec as P

STEP = 10
BN_EPS = 1e-05
FIRST_DECAY = 0.9
SECOND_DECAY = 0.999
ADAM_EPSILON = 1e-06
WEIGHT_DECAY = 0.01
MATRIX_RATE = 0.5
NORM_RATE = 0.3

ALL = ("x", "core", "wide")
CROSS = ("x", "wide")
BF = jnp.bfloat16
F32 = jnp.float32

SIDE = 14
LINE = 16
IMG = SIDE * LINE
NIMG = 2
ROWS = NIMG * IMG
SPAN = ROWS + LINE * (NIMG - 1)
PIECES = 8


def dot(a, b):
    return lax.dot_general(a, b, (((1,), (0,)), ((), ())), preferred_element_type=F32)


def dot_nt(a, b):
    return lax.dot_general(a, b, (((1,), (1,)), ((), ())), preferred_element_type=F32)


def dot_tn(a, b):
    return lax.dot_general(a, b, (((0,), (0,)), ((), ())), preferred_element_type=F32)


def lanes(parts):
    return jnp.concatenate(parts, axis=1)


def rows(parts):
    return jnp.concatenate(parts, axis=0)


def sigmoid(v):
    return 0.5 * jnp.tanh(0.5 * v) + 0.5


def silu(v):
    return v * sigmoid(v)


def silu_slope(v):
    s = sigmoid(v)
    return s * (1.0 + v * (1.0 - s))


def inside(shape):
    return (lax.broadcasted_iota(jnp.int32, shape, 0) & (LINE - 1)) < SIDE


def keep_inside(v):
    return jnp.where(inside(v.shape), v, 0.0)


def pack_rows(total, other):
    n = total.shape[1] // 128
    return rows([v[:, i * 128 : (i + 1) * 128] for v in (total, other) for i in range(n)])


def unpack_rows(block):
    n = block.shape[0] // 2
    return tuple(lanes([block[k * n + i : k * n + i + 1] for i in range(n)]) for k in range(2))


def column_sums(a, b):
    return pack_rows(jnp.sum(a, 0, keepdims=True), jnp.sum(b, 0, keepdims=True))


def mean_inverse(block, population):
    total, square = unpack_rows(block)
    mean = total / population
    return mean, lax.rsqrt(square / population - mean * mean + BN_EPS)


class Late:
    def __init__(self, buf, copy):
        self.buf = buf
        self.copy = copy
        self.shape = buf.shape
        self.waited = False
        copy.start()

    def wait(self):
        if not self.waited:
            self.copy.wait()
            self.waited = True

    def __getitem__(self, at):
        self.wait()
        return self.buf[at]


class Pair:
    def __init__(self, near, far):
        self.near = near
        self.far = far
        self.shape = near.shape

    def __getitem__(self, at):
        piece, rest = (at[0], at[1:]) if isinstance(at, tuple) else (at, ())
        inner = (piece & (PIECES - 1),) + rest
        return jnp.where(piece < PIECES, self.near[inner], self.far[inner])


def call(kernel, outs, *args, scratch=(), name=None, smem=(), limit=16, weight=None):
    vmem = pl.BlockSpec(memory_space=pltpu.VMEM)
    in_specs = [pl.BlockSpec(memory_space=pltpu.SMEM) if i in smem else vmem for i in range(len(args))]
    count = len(args)
    ins = list(args)
    scratch = list(scratch)
    cut = False
    if weight is not None:
        parts, (lo, hi) = weight
        ins += parts
        cut = parts[0].shape[1] != hi - lo
        in_specs += [pl.BlockSpec(memory_space=pl.ANY) if cut else vmem] * len(parts)
        if cut:
            scratch += [pltpu.VMEM((2 * PIECES, hi - lo, parts[0].shape[2]), BF), pltpu.SemaphoreType.DMA]
    total = len(ins)

    def whole(*refs):
        operands, results = refs[:count], refs[total:]
        if weight is None:
            return kernel(*operands, *results)
        held = refs[count:total]
        if not cut:
            return kernel(*operands, Pair(*held) if len(held) == 2 else held[0], *results)
        buf, sem = results[-2:]
        late = Late(buf, pltpu.make_async_copy(held[0].at[:, lo:hi], buf, sem))
        kernel(*operands, late, *results[:-2])
        late.wait()

    return pl.pallas_call(
        whole,
        out_shape=[jax.ShapeDtypeStruct(shape, dtype) for shape, dtype in outs],
        in_specs=in_specs,
        out_specs=[vmem] * len(outs),
        scratch_shapes=scratch,
        compiler_params=pltpu.CompilerParams(vmem_limit_bytes=limit * 1024 * 1024),
        name=name,
    )(*ins)


def place(ids, half, piece):
    return ids[4 + PIECES * half + piece]


def origin(ids, at):
    return ids[4 + 2 * PIECES + at]


def piece_of(ids, w, half, piece):
    return w[place(ids, half, piece)]


def expand_weights(ids, w, half):
    def piece(at):
        if w.shape[2] == 512:
            return w[at]
        depth = w.shape[1] // 4
        return lanes([w[at, i * depth : (i + 1) * depth] for i in range(4)])

    return rows([piece(place(ids, half, p)) for p in range(PIECES)])


def deal(ids, held, near, far):
    for start, dst in ((PIECES, far), (0, near)):
        for at in range(PIECES):
            dst[at] = held[origin(ids, start + at)]


def enter_kernel(ids, image_ref, grad_ref, keep_x, send_x, keep_g, send_g):
    x = ids[0]
    for src, keep, send in ((image_ref, keep_x, send_x), (grad_ref, keep_g, send_g)):
        for dst, owner in ((keep, x), (send, 1 - x)):
            for i in range(NIMG):
                img = src[owner * NIMG + i]
                pad = jnp.zeros((SIDE, LINE - SIDE, img.shape[2]), img.dtype)
                full = jnp.concatenate([img, pad], axis=1)
                dst[i * IMG : (i + 1) * IMG] = full.reshape(IMG, img.shape[2])


def join_kernel(ids, keep, recv, out):
    first = ids[0] == 0
    a = keep[...]
    b = recv[...]
    n = a.shape[1]
    out[:, :n] = jnp.where(first, a, b)
    out[:, n:] = jnp.where(first, b, a)


def params_kernel(ids, near_ref, far_ref, own_ref, oth_ref):
    first = ids[0] == 0
    for n, dst in ((0, own_ref), (1, oth_ref)):
        for lo, hi in ((0, 128), (128, 256), (256, 768)):
            a = near_ref[n, :, lo:hi]
            c = far_ref[n, :, lo:hi]
            dst[:, 2 * lo : lo + hi] = jnp.where(first, a, c)
            dst[:, lo + hi : 2 * hi] = jnp.where(first, c, a)


def centred(z, total, pixels):
    return keep_inside(z - total / pixels).astype(BF)


def reduce_kernel(ids, xo, xt, w, pre_out, centred_out, stat_out):
    core = ids[1]
    parts = []
    for c in (core, 1 - core):
        for k in range(2):
            for j in range(2):
                p = 2 * (2 * k + c) + j
                parts.append(lanes([piece_of(ids, w, 0, p), piece_of(ids, w, 1, p)]))
    pre = dot(lanes([xo[...], xt[...]]), rows(parts))
    total = jnp.sum(pre, 0, keepdims=True)
    stats = pack_rows(total, jnp.sum(pre * pre, 0, keepdims=True))
    pre_out[...] = pre
    centred_out[...] = centred(pre, total, NIMG * SIDE * SIDE)
    stat_out[...] = jnp.broadcast_to(stats[None], stat_out.shape)


def both_halves(ids, stat, pre, other, own_prm, oth_prm, lo, population, moments_out):
    x, core, wide = ids[0], ids[1], ids[2]
    own = stat[:, pl.ds(core, 1)]
    oth = stat[:, pl.ds(1 - core, 1)]
    own_sum = jnp.sum(own, axis=(0, 1, 2))
    oth_sum = jnp.sum(oth, axis=(0, 1, 2))
    local = stat[pl.ds(x, 1), pl.ds(1 - core, 1), pl.ds(wide, 1)].reshape(4, 128)
    mean, inverse = mean_inverse(own_sum, population)
    moments_out[...] = rows([mean, inverse, jnp.zeros((6, mean.shape[1]), F32)])
    hid_own = silu(own_prm[0:1, lo : lo + 256] * (pre[...] - mean) * inverse + own_prm[1:2, lo : lo + 256])
    mean_t, inverse_t = mean_inverse(oth_sum, population)
    local_mean = unpack_rows(local)[0] / (NIMG * SIDE * SIDE)
    hid_oth = silu(
        oth_prm[0:1, lo : lo + 256] * (other[...].astype(F32) + (local_mean - mean_t)) * inverse_t
        + oth_prm[1:2, lo : lo + 256]
    )
    hid_own = keep_inside(hid_own)
    hid_oth = keep_inside(hid_oth)
    first = core == 0
    parts = []
    for k in range(2):
        a = hid_own[:, k * 128 : (k + 1) * 128]
        b = hid_oth[:, k * 128 : (k + 1) * 128]
        parts += [jnp.where(first, a, b), jnp.where(first, b, a)]
    return lanes(parts)


def fill_shifts(dst, v, sign):
    for d in range(3):
        shifted = v if d == 1 else pltpu.roll(v, (sign * (d - 1)) % v.shape[0], 0)
        shifted = shifted.astype(BF)
        dst[d, 0:LINE] = jnp.zeros((LINE, v.shape[1]), BF)
        for i in range(NIMG):
            at = LINE + i * (IMG + LINE)
            dst[d, at : at + IMG] = shifted[i * IMG : (i + 1) * IMG]
            dst[d, at + IMG : at + IMG + LINE] = jnp.zeros((LINE, v.shape[1]), BF)


def squeeze(v):
    return rows([v[i * (IMG + LINE) : i * (IMG + LINE) + IMG] for i in range(NIMG)])


def tap_segments(tap, depth):
    lo, hi = tap * 512, (tap + 1) * 512
    found = []
    while lo < hi:
        piece = lo // depth
        end = min(hi, (piece + 1) * depth)
        found.append((piece, lo - piece * depth, end - piece * depth))
        lo = end
    return found


def tap_weights(ids, w, tap):
    return lanes(
        [
            rows([w[place(ids, h, p), a:b] for p, a, b in tap_segments(tap, w.shape[1])])
            for h in range(2)
        ]
    )


def spatial_kernel(
    population, ids, stat, pre, other, own_prm, oth_prm, w, hid_out, moments_out, pre_out, centred_out, stat_out, shifts
):
    hid = both_halves(ids, stat, pre, other, own_prm, oth_prm, 0, population, moments_out)
    fill_shifts(shifts, hid, -1)
    hid_out[...] = shifts[1, LINE : LINE + SPAN]
    acc = None
    for tap in range(9):
        at = (tap // 3) * LINE
        part = dot(shifts[tap % 3, at : at + SPAN], tap_weights(ids, w, tap))
        acc = part if acc is None else acc + part
    pre2 = keep_inside(squeeze(acc))
    total = jnp.sum(pre2, 0, keepdims=True)
    stats = pack_rows(total, jnp.sum(pre2 * pre2, 0, keepdims=True))
    pre_out[...] = pre2
    centred_out[...] = centred(pre2, total, NIMG * SIDE * SIDE)
    stat_out[...] = jnp.broadcast_to(stats[None], stat_out.shape)


def expand_kernel(population, ids, stat, pre, other, own_prm, oth_prm, w, hid_out, moments_out, pre_out, stat_out):
    hid = both_halves(ids, stat, pre, other, own_prm, oth_prm, 256, population, moments_out).astype(BF)
    hid_out[...] = hid
    total = []
    square = []
    for h in range(2):
        pre3 = dot(hid, expand_weights(ids, w, h))
        pre_out[:, h * 512 : (h + 1) * 512] = pre3
        total.append(jnp.sum(pre3, 0, keepdims=True))
        square.append(jnp.sum(pre3 * pre3, 0, keepdims=True))
    stats = pack_rows(lanes(total), lanes(square))
    stat_out[...] = jnp.broadcast_to(stats[None], stat_out.shape)


def close_kernel(population, stat, pre, stream, own_prm, moments_out, out, low_out):
    mean, inverse = mean_inverse(jnp.sum(stat[...], 0), population)
    moments_out[...] = rows([mean, inverse, jnp.zeros((6, mean.shape[1]), F32)])
    v = own_prm[0:1, 512:] * (pre[...] - mean) * inverse + own_prm[1:2, 512:] + stream[...].astype(F32)
    result = keep_inside(silu(v))
    out[...] = result
    low_out[...] = result.astype(BF)


def last_kernel(population, ids, stat, pre, stream, own_prm, keep_g, recv_g, moments_out, out, outside_out, stat_out):
    mean, inverse = mean_inverse(jnp.sum(stat[...], 0), population)
    moments_out[...] = rows([mean, inverse, jnp.zeros((6, mean.shape[1]), F32)])
    normed = (pre[...] - mean) * inverse
    v = own_prm[0:1, 512:] * normed + own_prm[1:2, 512:] + stream[...].astype(F32)
    s = sigmoid(v)
    out[...] = v * s
    first = ids[0] == 0
    a = keep_g[...]
    b = recv_g[...]
    grad = lanes([jnp.where(first, a, b), jnp.where(first, b, a)]).astype(F32)
    outside = keep_inside(grad * (s * (1.0 + v * (1.0 - s))))
    outside_out[...] = outside
    stat_out[...] = jnp.broadcast_to(column_sums(outside, outside * normed)[None], stat_out.shape)


def outer_back_kernel(moments, pre, stream, own_prm, outside_after, own_part, recv_part, outside_out, stat_out):
    mean = moments[0:1]
    inverse = moments[1:2]
    normed = (pre[...] - mean) * inverse
    v = own_prm[0:1, 512:] * normed + own_prm[1:2, 512:] + stream[...].astype(F32)
    upstream = outside_after[...] + own_part[...] + recv_part[...].astype(F32)
    outside = keep_inside(upstream * silu_slope(v))
    outside_out[...] = outside
    stat_out[...] = jnp.broadcast_to(column_sums(outside, outside * normed)[None], stat_out.shape)


def norm_back(sums, population, moments, pre, upstream, gain):
    shift_grad, gain_grad = unpack_rows(sums)
    mean = moments[0:1]
    inverse = moments[1:2]
    normed = (pre[...] - mean) * inverse
    lowered = gain * inverse * (upstream[...] - shift_grad / population - normed * (gain_grad / population))
    return keep_inside(lowered)


def split_cores(ids, parts, own_out, send_out):
    first = ids[1] == 0
    width = parts[0].shape[1]
    for k in range(2):
        a, b = parts[2 * k], parts[2 * k + 1]
        own_out[:, k * width : (k + 1) * width] = jnp.where(first, a, b)
        send_out[:, k * width : (k + 1) * width] = jnp.where(first, b, a).astype(BF)


def expand_back_kernel(population, ids, stat, moments, pre, outside, own_prm, w, low_out, own_out, send_out, sums_out):
    sums = jnp.sum(stat[...], 0)
    sums_out[...] = sums
    low = norm_back(sums, population, moments, pre, outside, own_prm[0:1, 512:]).astype(BF)
    low_out[...] = low
    acc = None
    for h in range(2):
        part = dot_nt(low[:, h * 512 : (h + 1) * 512], expand_weights(ids, w, h))
        acc = part if acc is None else acc + part
    split_cores(ids, [acc[:, n * 128 : (n + 1) * 128] for n in range(4)], own_out, send_out)


def expand_grad(ids, hid, low, held):
    grad = dot_tn(hid[...], low[...])
    lane_blocks = 512 // held.shape[2]
    depth = held.shape[1] // lane_blocks
    for h in range(2):
        for p in range(PIECES):
            piece = grad[p * depth : (p + 1) * depth, h * 512 : (h + 1) * 512].astype(BF)
            if lane_blocks == 1:
                held[h * PIECES + p] = piece
            else:
                for i in range(lane_blocks):
                    held[h * PIECES + p, i * depth : (i + 1) * depth] = piece[:, i * 128 : (i + 1) * 128]


def inner_back_kernel(lo, own_part, recv_part, moments, pre, own_prm, out, stat_out):
    normed = (pre[...] - moments[0:1]) * moments[1:2]
    v = own_prm[0:1, lo : lo + 256] * normed + own_prm[1:2, lo : lo + 256]
    upstream = (own_part[...] + recv_part[...].astype(F32)) * silu_slope(v)
    upstream = keep_inside(upstream)
    out[...] = upstream
    stat_out[...] = jnp.broadcast_to(column_sums(upstream, upstream * normed)[None], stat_out.shape)


def spatial_back_kernel(population, ids, stat, moments, pre, upstream, own_prm, w, shifts, own_out, send_out, sums_out):
    sums = jnp.sum(stat[:, pl.ds(ids[1], 1)], axis=(0, 1, 2))
    sums_out[...] = sums
    low = norm_back(sums, population, moments, pre, upstream, own_prm[0:1, 256:512])
    fill_shifts(shifts, low, 1)
    acc = None
    for tap in range(9):
        at = LINE * (2 - tap // 3)
        part = dot_nt(shifts[tap % 3, at : at + SPAN], tap_weights(ids, w, tap))
        acc = part if acc is None else acc + part
    acc = squeeze(acc)
    split_cores(ids, [acc[:, n * 128 : (n + 1) * 128] for n in range(4)], own_out, send_out)


def spatial_grad(ids, hid, shifts, held):
    turned = hid[...].T
    depth = held.shape[1]
    for tap in range(9):
        at = LINE * (2 - tap // 3)
        grad = dot(turned, shifts[tap % 3, at : at + SPAN]).astype(BF)
        row = 0
        for p, a, b in tap_segments(tap, depth):
            for h in range(2):
                held[h * PIECES + p, a:b] = grad[row : row + b - a, h * 128 : (h + 1) * 128]
            row += b - a


def reduce_back_kernel(population, ids, stat, moments, pre, upstream, own_prm, w, low_out, own_out, send_out, sums_out):
    sums = jnp.sum(stat[:, pl.ds(ids[1], 1)], axis=(0, 1, 2))
    sums_out[...] = sums
    low = norm_back(sums, population, moments, pre, upstream, own_prm[0:1, 0:256]).astype(BF)
    low_out[...] = low
    core = ids[1]
    for c, dst in ((1 - core, send_out), (core, own_out)):
        for k in range(2):
            for j in range(2):
                p = 2 * (2 * k + c) + j
                part = dot_nt(low, lanes([piece_of(ids, w, 0, p), piece_of(ids, w, 1, p)]))
                at = k * 512 + j * 256
                dst[:, at : at + 256] = part.astype(dst.dtype)


def reduce_grad(ids, xo, xt, low, held):
    core = ids[1]
    for c, src in ((core, xo), (1 - core, xt)):
        grad = dot_tn(src[...], low[...]).astype(BF)
        for k in range(2):
            for j in range(2):
                p = 2 * (2 * k + c) + j
                at = k * 512 + j * 256
                for h in range(2):
                    held[h * PIECES + p] = grad[at : at + 256, h * 128 : (h + 1) * 128]


def leave_kernel(ids, full, keep_out, send_out):
    first = ids[0] == 0
    a = full[:, :512]
    b = full[:, 512:]
    keep_out[...] = jnp.where(first, a, b)
    send_out[...] = jnp.where(first, b, a).astype(BF)


def leave_sum_kernel(ids, outside, own_part, recv_part, keep_out, send_out):
    first = ids[0] == 0
    full = outside[...] + own_part[...] + recv_part[...].astype(F32)
    a = full[:, :512]
    b = full[:, 512:]
    keep_out[...] = jnp.where(first, a, b)
    send_out[...] = jnp.where(first, b, a).astype(BF)


def arrive_kernel(ids, keep, recv, out):
    x = ids[0]
    for src, owner in ((keep, x), (recv, 1 - x)):
        for i in range(NIMG):
            img = src[i * IMG : (i + 1) * IMG].astype(F32).reshape(SIDE, LINE, src.shape[1])
            out[owner * NIMG + i] = img[:, :SIDE, :]


def moments_step(first, second, gradient):
    first_new = FIRST_DECAY * first + (1.0 - FIRST_DECAY) * gradient
    second_new = SECOND_DECAY * second + (1.0 - SECOND_DECAY) * gradient * gradient
    update = (first_new / (1.0 - FIRST_DECAY**STEP)) / (
        jnp.sqrt(second_new / (1.0 - SECOND_DECAY**STEP)) + ADAM_EPSILON
    )
    return second_new, update


def cell(v, lane):
    return jnp.where(lax.broadcasted_iota(jnp.int32, (1, 128), 1) == lane, jnp.sum(v), 0.0)


def lamb_kernel(plans, cuts, lines, arrays, *refs):
    blocks = iter(refs[:arrays])
    refs = refs[arrays:]
    count = sum(len(cut) for cut in cuts)
    masters, firsts, seconds = (refs[i * count : (i + 1) * count] for i in range(3))
    before = refs[3 * count : 3 * count + lines]
    outs = refs[len(refs) - 3 * count - 1 :]
    line = jnp.zeros((1, 128), F32)
    for ref in before:
        line = line + ref[...]
    i = 0
    for plan, cut in zip(plans, cuts):
        total = evaluate(plan, blocks)[0]
        for (b, m), lo, hi in cut:
            grad = total[lo:hi]
            master = masters[i][0]
            if grad.shape != master.shape:
                depth = master.shape[0]
                grad = lanes([grad[n * depth : (n + 1) * depth] for n in range(grad.shape[0] // depth)])
            second_new, update = moments_step(firsts[i][0], seconds[i][0], grad)
            update = update + WEIGHT_DECAY * master
            outs[3 * i][0] = grad
            outs[3 * i + 1][0] = second_new
            outs[3 * i + 2][0] = update
            line = line + cell(master * master, (b * 3 + m) * 2) + cell(update * update, (b * 3 + m) * 2 + 1)
            i += 1
    outs[-1][...] = jnp.broadcast_to(line[None], outs[-1].shape) if len(outs[-1].shape) == 3 else line


def lamb(sources, masters, firsts, seconds, filled, lines, count):
    whole = pl.BlockSpec(memory_space=pltpu.VMEM)
    tasks = [task for task, _ in sources]
    cuts = [cut for _, cut in sources]
    items = [item for cut in cuts for item, _, _ in cut]
    args, specs = slices(tasks, 1, 0)
    arrays = len(args)
    outs, out_specs, aliases = [], [], {}

    def one(b, m):
        return pl.BlockSpec((1,) + masters[m].shape[1:], lambda _: (b, 0, 0))

    for source in (masters, firsts, seconds):
        for b, m in items:
            args.append(source[m])
            specs.append(one(b, m))
    for line in lines:
        args.append(line)
        specs.append(whole)
    for b, m in items:
        for k in range(3):
            if filled[m] is not None:
                aliases[len(args)] = len(outs)
                args.append(filled[m][k])
                specs.append(pl.BlockSpec(memory_space=pl.ANY))
            outs.append(jax.ShapeDtypeStruct(masters[m].shape, F32))
            out_specs.append(one(b, m))
    outs.append(jax.ShapeDtypeStruct((count, 1, 128) if count else (1, 128), F32))
    out_specs.append(whole)
    found = pl.pallas_call(
        functools.partial(lamb_kernel, [task.plan() for task in tasks], cuts, len(lines), arrays),
        out_shape=outs,
        grid=(1,),
        in_specs=specs,
        out_specs=out_specs,
        input_output_aliases=aliases,
        compiler_params=pltpu.CompilerParams(vmem_limit_bytes=16 * 1024 * 1024),
        name="lamb",
    )(*args)
    for i, (b, m) in enumerate(items):
        filled[m] = tuple(found[3 * i : 3 * i + 3])
    return found[-1]


def renew_kernel(blocks, stat, *refs):
    masters, updates, outs, norms_out = refs[0:3], refs[3:6], refs[6:9], refs[9]
    norms = jnp.sqrt(jnp.sum(stat[...], 0))
    norms_out[...] = norms
    for b in range(blocks):
        for m in range(3):
            at = (b * 3 + m) * 2
            ratio = norms[:, at : at + 1] / norms[:, at + 1 : at + 2]
            outs[m][b] = masters[m][b] - MATRIX_RATE * ratio * updates[m][b]


def norm_kernel(blocks, ids, *refs):
    sums = refs[: 3 * blocks]
    params, first, second = refs[3 * blocks : 3 * blocks + 3]
    grads_out, square_out, new_out = refs[3 * blocks + 3 :]
    front = ids[0] == 0
    for b in range(blocks):
        parts = [[], []]
        for n in range(3):
            pair = unpack_rows(sums[3 * b + n][...])
            for kind in range(2):
                v = pair[1 - kind]
                half = v.shape[1] // 2
                parts[kind].append(jnp.where(front, v[:, :half], v[:, half:]))
        for kind in range(2):
            g = lanes(parts[kind])
            second_new, update = moments_step(first[b, kind], second[b, kind], g)
            grads_out[b, kind] = g
            square_out[b, kind] = second_new
            new_out[b, kind] = params[b, kind] - NORM_RATE * update


def exchange(step):
    pairs = []
    for i in range(32):
        core = (i >> 3) & 1
        pairs.append((i, i ^ (4, 2, 16 if core else 1, 1 if core else 16)[step]))
    return pairs


class Gather:
    def __init__(self, held):
        self.parts = (held,)

    def step(self, step, *after):
        if after:
            self.wait(*after)
        held = self.held()
        self.parts = (held, lax.ppermute(held, ALL, exchange(step)))

    def wait(self, *after):
        self.parts = order(self.parts, *after)

    def held(self):
        return self.parts[0] if len(self.parts) == 1 else jnp.concatenate(self.parts, 0)

    def last(self):
        return self.parts[-1]

    def weight(self):
        return list(self.parts), (0, self.parts[0].shape[1])


def order(value, *before):
    return lax.optimization_barrier((value, before))[0]


class Scatter:
    def __init__(self, near=None, far=None, parts=()):
        self.terms = [] if near is None else [near]
        self.far = far
        self.parts = parts

    def wait(self, *after):
        for part in self.parts:
            part.wait(*after)
        if self.terms:
            self.terms = list(order(tuple(self.terms), *after))

    def arrays(self):
        return [array for part in self.parts for array in part.arrays()] + self.terms

    def rows(self):
        return self.terms[0].shape[1] if self.terms else sum(part.rows() for part in self.parts)

    def plan(self):
        return [part.plan() for part in self.parts], len(self.terms)

    def send(self, step, value):
        self.terms.append(lax.ppermute(value, ALL, exchange(step)))


def evaluate(plan, refs):
    parts, count = plan
    found = [jnp.concatenate([evaluate(part, refs) for part in parts], axis=1)] if parts else []
    found += [next(refs)[...].astype(F32) for _ in range(count)]
    return functools.reduce(jnp.add, found)


def slices(tasks, size, at):
    arrays = [array for task in tasks for array in task.arrays()]
    return arrays, [pl.BlockSpec((size,) + array.shape[1:], lambda _: (at, 0, 0)) for array in arrays]


def add_up_kernel(plans, *refs):
    blocks = iter(refs[: len(refs) - len(plans)])
    for plan, out in zip(plans, refs[len(refs) - len(plans) :]):
        out[...] = evaluate(plan, blocks).astype(out.dtype)


def advance_sums(steps, *after):
    arrays, specs, outs, plans = [], [], [], []
    for task, step in steps:
        task.wait(*after)
    for task, step in steps:
        size = 1 << step
        more, blocks = slices([task], size, 1)
        arrays += more
        specs += blocks
        outs.append(jax.ShapeDtypeStruct((size, task.rows(), 128), BF))
        plans.append(task.plan())
    sends = pl.pallas_call(
        functools.partial(add_up_kernel, plans),
        out_shape=outs,
        grid=(1,),
        in_specs=specs,
        out_specs=[pl.BlockSpec(memory_space=pltpu.VMEM)] * len(outs),
        compiler_params=pltpu.CompilerParams(vmem_limit_bytes=16 * 1024 * 1024),
        name="add_up",
    )(*arrays)
    for (task, step), value in zip(steps, sends):
        task.send(step, value)
    return sends


def body(
    wide,
    block_input,
    out_grad,
    conv_reduce,
    conv_spatial,
    conv_expand,
    first_reduce,
    first_spatial,
    first_expand,
    second_reduce,
    second_spatial,
    second_expand,
    norm_params,
    norm_first,
    norm_second,
):
    blocks = conv_reduce.shape[0]
    population = float(block_input.shape[0] * SIDE * SIDE * wide)
    count = 4 * wide
    x = lax.axis_index("x").astype(jnp.int32)
    core = lax.axis_index("core").astype(jnp.int32)
    w = lax.axis_index("wide").astype(jnp.int32)
    fast = wide == PIECES
    here = jnp.stack([x, core, w, jnp.zeros((), jnp.int32)])
    count_up = jnp.arange(2 * PIECES, dtype=jnp.int32)
    ids = jnp.concatenate([here, count_up, count_up])
    to_x = count_up // PIECES
    to_w = count_up % PIECES

    apart_x = to_x ^ x
    apart_w = to_w ^ w
    back = jnp.where(core == 0, apart_w & 1, apart_x)
    front = jnp.where(core == 0, apart_x, apart_w & 1)
    places = front * 8 + back * 4 + ((apart_w & 2) | (apart_w >> 2))
    bit3, bit2 = count_up >> 3, (count_up >> 2) & 1
    from_x = x ^ jnp.where(core == 0, bit3, bit2)
    from_w = w ^ (jnp.where(core == 0, bit2, bit3) | (count_up & 2) | ((count_up & 1) << 2))
    relative = jnp.concatenate([here, places, from_x * PIECES + from_w])

    swap = [(0, 1), (1, 0)]

    def over_core(v):
        return lax.ppermute(v, "core", swap)

    def over_x(v):
        return lax.ppermute(v, "x", swap)

    def share(v, axes):
        return lax.all_to_all(v, axes, 0, 0)

    def run(kernel, outs, *args, places=None, **kw):
        return call(kernel, outs, ids if places is None else places, *args, smem=(0,), **kw)

    wide_row = norm_params.shape[-1]
    near = norm_params.reshape(2 * blocks, wide_row)
    both = jnp.stack([near, over_core(near)])
    far = over_x(both)
    own_all, oth_all = run(
        params_kernel, [((2 * blocks, 2 * wide_row), F32)] * 2, both, far, name="norm_rows"
    )
    own_prm = [own_all[2 * b : 2 * b + 2] for b in range(blocks)]
    oth_prm = [oth_all[2 * b : 2 * b + 2] for b in range(blocks)]

    act = (ROWS, 512)
    keep_x, send_x, keep_g, send_g = run(enter_kernel, [(act, BF)] * 4, block_input, out_grad, name="enter")
    recv_x = over_x(send_x)
    low_stream = stream = run(join_kernel, [((ROWS, 1024), BF)], keep_x, recv_x, name="join")[0]

    def gather(shard, columns):
        whole = lax.all_gather(shard.astype(BF), CROSS, axis=0, tiled=True).reshape(2 * PIECES, -1, columns)
        return [whole], (0, whole.shape[1])

    table = relative if fast else ids
    tables = [table] + [ids] * (blocks - 1)
    gathers = []
    weights = None
    if fast:
        depth = conv_expand.shape[1]

        def shards(b):
            blocked = conv_expand[b].astype(BF).reshape(depth, 4, 128).swapaxes(0, 1).reshape(4 * depth, 128)
            return [conv_reduce[b].astype(BF), conv_spatial[b].astype(BF), blocked]

        gathers = [Gather(shard[None]) for shard in shards(0)]
        gathers[0].step(0, send_x)
        gathers[0].step(1)
        gathers[1].step(0, gathers[0].parts[0])
        gathers[0].step(2, recv_x, far)
        gathers[1].step(1, gathers[0].parts[0])
        gathers[2].step(0, gathers[1].parts[0])
        gathers[2].step(1)
        gathers[0].step(3)
        wholes = [lax.all_gather(jnp.concatenate(shards(b)), CROSS, axis=0, tiled=False) for b in range(1, blocks)]
        one = conv_reduce.shape[1]
        two = one + conv_spatial.shape[1]
        cuts = ((0, one), (one, two), (two, two + 4 * depth))
    else:
        weights = [
            (gather(conv_reduce[b], 128), gather(conv_spatial[b], 128), gather(conv_expand[b], 512)) for b in range(blocks)
        ]

    def weight_of(b, m):
        if not fast:
            return weights[b][m]
        return gathers[m].weight() if b == 0 else ([wholes[b - 1]], cuts[m])

    def advance(stage, stat, out):
        if not fast:
            return
        if stage == 1:
            gathers[1].step(2, out)
            gathers[1].step(3, stat)
        elif stage == 2:
            gathers[2].step(2, gathers[1].last())
            gathers[2].step(3, out)

    inner = (count, 4, 128)
    outer = (2 * wide, 16, 128)
    saved = []
    for b in range(blocks):
        other = over_core(low_stream)
        pre1, low1, stat = run(
            reduce_kernel,
            [((ROWS, 256), F32), ((ROWS, 256), BF), (inner, F32)],
            low_stream,
            other,
            weight=weight_of(b, 0),
            places=tables[b],
            name="reduce",
        )
        low1 = over_core(low1)
        stat = share(stat, ALL)
        advance(3 * b + 1, stat, pre1)
        if fast and b == 0:
            stat, *wholes = lax.optimization_barrier((stat, *wholes))
        stat = stat.reshape(2, 2, wide, 4, 128)
        hid1, moments1, pre2, low2, stat = run(
            functools.partial(spatial_kernel, population),
            [((SPAN, 512), BF), ((8, 256), F32), ((ROWS, 256), F32), ((ROWS, 256), BF), (inner, F32)],
            stat,
            pre1,
            low1,
            own_prm[b],
            oth_prm[b],
            weight=weight_of(b, 1),
            scratch=[pltpu.VMEM((3, SPAN + 2 * LINE, 512), BF)],
            places=tables[b],
            name="spatial",
        )
        low2 = over_core(low2)
        if b > 0:
            stat = order(stat, low2)
        stat = share(stat, ALL)
        advance(3 * b + 2, stat, pre2)
        stat = stat.reshape(2, 2, wide, 4, 128)
        before = stat
        hid2, moments2, pre3, stat = run(
            functools.partial(expand_kernel, population),
            [((ROWS, 512), BF), ((8, 256), F32), ((ROWS, 1024), F32), (outer, F32)],
            stat,
            pre2,
            low2,
            own_prm[b],
            oth_prm[b],
            weight=weight_of(b, 2),
            places=tables[b],
            name="expand",
        )
        if b == blocks - 1:
            recv_g = over_x(order(send_g, before))
        stat = share(stat, CROSS)
        advance(3 * b + 3, stat, pre3)
        item = dict(
            xo=low_stream, xt=other, stream=stream, pre1=pre1, hid1=hid1, m1=moments1, pre2=pre2, hid2=hid2, m2=moments2, pre3=pre3
        )
        if b < blocks - 1:
            item["m3"], stream, low_stream = call(
                functools.partial(close_kernel, population),
                [((8, 1024), F32), ((ROWS, 1024), F32), ((ROWS, 1024), BF)],
                stat,
                pre3,
                stream,
                own_prm[b],
                name="close",
            )
        else:
            item["m3"], result, outside, stat = run(
                functools.partial(last_kernel, population),
                [((8, 1024), F32), ((ROWS, 1024), F32), ((ROWS, 1024), F32), (outer, F32)],
                stat,
                pre3,
                stream,
                own_prm[b],
                keep_g,
                recv_g,
                name="last",
            )
        saved.append(item)

    tasks = {}

    def hook(kind, b, grads):
        if not fast:
            return []
        near, far = grads
        tasks[kind, b] = Scatter(near, far)
        if (kind, b) != ("reduce", 1):
            tasks[kind, b].send(3, far)
        return [far]

    def ahead(kind, b, stat):
        if not fast:
            return stat
        steps = []
        if b == 1 and kind == "spatial":
            stat = order(stat, tasks["expand", 1].terms[-1])
        if b == 0 and kind == "reduce":
            stat = order(stat, *(tasks[name].terms[-1] for name in ("big", ("expand", 0), ("reduce", 1))))
        if b == 1 and kind == "reduce":
            tasks["big"] = Scatter(parts=(tasks["expand", 1], tasks["spatial", 1]))
            steps = [(tasks["big"], 2)]
        if b == 0 and kind == "expand":
            tasks["reduce", 1].send(3, order(tasks["reduce", 1].far, stat))
            steps = [(tasks["big"], 1)]
        if b == 0 and kind == "spatial":
            steps = [(tasks["expand", 0], 2), (tasks["reduce", 1], 2), (tasks["big"], 0)]
        if b == 0 and kind == "reduce":
            steps = [(tasks["spatial", 0], 2)]
        return order(stat, *advance_sums(steps, stat)) if steps else stat

    def whole(task, b, m):
        return task, [((b, m), 0, task.rows())]

    def step_of(sources, last=False):
        line = lamb(sources, masters, firsts, seconds, filled, lines if last else [], count if last else 0)
        lines.append(line)
        return line

    images = []

    def finish_images(full, gate, kernel, name):
        keep, send = run(kernel, [(act, F32), (act, BF)], *order(full, gate), name=name)
        images.extend(run(arrive_kernel, [(block_input.shape, F32)], keep, over_x(send), name="arrive"))
        return send

    def finish():
        small, middle, large = (tasks[kind, 0] for kind in ("expand", "reduce", "spatial"))
        advance_sums([(small, 1), (tasks["reduce", 1], 1)], middle.terms[0])
        leaving = finish_images((result,), middle.terms[0], leave_kernel, "leave")
        big = tasks["big"]
        cut = 4 * conv_expand.shape[1]
        sent = advance_sums([(large, 1)], small.terms[-1], tasks["reduce", 1].terms[-1], leaving)
        rest = Scatter(parts=(small, tasks["reduce", 1]))
        sent = advance_sums([(middle, 2), (rest, 0)], sent)
        finish_images(after, sent[0], leave_sum_kernel, "leave_sum")
        line = step_of([(big, [((1, 2), 0, cut), ((1, 1), cut, big.rows())])])
        sent = advance_sums([(middle, 1)], sent, line, norm_grads)
        sent = advance_sums([(large, 0)], sent, rest.terms[-1])
        advance_sums([(middle, 0)], sent)
        line = step_of([(rest, [((0, 2), 0, cut), ((1, 0), cut, rest.rows())])])
        for task in (large, middle):
            task.wait(line, *images)
        return [[whole(large, 0, 1), whole(middle, 0, 0)]]

    def gradient(b, m, kernel, *args, name):
        parts, (lo, hi) = weight_of(b, m)
        shape = (hi - lo, parts[0].shape[2])
        whole = pltpu.VMEM((2 * PIECES,) + shape, BF)
        half = ((PIECES,) + shape, BF)

        def halves(ids, *refs):
            kernel(ids, *refs[:-3], refs[-1])
            deal(ids, refs[-1], refs[-3], refs[-2])

        return run(halves, [half] * 2, *args, scratch=[whole], places=table, name=name)

    sums = [None] * (3 * blocks)
    local = [None] * blocks
    after = None
    for b in reversed(range(blocks)):
        item = saved[b]
        w_reduce, w_spatial, w_expand = (weight_of(b, m) for m in range(3))
        if after is not None:
            outside, stat = call(
                outer_back_kernel,
                [((ROWS, 1024), F32), (outer, F32)],
                item["m3"],
                item["pre3"],
                item["stream"],
                own_prm[b],
                *after,
                name="outer_back",
            )
        stat = ahead("expand", b, share(stat, CROSS))
        low3, own_part, send, sums[3 * b + 2] = run(
            functools.partial(expand_back_kernel, population),
            [((ROWS, 1024), BF), ((ROWS, 256), F32), ((ROWS, 256), BF), ((16, 128), F32)],
            stat,
            item["m3"],
            item["pre3"],
            outside,
            own_prm[b],
            weight=w_expand,
            places=tables[b],
            name="expand_back",
        )
        recv = over_core(send)
        grad_expand = gradient(b, 2, expand_grad, item["hid2"], low3, name="expand_grad")
        own_part = order(own_part, *grad_expand, *hook("expand", b, grad_expand))
        upstream, stat = call(
            functools.partial(inner_back_kernel, 256),
            [((ROWS, 256), F32), (inner, F32)],
            own_part,
            recv,
            item["m2"],
            item["pre2"],
            own_prm[b],
            name="inner_back",
        )
        stat = ahead("spatial", b, share(stat, ALL)).reshape(2, 2, wide, 4, 128)
        shifts, own_part, send, sums[3 * b + 1] = run(
            functools.partial(spatial_back_kernel, population),
            [((3, SPAN + 2 * LINE, 256), BF), ((ROWS, 256), F32), ((ROWS, 256), BF), ((4, 128), F32)],
            stat,
            item["m2"],
            item["pre2"],
            upstream,
            own_prm[b],
            weight=w_spatial,
            places=tables[b],
            name="spatial_back",
        )
        recv = over_core(send)
        grad_spatial = gradient(b, 1, spatial_grad, item["hid1"], shifts, name="spatial_grad")
        own_part = order(own_part, *grad_spatial, *hook("spatial", b, grad_spatial))
        upstream, stat = call(
            functools.partial(inner_back_kernel, 0),
            [((ROWS, 256), F32), (inner, F32)],
            own_part,
            recv,
            item["m1"],
            item["pre1"],
            own_prm[b],
            name="inner_back",
        )
        stat = ahead("reduce", b, share(stat, ALL)).reshape(2, 2, wide, 4, 128)
        low1, own_part, send, sums[3 * b] = run(
            functools.partial(reduce_back_kernel, population),
            [((ROWS, 256), BF), ((ROWS, 1024), F32), ((ROWS, 1024), BF), ((4, 128), F32)],
            stat,
            item["m1"],
            item["pre1"],
            upstream,
            own_prm[b],
            weight=w_reduce,
            places=tables[b],
            name="reduce_back",
        )
        recv = over_core(send)
        grad_reduce = gradient(b, 0, reduce_grad, item["xo"], item["xt"], low1, name="reduce_grad")
        own_part = order(own_part, *grad_reduce, *hook("reduce", b, grad_reduce))
        after = (outside, own_part, recv)
        local[b] = (grad_reduce, grad_spatial, grad_expand)

    def scatter(pair):
        flat = jnp.concatenate(pair).reshape(-1, pair[0].shape[-1])
        return lax.psum_scatter(flat, CROSS, scatter_dimension=0, tiled=True).astype(F32)

    norm_shape = (norm_params.shape, F32)
    norm_grads, norm_square, norm_new = run(
        functools.partial(norm_kernel, blocks), [norm_shape] * 3, *sums, norm_params, norm_first, norm_second, name="norms"
    )
    masters = (conv_reduce, conv_spatial, conv_expand)
    firsts = (first_reduce, first_spatial, first_expand)
    seconds = (second_reduce, second_spatial, second_expand)
    filled = [None] * 3
    lines = []
    if fast:
        batches = finish()
    else:
        finish_images((result,), after[1], leave_kernel, "leave")
        finish_images(after, after[1], leave_sum_kernel, "leave_sum")
        batches = []
        for b in range(blocks):
            for m in range(3):
                part = scatter(local[b][m])
                batches.append([(Scatter(part[None]), [((b, m), 0, part.shape[0])])])
    for n, sources in enumerate(batches):
        step_of(sources, n == len(batches) - 1)
    block_output, input_grad = images
    gradients = [filled[m][0] for m in range(3)]
    squares = [filled[m][1] for m in range(3)]
    updates = [filled[m][2] for m in range(3)]
    line = order(lines[-1], block_output, input_grad, norm_grads, norm_square, norm_new)
    stat = share(line, ALL)
    shapes = [(m.shape, F32) for m in masters]
    renewed = call(
        functools.partial(renew_kernel, blocks), shapes + [((1, 128), F32)], stat, *masters, *updates, name="renew"
    )
    layer_norms = renewed[3][0, : 6 * blocks].reshape(blocks, 3, 2)
    return (
        block_output,
        input_grad,
        *gradients,
        *squares,
        *renewed[:3],
        norm_grads,
        norm_square,
        norm_new,
        layer_norms,
    )


def solution(mesh):
    wide = mesh.shape["wide"]
    fine = Mesh(np.asarray(mesh.devices).reshape(2, 2, wide), ALL)
    narrow = ("x", "core")
    image = P("wide", None, None, narrow)
    matrix = P(None, "wide", narrow)
    row = P(None, None, narrow, None)
    return jax.shard_map(
        functools.partial(body, wide),
        mesh=fine,
        in_specs=(image,) * 2 + (matrix,) * 9 + (row,) * 3,
        out_specs=(image,) * 2 + (matrix,) * 9 + (row,) * 3 + (P(),),
        check_vma=False,
    )
```

```python
import functools

import jax
import jax.numpy as jnp
import numpy as np
from jax import lax
from jax.experimental import pallas as pl
from jax.experimental.pallas import tpu as pltpu
from jax.sharding import Mesh
from jax.sharding import PartitionSpec as P

STEP = 10
BN_EPS = 1e-05
FIRST_DECAY = 0.9
SECOND_DECAY = 0.999
ADAM_EPSILON = 1e-06
WEIGHT_DECAY = 0.01
MATRIX_RATE = 0.5
NORM_RATE = 0.3

ALL = ("x", "core", "wide")
CROSS = ("x", "wide")
BF = jnp.bfloat16
F32 = jnp.float32

SIDE = 14
LINE = 16
IMG = SIDE * LINE
NIMG = 2
ROWS = NIMG * IMG
SPAN = ROWS + LINE * (NIMG - 1)
PIECES = 8


def dot(a, b):
    return lax.dot_general(a, b, (((1,), (0,)), ((), ())), preferred_element_type=F32)


def dot_nt(a, b):
    return lax.dot_general(a, b, (((1,), (1,)), ((), ())), preferred_element_type=F32)


def dot_tn(a, b):
    return lax.dot_general(a, b, (((0,), (0,)), ((), ())), preferred_element_type=F32)


def lanes(parts):
    return jnp.concatenate(parts, axis=1)


def rows(parts):
    return jnp.concatenate(parts, axis=0)


def sigmoid(v):
    return 0.5 * jnp.tanh(0.5 * v) + 0.5


def silu(v):
    return v * sigmoid(v)


def silu_slope(v):
    s = sigmoid(v)
    return s * (1.0 + v * (1.0 - s))


def inside(shape):
    return (lax.broadcasted_iota(jnp.int32, shape, 0) & (LINE - 1)) < SIDE


def keep_inside(v):
    return jnp.where(inside(v.shape), v, 0.0)


def pack_rows(total, other):
    n = total.shape[1] // 128
    return rows([v[:, i * 128 : (i + 1) * 128] for v in (total, other) for i in range(n)])


def unpack_rows(block):
    n = block.shape[0] // 2
    return tuple(lanes([block[k * n + i : k * n + i + 1] for i in range(n)]) for k in range(2))


def column_sums(a, b):
    return pack_rows(jnp.sum(a, 0, keepdims=True), jnp.sum(b, 0, keepdims=True))


def mean_inverse(block, population):
    total, square = unpack_rows(block)
    mean = total / population
    return mean, lax.rsqrt(square / population - mean * mean + BN_EPS)


class Late:
    def __init__(self, buf, copy):
        self.buf = buf
        self.copy = copy
        self.shape = buf.shape
        self.waited = False
        copy.start()

    def wait(self):
        if not self.waited:
            self.copy.wait()
            self.waited = True

    def __getitem__(self, at):
        self.wait()
        return self.buf[at]


class Pair:
    def __init__(self, near, far):
        self.near = near
        self.far = far
        self.shape = near.shape

    def __getitem__(self, at):
        piece, rest = (at[0], at[1:]) if isinstance(at, tuple) else (at, ())
        inner = (piece & (PIECES - 1),) + rest
        return jnp.where(piece < PIECES, self.near[inner], self.far[inner])


def call(kernel, outs, *args, scratch=(), name=None, smem=(), limit=16, weight=None):
    vmem = pl.BlockSpec(memory_space=pltpu.VMEM)
    in_specs = [pl.BlockSpec(memory_space=pltpu.SMEM) if i in smem else vmem for i in range(len(args))]
    count = len(args)
    ins = list(args)
    scratch = list(scratch)
    cut = False
    if weight is not None:
        parts, (lo, hi) = weight
        ins += parts
        cut = parts[0].shape[1] != hi - lo
        in_specs += [pl.BlockSpec(memory_space=pl.ANY) if cut else vmem] * len(parts)
        if cut:
            scratch += [pltpu.VMEM((2 * PIECES, hi - lo, parts[0].shape[2]), BF), pltpu.SemaphoreType.DMA]
    total = len(ins)

    def whole(*refs):
        operands, results = refs[:count], refs[total:]
        if weight is None:
            return kernel(*operands, *results)
        held = refs[count:total]
        if not cut:
            return kernel(*operands, Pair(*held) if len(held) == 2 else held[0], *results)
        buf, sem = results[-2:]
        late = Late(buf, pltpu.make_async_copy(held[0].at[:, lo:hi], buf, sem))
        kernel(*operands, late, *results[:-2])
        late.wait()

    return pl.pallas_call(
        whole,
        out_shape=[jax.ShapeDtypeStruct(shape, dtype) for shape, dtype in outs],
        in_specs=in_specs,
        out_specs=[vmem] * len(outs),
        scratch_shapes=scratch,
        compiler_params=pltpu.CompilerParams(vmem_limit_bytes=limit * 1024 * 1024),
        name=name,
    )(*ins)


def place(ids, half, piece):
    return ids[4 + PIECES * half + piece]


def origin(ids, at):
    return ids[4 + 2 * PIECES + at]


def piece_of(ids, w, half, piece):
    return w[place(ids, half, piece)]


def expand_weights(ids, w, half):
    def piece(at):
        if w.shape[2] == 512:
            return w[at]
        depth = w.shape[1] // 4
        return lanes([w[at, i * depth : (i + 1) * depth] for i in range(4)])

    return rows([piece(place(ids, half, p)) for p in range(PIECES)])


def deal(ids, held, near, far):
    for start, dst in ((PIECES, far), (0, near)):
        for at in range(PIECES):
            dst[at] = held[origin(ids, start + at)]


def enter_kernel(ids, image_ref, grad_ref, keep_x, send_x, keep_g, send_g):
    x = ids[0]
    for src, keep, send in ((image_ref, keep_x, send_x), (grad_ref, keep_g, send_g)):
        for dst, owner in ((keep, x), (send, 1 - x)):
            for i in range(NIMG):
                img = src[owner * NIMG + i]
                pad = jnp.zeros((SIDE, LINE - SIDE, img.shape[2]), img.dtype)
                full = jnp.concatenate([img, pad], axis=1)
                dst[i * IMG : (i + 1) * IMG] = full.reshape(IMG, img.shape[2])


def join_kernel(ids, keep, recv, out):
    first = ids[0] == 0
    a = keep[...]
    b = recv[...]
    n = a.shape[1]
    out[:, :n] = jnp.where(first, a, b)
    out[:, n:] = jnp.where(first, b, a)


def params_kernel(ids, near_ref, far_ref, own_ref, oth_ref):
    first = ids[0] == 0
    for n, dst in ((0, own_ref), (1, oth_ref)):
        for lo, hi in ((0, 128), (128, 256), (256, 768)):
            a = near_ref[n, :, lo:hi]
            c = far_ref[n, :, lo:hi]
            dst[:, 2 * lo : lo + hi] = jnp.where(first, a, c)
            dst[:, lo + hi : 2 * hi] = jnp.where(first, c, a)


def centred(z, total, pixels):
    return keep_inside(z - total / pixels).astype(BF)


def reduce_kernel(ids, xo, xt, w, pre_out, centred_out, stat_out):
    core = ids[1]
    parts = []
    for c in (core, 1 - core):
        for k in range(2):
            for j in range(2):
                p = 2 * (2 * k + c) + j
                parts.append(lanes([piece_of(ids, w, 0, p), piece_of(ids, w, 1, p)]))
    pre = dot(lanes([xo[...], xt[...]]), rows(parts))
    total = jnp.sum(pre, 0, keepdims=True)
    stats = pack_rows(total, jnp.sum(pre * pre, 0, keepdims=True))
    pre_out[...] = pre
    centred_out[...] = centred(pre, total, NIMG * SIDE * SIDE)
    stat_out[...] = jnp.broadcast_to(stats[None], stat_out.shape)


def both_halves(ids, stat, pre, other, own_prm, oth_prm, lo, population, moments_out):
    x, core, wide = ids[0], ids[1], ids[2]
    own = stat[:, pl.ds(core, 1)]
    oth = stat[:, pl.ds(1 - core, 1)]
    own_sum = jnp.sum(own, axis=(0, 1, 2))
    oth_sum = jnp.sum(oth, axis=(0, 1, 2))
    local = stat[pl.ds(x, 1), pl.ds(1 - core, 1), pl.ds(wide, 1)].reshape(4, 128)
    mean, inverse = mean_inverse(own_sum, population)
    moments_out[...] = rows([mean, inverse, jnp.zeros((6, mean.shape[1]), F32)])
    hid_own = silu(own_prm[0:1, lo : lo + 256] * (pre[...] - mean) * inverse + own_prm[1:2, lo : lo + 256])
    mean_t, inverse_t = mean_inverse(oth_sum, population)
    local_mean = unpack_rows(local)[0] / (NIMG * SIDE * SIDE)
    hid_oth = silu(
        oth_prm[0:1, lo : lo + 256] * (other[...].astype(F32) + (local_mean - mean_t)) * inverse_t
        + oth_prm[1:2, lo : lo + 256]
    )
    hid_own = keep_inside(hid_own)
    hid_oth = keep_inside(hid_oth)
    first = core == 0
    parts = []
    for k in range(2):
        a = hid_own[:, k * 128 : (k + 1) * 128]
        b = hid_oth[:, k * 128 : (k + 1) * 128]
        parts += [jnp.where(first, a, b), jnp.where(first, b, a)]
    return lanes(parts)


def fill_shifts(dst, v, sign):
    for d in range(3):
        shifted = v if d == 1 else pltpu.roll(v, (sign * (d - 1)) % v.shape[0], 0)
        shifted = shifted.astype(BF)
        dst[d, 0:LINE] = jnp.zeros((LINE, v.shape[1]), BF)
        for i in range(NIMG):
            at = LINE + i * (IMG + LINE)
            dst[d, at : at + IMG] = shifted[i * IMG : (i + 1) * IMG]
            dst[d, at + IMG : at + IMG + LINE] = jnp.zeros((LINE, v.shape[1]), BF)


def squeeze(v):
    return rows([v[i * (IMG + LINE) : i * (IMG + LINE) + IMG] for i in range(NIMG)])


def tap_segments(tap, depth):
    lo, hi = tap * 512, (tap + 1) * 512
    found = []
    while lo < hi:
        piece = lo // depth
        end = min(hi, (piece + 1) * depth)
        found.append((piece, lo - piece * depth, end - piece * depth))
        lo = end
    return found


def tap_weights(ids, w, tap):
    return lanes(
        [
            rows([w[place(ids, h, p), a:b] for p, a, b in tap_segments(tap, w.shape[1])])
            for h in range(2)
        ]
    )


def spatial_kernel(
    population, ids, stat, pre, other, own_prm, oth_prm, w, hid_out, moments_out, pre_out, centred_out, stat_out, shifts
):
    hid = both_halves(ids, stat, pre, other, own_prm, oth_prm, 0, population, moments_out)
    fill_shifts(shifts, hid, -1)
    hid_out[...] = shifts[1, LINE : LINE + SPAN]
    acc = None
    for tap in range(9):
        at = (tap // 3) * LINE
        part = dot(shifts[tap % 3, at : at + SPAN], tap_weights(ids, w, tap))
        acc = part if acc is None else acc + part
    pre2 = keep_inside(squeeze(acc))
    total = jnp.sum(pre2, 0, keepdims=True)
    stats = pack_rows(total, jnp.sum(pre2 * pre2, 0, keepdims=True))
    pre_out[...] = pre2
    centred_out[...] = centred(pre2, total, NIMG * SIDE * SIDE)
    stat_out[...] = jnp.broadcast_to(stats[None], stat_out.shape)


def expand_kernel(population, ids, stat, pre, other, own_prm, oth_prm, w, hid_out, moments_out, pre_out, stat_out):
    hid = both_halves(ids, stat, pre, other, own_prm, oth_prm, 256, population, moments_out).astype(BF)
    hid_out[...] = hid
    total = []
    square = []
    for h in range(2):
        pre3 = dot(hid, expand_weights(ids, w, h))
        pre_out[:, h * 512 : (h + 1) * 512] = pre3
        total.append(jnp.sum(pre3, 0, keepdims=True))
        square.append(jnp.sum(pre3 * pre3, 0, keepdims=True))
    stats = pack_rows(lanes(total), lanes(square))
    stat_out[...] = jnp.broadcast_to(stats[None], stat_out.shape)


def close_kernel(population, stat, pre, stream, own_prm, moments_out, out, low_out):
    mean, inverse = mean_inverse(jnp.sum(stat[...], 0), population)
    moments_out[...] = rows([mean, inverse, jnp.zeros((6, mean.shape[1]), F32)])
    v = own_prm[0:1, 512:] * (pre[...] - mean) * inverse + own_prm[1:2, 512:] + stream[...].astype(F32)
    result = keep_inside(silu(v))
    out[...] = result
    low_out[...] = result.astype(BF)


def last_kernel(population, ids, stat, pre, stream, own_prm, keep_g, recv_g, moments_out, out, outside_out, stat_out):
    mean, inverse = mean_inverse(jnp.sum(stat[...], 0), population)
    moments_out[...] = rows([mean, inverse, jnp.zeros((6, mean.shape[1]), F32)])
    normed = (pre[...] - mean) * inverse
    v = own_prm[0:1, 512:] * normed + own_prm[1:2, 512:] + stream[...].astype(F32)
    s = sigmoid(v)
    out[...] = v * s
    first = ids[0] == 0
    a = keep_g[...]
    b = recv_g[...]
    grad = lanes([jnp.where(first, a, b), jnp.where(first, b, a)]).astype(F32)
    outside = keep_inside(grad * (s * (1.0 + v * (1.0 - s))))
    outside_out[...] = outside
    stat_out[...] = jnp.broadcast_to(column_sums(outside, outside * normed)[None], stat_out.shape)


def outer_back_kernel(moments, pre, stream, own_prm, outside_after, own_part, recv_part, outside_out, stat_out):
    mean = moments[0:1]
    inverse = moments[1:2]
    normed = (pre[...] - mean) * inverse
    v = own_prm[0:1, 512:] * normed + own_prm[1:2, 512:] + stream[...].astype(F32)
    upstream = outside_after[...] + own_part[...] + recv_part[...].astype(F32)
    outside = keep_inside(upstream * silu_slope(v))
    outside_out[...] = outside
    stat_out[...] = jnp.broadcast_to(column_sums(outside, outside * normed)[None], stat_out.shape)


def norm_back(sums, population, moments, pre, upstream, gain):
    shift_grad, gain_grad = unpack_rows(sums)
    mean = moments[0:1]
    inverse = moments[1:2]
    normed = (pre[...] - mean) * inverse
    lowered = gain * inverse * (upstream[...] - shift_grad / population - normed * (gain_grad / population))
    return keep_inside(lowered)


def split_cores(ids, parts, own_out, send_out):
    first = ids[1] == 0
    width = parts[0].shape[1]
    for k in range(2):
        a, b = parts[2 * k], parts[2 * k + 1]
        own_out[:, k * width : (k + 1) * width] = jnp.where(first, a, b)
        send_out[:, k * width : (k + 1) * width] = jnp.where(first, b, a).astype(BF)


def expand_back_kernel(population, ids, stat, moments, pre, outside, own_prm, w, low_out, own_out, send_out, sums_out):
    sums = jnp.sum(stat[...], 0)
    sums_out[...] = sums
    low = norm_back(sums, population, moments, pre, outside, own_prm[0:1, 512:]).astype(BF)
    low_out[...] = low
    acc = None
    for h in range(2):
        part = dot_nt(low[:, h * 512 : (h + 1) * 512], expand_weights(ids, w, h))
        acc = part if acc is None else acc + part
    split_cores(ids, [acc[:, n * 128 : (n + 1) * 128] for n in range(4)], own_out, send_out)


def expand_grad(ids, hid, low, held):
    grad = dot_tn(hid[...], low[...])
    lane_blocks = 512 // held.shape[2]
    depth = held.shape[1] // lane_blocks
    for h in range(2):
        for p in range(PIECES):
            piece = grad[p * depth : (p + 1) * depth, h * 512 : (h + 1) * 512].astype(BF)
            if lane_blocks == 1:
                held[h * PIECES + p] = piece
            else:
                for i in range(lane_blocks):
                    held[h * PIECES + p, i * depth : (i + 1) * depth] = piece[:, i * 128 : (i + 1) * 128]


def inner_back_kernel(lo, own_part, recv_part, moments, pre, own_prm, out, stat_out):
    normed = (pre[...] - moments[0:1]) * moments[1:2]
    v = own_prm[0:1, lo : lo + 256] * normed + own_prm[1:2, lo : lo + 256]
    upstream = (own_part[...] + recv_part[...].astype(F32)) * silu_slope(v)
    upstream = keep_inside(upstream)
    out[...] = upstream
    stat_out[...] = jnp.broadcast_to(column_sums(upstream, upstream * normed)[None], stat_out.shape)


def spatial_back_kernel(population, ids, stat, moments, pre, upstream, own_prm, w, shifts, own_out, send_out, sums_out):
    sums = jnp.sum(stat[:, pl.ds(ids[1], 1)], axis=(0, 1, 2))
    sums_out[...] = sums
    low = norm_back(sums, population, moments, pre, upstream, own_prm[0:1, 256:512])
    fill_shifts(shifts, low, 1)
    acc = None
    for tap in range(9):
        at = LINE * (2 - tap // 3)
        part = dot_nt(shifts[tap % 3, at : at + SPAN], tap_weights(ids, w, tap))
        acc = part if acc is None else acc + part
    acc = squeeze(acc)
    split_cores(ids, [acc[:, n * 128 : (n + 1) * 128] for n in range(4)], own_out, send_out)


def spatial_grad(ids, hid, shifts, held):
    turned = hid[...].T
    depth = held.shape[1]
    for tap in range(9):
        at = LINE * (2 - tap // 3)
        grad = dot(turned, shifts[tap % 3, at : at + SPAN]).astype(BF)
        row = 0
        for p, a, b in tap_segments(tap, depth):
            for h in range(2):
                held[h * PIECES + p, a:b] = grad[row : row + b - a, h * 128 : (h + 1) * 128]
            row += b - a


def reduce_back_kernel(population, ids, stat, moments, pre, upstream, own_prm, w, low_out, own_out, send_out, sums_out):
    sums = jnp.sum(stat[:, pl.ds(ids[1], 1)], axis=(0, 1, 2))
    sums_out[...] = sums
    low = norm_back(sums, population, moments, pre, upstream, own_prm[0:1, 0:256]).astype(BF)
    low_out[...] = low
    core = ids[1]
    for c, dst in ((1 - core, send_out), (core, own_out)):
        for k in range(2):
            for j in range(2):
                p = 2 * (2 * k + c) + j
                part = dot_nt(low, lanes([piece_of(ids, w, 0, p), piece_of(ids, w, 1, p)]))
                at = k * 512 + j * 256
                dst[:, at : at + 256] = part.astype(dst.dtype)


def reduce_grad(ids, xo, xt, low, held):
    core = ids[1]
    for c, src in ((core, xo), (1 - core, xt)):
        grad = dot_tn(src[...], low[...]).astype(BF)
        for k in range(2):
            for j in range(2):
                p = 2 * (2 * k + c) + j
                at = k * 512 + j * 256
                for h in range(2):
                    held[h * PIECES + p] = grad[at : at + 256, h * 128 : (h + 1) * 128]


def leave_kernel(ids, full, keep_out, send_out):
    first = ids[0] == 0
    a = full[:, :512]
    b = full[:, 512:]
    keep_out[...] = jnp.where(first, a, b)
    send_out[...] = jnp.where(first, b, a).astype(BF)


def leave_sum_kernel(ids, outside, own_part, recv_part, keep_out, send_out):
    first = ids[0] == 0
    full = outside[...] + own_part[...] + recv_part[...].astype(F32)
    a = full[:, :512]
    b = full[:, 512:]
    keep_out[...] = jnp.where(first, a, b)
    send_out[...] = jnp.where(first, b, a).astype(BF)


def arrive_kernel(ids, keep, recv, out):
    x = ids[0]
    for src, owner in ((keep, x), (recv, 1 - x)):
        for i in range(NIMG):
            img = src[i * IMG : (i + 1) * IMG].astype(F32).reshape(SIDE, LINE, src.shape[1])
            out[owner * NIMG + i] = img[:, :SIDE, :]


def moments_step(first, second, gradient):
    first_new = FIRST_DECAY * first + (1.0 - FIRST_DECAY) * gradient
    second_new = SECOND_DECAY * second + (1.0 - SECOND_DECAY) * gradient * gradient
    update = (first_new / (1.0 - FIRST_DECAY**STEP)) / (
        jnp.sqrt(second_new / (1.0 - SECOND_DECAY**STEP)) + ADAM_EPSILON
    )
    return second_new, update


def cell(v, lane):
    return jnp.where(lax.broadcasted_iota(jnp.int32, (1, 128), 1) == lane, jnp.sum(v), 0.0)


def lamb_kernel(plans, cuts, lines, arrays, *refs):
    blocks = iter(refs[:arrays])
    refs = refs[arrays:]
    count = sum(len(cut) for cut in cuts)
    masters, firsts, seconds = (refs[i * count : (i + 1) * count] for i in range(3))
    before = refs[3 * count : 3 * count + lines]
    outs = refs[len(refs) - 3 * count - 1 :]
    line = jnp.zeros((1, 128), F32)
    for ref in before:
        line = line + ref[...]
    i = 0
    for plan, cut in zip(plans, cuts):
        total = evaluate(plan, blocks)[0]
        for (b, m), lo, hi in cut:
            grad = total[lo:hi]
            master = masters[i][0]
            if grad.shape != master.shape:
                depth = master.shape[0]
                grad = lanes([grad[n * depth : (n + 1) * depth] for n in range(grad.shape[0] // depth)])
            second_new, update = moments_step(firsts[i][0], seconds[i][0], grad)
            update = update + WEIGHT_DECAY * master
            outs[3 * i][0] = grad
            outs[3 * i + 1][0] = second_new
            outs[3 * i + 2][0] = update
            line = line + cell(master * master, (b * 3 + m) * 2) + cell(update * update, (b * 3 + m) * 2 + 1)
            i += 1
    outs[-1][...] = jnp.broadcast_to(line[None], outs[-1].shape) if len(outs[-1].shape) == 3 else line


def lamb(sources, masters, firsts, seconds, filled, lines, count):
    whole = pl.BlockSpec(memory_space=pltpu.VMEM)
    tasks = [task for task, _ in sources]
    cuts = [cut for _, cut in sources]
    items = [item for cut in cuts for item, _, _ in cut]
    args, specs = slices(tasks, 1, 0)
    arrays = len(args)
    outs, out_specs, aliases = [], [], {}

    def one(b, m):
        return pl.BlockSpec((1,) + masters[m].shape[1:], lambda _: (b, 0, 0))

    for source in (masters, firsts, seconds):
        for b, m in items:
            args.append(source[m])
            specs.append(one(b, m))
    for line in lines:
        args.append(line)
        specs.append(whole)
    for b, m in items:
        for k in range(3):
            if filled[m] is not None:
                aliases[len(args)] = len(outs)
                args.append(filled[m][k])
                specs.append(pl.BlockSpec(memory_space=pl.ANY))
            outs.append(jax.ShapeDtypeStruct(masters[m].shape, F32))
            out_specs.append(one(b, m))
    outs.append(jax.ShapeDtypeStruct((count, 1, 128) if count else (1, 128), F32))
    out_specs.append(whole)
    found = pl.pallas_call(
        functools.partial(lamb_kernel, [task.plan() for task in tasks], cuts, len(lines), arrays),
        out_shape=outs,
        grid=(1,),
        in_specs=specs,
        out_specs=out_specs,
        input_output_aliases=aliases,
        compiler_params=pltpu.CompilerParams(vmem_limit_bytes=16 * 1024 * 1024),
        name="lamb",
    )(*args)
    for i, (b, m) in enumerate(items):
        filled[m] = tuple(found[3 * i : 3 * i + 3])
    return found[-1]


def renew_kernel(blocks, stat, *refs):
    masters, updates, outs, norms_out = refs[0:3], refs[3:6], refs[6:9], refs[9]
    norms = jnp.sqrt(jnp.sum(stat[...], 0))
    norms_out[...] = norms
    for b in range(blocks):
        for m in range(3):
            at = (b * 3 + m) * 2
            ratio = norms[:, at : at + 1] / norms[:, at + 1 : at + 2]
            outs[m][b] = masters[m][b] - MATRIX_RATE * ratio * updates[m][b]


def norm_kernel(blocks, ids, *refs):
    sums = refs[: 3 * blocks]
    params, first, second = refs[3 * blocks : 3 * blocks + 3]
    grads_out, square_out, new_out = refs[3 * blocks + 3 :]
    front = ids[0] == 0
    for b in range(blocks):
        parts = [[], []]
        for n in range(3):
            pair = unpack_rows(sums[3 * b + n][...])
            for kind in range(2):
                v = pair[1 - kind]
                half = v.shape[1] // 2
                parts[kind].append(jnp.where(front, v[:, :half], v[:, half:]))
        for kind in range(2):
            g = lanes(parts[kind])
            second_new, update = moments_step(first[b, kind], second[b, kind], g)
            grads_out[b, kind] = g
            square_out[b, kind] = second_new
            new_out[b, kind] = params[b, kind] - NORM_RATE * update


def exchange(step):
    pairs = []
    for i in range(32):
        core = (i >> 3) & 1
        pairs.append((i, i ^ (4, 2, 16 if core else 1, 1 if core else 16)[step]))
    return pairs


class Gather:
    def __init__(self, held):
        self.parts = (held,)

    def step(self, step, *after):
        if after:
            self.wait(*after)
        held = self.held()
        self.parts = (held, lax.ppermute(held, ALL, exchange(step)))

    def wait(self, *after):
        self.parts = order(self.parts, *after)

    def held(self):
        return self.parts[0] if len(self.parts) == 1 else jnp.concatenate(self.parts, 0)

    def last(self):
        return self.parts[-1]

    def weight(self):
        return list(self.parts), (0, self.parts[0].shape[1])


def order(value, *before):
    return lax.optimization_barrier((value, before))[0]


class Scatter:
    def __init__(self, near=None, far=None, parts=()):
        self.terms = [] if near is None else [near]
        self.far = far
        self.parts = parts

    def wait(self, *after):
        for part in self.parts:
            part.wait(*after)
        if self.terms:
            self.terms = list(order(tuple(self.terms), *after))

    def arrays(self):
        return [array for part in self.parts for array in part.arrays()] + self.terms

    def rows(self):
        return self.terms[0].shape[1] if self.terms else sum(part.rows() for part in self.parts)

    def plan(self):
        return [part.plan() for part in self.parts], len(self.terms)

    def send(self, step, value):
        self.terms.append(lax.ppermute(value, ALL, exchange(step)))


def evaluate(plan, refs):
    parts, count = plan
    found = [jnp.concatenate([evaluate(part, refs) for part in parts], axis=1)] if parts else []
    found += [next(refs)[...].astype(F32) for _ in range(count)]
    return functools.reduce(jnp.add, found)


def slices(tasks, size, at):
    arrays = [array for task in tasks for array in task.arrays()]
    return arrays, [pl.BlockSpec((size,) + array.shape[1:], lambda _: (at, 0, 0)) for array in arrays]


def add_up_kernel(plans, *refs):
    blocks = iter(refs[: len(refs) - len(plans)])
    for plan, out in zip(plans, refs[len(refs) - len(plans) :]):
        out[...] = evaluate(plan, blocks).astype(out.dtype)


def advance_sums(steps, *after):
    arrays, specs, outs, plans = [], [], [], []
    for task, step in steps:
        task.wait(*after)
    for task, step in steps:
        size = 1 << step
        more, blocks = slices([task], size, 1)
        arrays += more
        specs += blocks
        outs.append(jax.ShapeDtypeStruct((size, task.rows(), 128), BF))
        plans.append(task.plan())
    sends = pl.pallas_call(
        functools.partial(add_up_kernel, plans),
        out_shape=outs,
        grid=(1,),
        in_specs=specs,
        out_specs=[pl.BlockSpec(memory_space=pltpu.VMEM)] * len(outs),
        compiler_params=pltpu.CompilerParams(vmem_limit_bytes=16 * 1024 * 1024),
        name="add_up",
    )(*arrays)
    for (task, step), value in zip(steps, sends):
        task.send(step, value)
    return sends


def body(
    wide,
    block_input,
    out_grad,
    conv_reduce,
    conv_spatial,
    conv_expand,
    first_reduce,
    first_spatial,
    first_expand,
    second_reduce,
    second_spatial,
    second_expand,
    norm_params,
    norm_first,
    norm_second,
):
    blocks = conv_reduce.shape[0]
    population = float(block_input.shape[0] * SIDE * SIDE * wide)
    count = 4 * wide
    x = lax.axis_index("x").astype(jnp.int32)
    core = lax.axis_index("core").astype(jnp.int32)
    w = lax.axis_index("wide").astype(jnp.int32)
    fast = wide == PIECES
    here = jnp.stack([x, core, w, jnp.zeros((), jnp.int32)])
    count_up = jnp.arange(2 * PIECES, dtype=jnp.int32)
    ids = jnp.concatenate([here, count_up, count_up])
    to_x = count_up // PIECES
    to_w = count_up % PIECES

    apart_x = to_x ^ x
    apart_w = to_w ^ w
    back = jnp.where(core == 0, apart_w & 1, apart_x)
    front = jnp.where(core == 0, apart_x, apart_w & 1)
    places = front * 8 + back * 4 + ((apart_w & 2) | (apart_w >> 2))
    bit3, bit2 = count_up >> 3, (count_up >> 2) & 1
    from_x = x ^ jnp.where(core == 0, bit3, bit2)
    from_w = w ^ (jnp.where(core == 0, bit2, bit3) | (count_up & 2) | ((count_up & 1) << 2))
    relative = jnp.concatenate([here, places, from_x * PIECES + from_w])

    swap = [(0, 1), (1, 0)]

    def over_core(v):
        return lax.ppermute(v, "core", swap)

    def over_x(v):
        return lax.ppermute(v, "x", swap)

    def share(v, axes):
        return lax.all_to_all(v, axes, 0, 0)

    def run(kernel, outs, *args, places=None, **kw):
        return call(kernel, outs, ids if places is None else places, *args, smem=(0,), **kw)

    wide_row = norm_params.shape[-1]
    near = norm_params.reshape(2 * blocks, wide_row)
    both = jnp.stack([near, over_core(near)])
    far = over_x(both)
    own_all, oth_all = run(
        params_kernel, [((2 * blocks, 2 * wide_row), F32)] * 2, both, far, name="norm_rows"
    )
    own_prm = [own_all[2 * b : 2 * b + 2] for b in range(blocks)]
    oth_prm = [oth_all[2 * b : 2 * b + 2] for b in range(blocks)]

    act = (ROWS, 512)
    keep_x, send_x, keep_g, send_g = run(enter_kernel, [(act, BF)] * 4, block_input, out_grad, name="enter")
    recv_x = over_x(send_x)
    low_stream = stream = run(join_kernel, [((ROWS, 1024), BF)], keep_x, recv_x, name="join")[0]

    def gather(shard, columns):
        whole = lax.all_gather(shard.astype(BF), CROSS, axis=0, tiled=True).reshape(2 * PIECES, -1, columns)
        return [whole], (0, whole.shape[1])

    table = relative if fast else ids
    tables = [table] + [ids] * (blocks - 1)
    gathers = []
    weights = None
    if fast:
        depth = conv_expand.shape[1]

        def shards(b):
            blocked = conv_expand[b].astype(BF).reshape(depth, 4, 128).swapaxes(0, 1).reshape(4 * depth, 128)
            return [conv_reduce[b].astype(BF), conv_spatial[b].astype(BF), blocked]

        gathers = [Gather(shard[None]) for shard in shards(0)]
        gathers[0].step(0, send_x)
        gathers[0].step(1)
        gathers[1].step(0, gathers[0].parts[0])
        gathers[0].step(2, recv_x, far)
        gathers[1].step(1, gathers[0].parts[0])
        gathers[2].step(0, gathers[1].parts[0])
        gathers[2].step(1)
        gathers[0].step(3)
        wholes = [lax.all_gather(jnp.concatenate(shards(b)), CROSS, axis=0, tiled=False) for b in range(1, blocks)]
        one = conv_reduce.shape[1]
        two = one + conv_spatial.shape[1]
        cuts = ((0, one), (one, two), (two, two + 4 * depth))
    else:
        weights = [
            (gather(conv_reduce[b], 128), gather(conv_spatial[b], 128), gather(conv_expand[b], 512)) for b in range(blocks)
        ]

    def weight_of(b, m):
        if not fast:
            return weights[b][m]
        return gathers[m].weight() if b == 0 else ([wholes[b - 1]], cuts[m])

    def advance(stage, stat, out):
        if not fast:
            return
        if stage == 1:
            gathers[1].step(2, out)
            gathers[1].step(3, stat)
        elif stage == 2:
            gathers[2].step(2, gathers[1].last())
            gathers[2].step(3, out)

    inner = (count, 4, 128)
    outer = (2 * wide, 16, 128)
    saved = []
    for b in range(blocks):
        other = over_core(low_stream)
        pre1, low1, stat = run(
            reduce_kernel,
            [((ROWS, 256), F32), ((ROWS, 256), BF), (inner, F32)],
            low_stream,
            other,
            weight=weight_of(b, 0),
            places=tables[b],
            name="reduce",
        )
        low1 = over_core(low1)
        stat = share(stat, ALL)
        advance(3 * b + 1, stat, pre1)
        if fast and b == 0:
            stat, *wholes = lax.optimization_barrier((stat, *wholes))
        stat = stat.reshape(2, 2, wide, 4, 128)
        hid1, moments1, pre2, low2, stat = run(
            functools.partial(spatial_kernel, population),
            [((SPAN, 512), BF), ((8, 256), F32), ((ROWS, 256), F32), ((ROWS, 256), BF), (inner, F32)],
            stat,
            pre1,
            low1,
            own_prm[b],
            oth_prm[b],
            weight=weight_of(b, 1),
            scratch=[pltpu.VMEM((3, SPAN + 2 * LINE, 512), BF)],
            places=tables[b],
            name="spatial",
        )
        low2 = over_core(low2)
        if b > 0:
            stat = order(stat, low2)
        stat = share(stat, ALL)
        advance(3 * b + 2, stat, pre2)
        stat = stat.reshape(2, 2, wide, 4, 128)
        before = stat
        hid2, moments2, pre3, stat = run(
            functools.partial(expand_kernel, population),
            [((ROWS, 512), BF), ((8, 256), F32), ((ROWS, 1024), F32), (outer, F32)],
            stat,
            pre2,
            low2,
            own_prm[b],
            oth_prm[b],
            weight=weight_of(b, 2),
            places=tables[b],
            name="expand",
        )
        if b == blocks - 1:
            recv_g = over_x(order(send_g, before))
        stat = share(stat, CROSS)
        advance(3 * b + 3, stat, pre3)
        item = dict(
            xo=low_stream, xt=other, stream=stream, pre1=pre1, hid1=hid1, m1=moments1, pre2=pre2, hid2=hid2, m2=moments2, pre3=pre3
        )
        if b < blocks - 1:
            item["m3"], stream, low_stream = call(
                functools.partial(close_kernel, population),
                [((8, 1024), F32), ((ROWS, 1024), F32), ((ROWS, 1024), BF)],
                stat,
                pre3,
                stream,
                own_prm[b],
                name="close",
            )
        else:
            item["m3"], result, outside, stat = run(
                functools.partial(last_kernel, population),
                [((8, 1024), F32), ((ROWS, 1024), F32), ((ROWS, 1024), F32), (outer, F32)],
                stat,
                pre3,
                stream,
                own_prm[b],
                keep_g,
                recv_g,
                name="last",
            )
        saved.append(item)

    tasks = {}

    def hook(kind, b, grads):
        if not fast:
            return []
        near, far = grads
        tasks[kind, b] = Scatter(near, far)
        if (kind, b) != ("reduce", 1):
            tasks[kind, b].send(3, far)
        return [far]

    def ahead(kind, b, stat):
        if not fast:
            return stat
        steps = []
        if b == 1 and kind == "spatial":
            stat = order(stat, tasks["expand", 1].terms[-1])
        if b == 0 and kind == "reduce":
            stat = order(stat, *(tasks[name].terms[-1] for name in ("big", ("expand", 0), ("reduce", 1))))
        if b == 1 and kind == "reduce":
            tasks["big"] = Scatter(parts=(tasks["expand", 1], tasks["spatial", 1]))
            steps = [(tasks["big"], 2)]
        if b == 0 and kind == "expand":
            tasks["reduce", 1].send(3, order(tasks["reduce", 1].far, stat))
            steps = [(tasks["big"], 1)]
        if b == 0 and kind == "spatial":
            steps = [(tasks["expand", 0], 2), (tasks["reduce", 1], 2), (tasks["big"], 0)]
        if b == 0 and kind == "reduce":
            steps = [(tasks["spatial", 0], 2)]
        return order(stat, *advance_sums(steps, stat)) if steps else stat

    def whole(task, b, m):
        return task, [((b, m), 0, task.rows())]

    def step_of(sources, last=False):
        line = lamb(sources, masters, firsts, seconds, filled, lines if last else [], count if last else 0)
        lines.append(line)
        return line

    images = []

    def finish_images(full, gate, kernel, name):
        keep, send = run(kernel, [(act, F32), (act, BF)], *order(full, gate), name=name)
        images.extend(run(arrive_kernel, [(block_input.shape, F32)], keep, over_x(send), name="arrive"))
        return send

    def finish():
        small, middle, large = (tasks[kind, 0] for kind in ("expand", "reduce", "spatial"))
        advance_sums([(small, 1), (tasks["reduce", 1], 1)], middle.terms[0])
        leaving = finish_images((result,), middle.terms[0], leave_kernel, "leave")
        big = tasks["big"]
        cut = 4 * conv_expand.shape[1]
        sent = advance_sums([(large, 1)], small.terms[-1], tasks["reduce", 1].terms[-1], leaving)
        rest = Scatter(parts=(small, tasks["reduce", 1]))
        sent = advance_sums([(middle, 2), (rest, 0)], sent)
        finish_images(after, sent[0], leave_sum_kernel, "leave_sum")
        line = step_of([(big, [((1, 2), 0, cut), ((1, 1), cut, big.rows())])])
        sent = advance_sums([(middle, 1)], sent, line, norm_grads)
        sent = advance_sums([(large, 0)], sent, rest.terms[-1])
        advance_sums([(middle, 0)], sent)
        line = step_of([(rest, [((0, 2), 0, cut), ((1, 0), cut, rest.rows())])])
        for task in (large, middle):
            task.wait(line, *images)
        return [[whole(large, 0, 1), whole(middle, 0, 0)]]

    def gradient(b, m, kernel, *args, name):
        parts, (lo, hi) = weight_of(b, m)
        shape = (hi - lo, parts[0].shape[2])
        whole = pltpu.VMEM((2 * PIECES,) + shape, BF)
        half = ((PIECES,) + shape, BF)

        def halves(ids, *refs):
            kernel(ids, *refs[:-3], refs[-1])
            deal(ids, refs[-1], refs[-3], refs[-2])

        return run(halves, [half] * 2, *args, scratch=[whole], places=table, name=name)

    sums = [None] * (3 * blocks)
    local = [None] * blocks
    after = None
    for b in reversed(range(blocks)):
        item = saved[b]
        w_reduce, w_spatial, w_expand = (weight_of(b, m) for m in range(3))
        if after is not None:
            outside, stat = call(
                outer_back_kernel,
                [((ROWS, 1024), F32), (outer, F32)],
                item["m3"],
                item["pre3"],
                item["stream"],
                own_prm[b],
                *after,
                name="outer_back",
            )
        stat = ahead("expand", b, share(stat, CROSS))
        low3, own_part, send, sums[3 * b + 2] = run(
            functools.partial(expand_back_kernel, population),
            [((ROWS, 1024), BF), ((ROWS, 256), F32), ((ROWS, 256), BF), ((16, 128), F32)],
            stat,
            item["m3"],
            item["pre3"],
            outside,
            own_prm[b],
            weight=w_expand,
            places=tables[b],
            name="expand_back",
        )
        recv = over_core(send)
        grad_expand = gradient(b, 2, expand_grad, item["hid2"], low3, name="expand_grad")
        own_part = order(own_part, *grad_expand, *hook("expand", b, grad_expand))
        upstream, stat = call(
            functools.partial(inner_back_kernel, 256),
            [((ROWS, 256), F32), (inner, F32)],
            own_part,
            recv,
            item["m2"],
            item["pre2"],
            own_prm[b],
            name="inner_back",
        )
        stat = ahead("spatial", b, share(stat, ALL)).reshape(2, 2, wide, 4, 128)
        shifts, own_part, send, sums[3 * b + 1] = run(
            functools.partial(spatial_back_kernel, population),
            [((3, SPAN + 2 * LINE, 256), BF), ((ROWS, 256), F32), ((ROWS, 256), BF), ((4, 128), F32)],
            stat,
            item["m2"],
            item["pre2"],
            upstream,
            own_prm[b],
            weight=w_spatial,
            places=tables[b],
            name="spatial_back",
        )
        recv = over_core(send)
        grad_spatial = gradient(b, 1, spatial_grad, item["hid1"], shifts, name="spatial_grad")
        own_part = order(own_part, *grad_spatial, *hook("spatial", b, grad_spatial))
        if fast and b == 0:
            own_part = order(own_part, *(tasks[name].terms[-1] for name in ("big", ("expand", 0), ("reduce", 1))))
        upstream, stat = call(
            functools.partial(inner_back_kernel, 0),
            [((ROWS, 256), F32), (inner, F32)],
            own_part,
            recv,
            item["m1"],
            item["pre1"],
            own_prm[b],
            name="inner_back",
        )
        stat = ahead("reduce", b, share(stat, ALL)).reshape(2, 2, wide, 4, 128)
        low1, own_part, send, sums[3 * b] = run(
            functools.partial(reduce_back_kernel, population),
            [((ROWS, 256), BF), ((ROWS, 1024), F32), ((ROWS, 1024), BF), ((4, 128), F32)],
            stat,
            item["m1"],
            item["pre1"],
            upstream,
            own_prm[b],
            weight=w_reduce,
            places=tables[b],
            name="reduce_back",
        )
        recv = over_core(send)
        grad_reduce = gradient(b, 0, reduce_grad, item["xo"], item["xt"], low1, name="reduce_grad")
        own_part = order(own_part, *grad_reduce, *hook("reduce", b, grad_reduce))
        after = (outside, own_part, recv)
        local[b] = (grad_reduce, grad_spatial, grad_expand)

    def scatter(pair):
        flat = jnp.concatenate(pair).reshape(-1, pair[0].shape[-1])
        return lax.psum_scatter(flat, CROSS, scatter_dimension=0, tiled=True).astype(F32)

    norm_shape = (norm_params.shape, F32)
    norm_grads, norm_square, norm_new = run(
        functools.partial(norm_kernel, blocks), [norm_shape] * 3, *sums, norm_params, norm_first, norm_second, name="norms"
    )
    masters = (conv_reduce, conv_spatial, conv_expand)
    firsts = (first_reduce, first_spatial, first_expand)
    seconds = (second_reduce, second_spatial, second_expand)
    filled = [None] * 3
    lines = []
    if fast:
        batches = finish()
    else:
        finish_images((result,), after[1], leave_kernel, "leave")
        finish_images(after, after[1], leave_sum_kernel, "leave_sum")
        batches = []
        for b in range(blocks):
            for m in range(3):
                part = scatter(local[b][m])
                batches.append([(Scatter(part[None]), [((b, m), 0, part.shape[0])])])
    for n, sources in enumerate(batches):
        step_of(sources, n == len(batches) - 1)
    block_output, input_grad = images
    gradients = [filled[m][0] for m in range(3)]
    squares = [filled[m][1] for m in range(3)]
    updates = [filled[m][2] for m in range(3)]
    line = order(lines[-1], block_output, input_grad, norm_grads, norm_square, norm_new)
    stat = share(line, ALL)
    shapes = [(m.shape, F32) for m in masters]
    renewed = call(
        functools.partial(renew_kernel, blocks), shapes + [((1, 128), F32)], stat, *masters, *updates, name="renew"
    )
    layer_norms = renewed[3][0, : 6 * blocks].reshape(blocks, 3, 2)
    return (
        block_output,
        input_grad,
        *gradients,
        *squares,
        *renewed[:3],
        norm_grads,
        norm_square,
        norm_new,
        layer_norms,
    )


def solution(mesh):
    wide = mesh.shape["wide"]
    fine = Mesh(np.asarray(mesh.devices).reshape(2, 2, wide), ALL)
    narrow = ("x", "core")
    image = P("wide", None, None, narrow)
    matrix = P(None, "wide", narrow)
    row = P(None, None, narrow, None)
    return jax.shard_map(
        functools.partial(body, wide),
        mesh=fine,
        in_specs=(image,) * 2 + (matrix,) * 9 + (row,) * 3,
        out_specs=(image,) * 2 + (matrix,) * 9 + (row,) * 3 + (P(),),
        check_vma=False,
    )
```
